32 devices in a mesh: narrow: 4 (over z), wide: 8 (over y, x, core).
Axes of the slice: x: 2, y: 2, z: 4, core: 2. Of those that a mesh axis runs over, the one named last changes fastest.
Arguments:
- tokens: bfloat16 [64, 512, 768], P(('narrow', 'wide')), may hold values from -6 to 6
- w_query: bfloat16 [768, 768], P(('narrow', 'wide')), may hold values from -0.109375 to 0.109375
- w_key: bfloat16 [768, 768], P(('narrow', 'wide')), may hold values from -0.109375 to 0.109375
- w_value: bfloat16 [768, 768], P(('narrow', 'wide')), may hold values from -0.21875 to 0.21875
- w_output: bfloat16 [768, 768], P(('narrow', 'wide')), may hold values from -0.625 to 0.625
- w_router: bfloat16 [768, 32], P(('narrow', 'wide')), may hold values from -0.15625 to 0.15625
- gain_attn: bfloat16 [768], P(('narrow', 'wide')), may hold values from 0.25 to 1.75
- gain_ffn: bfloat16 [768], P(('narrow', 'wide')), may hold values from 0.25 to 1.75
- rel_bias: bfloat16 [384], P(('narrow', 'wide')), may hold values from -4 to 4
- router_bias: bfloat16 [32], P(('narrow', 'wide')), may hold values from -0.59765625 to 0.59765625
- w_in: bfloat16 [32, 768, 3072], P(('narrow', 'wide')), may hold values from -0.21875 to 0.21875
- w_out: bfloat16 [32, 3072, 768], P(('narrow', 'wide')), may hold values from -4.96875 to 4.96875
- routes: int32 [64, 512, 1], P(('narrow', 'wide')), may hold values from 0 to 31
- fill_rank: int32 [64, 512], P(('narrow', 'wide')), may hold values from 0 to 511, each once within a row
- bucket_map: int32 [1023], replicated, may hold values from 0 to 31
- upstream_grad: bfloat16 [64, 512, 768], P(('narrow', 'wide')), may hold values from -6 to 6
Outputs:
- layer_out: bfloat16 [64, 512, 768], P(('narrow', 'wide'))
- grad_tokens: bfloat16 [64, 512, 768], P(('narrow', 'wide'))
- grad_query_w: float32 [768, 768], P(('narrow', 'wide'))
- grad_key_w: float32 [768, 768], P(('narrow', 'wide'))
- grad_value_w: float32 [768, 768], P(('narrow', 'wide'))
- grad_output_w: float32 [768, 768], P(('narrow', 'wide'))
- grad_router_w: float32 [768, 32], P(('narrow', 'wide'))
- grad_gain_attn: float32 [768], P(('narrow', 'wide'))
- grad_gain_ffn: float32 [768], P(('narrow', 'wide'))
- grad_rel_bias: float32 [384], P(('narrow', 'wide'))
- grad_router_bias: float32 [32], P(('narrow', 'wide'))
- grad_w_in: float32 [32, 768, 3072], P(('narrow', 'wide'))
- grad_w_out: float32 [32, 3072, 768], P(('narrow', 'wide'))
The draws below stay inside these ranges and needn't reach their ends.
Inputs may be any that keep to these rules, and one draw needn't show every extreme that they name: `routes`: each token's single expert. `fill_rank`: in each sequence a permutation of 0 to 511.
All inputs are finite; a program needn't handle non-finite values.
Results may differ from the reference program's by a relative error of at most 0.025.
Values may be sent and summed in bfloat16 or wider, within the bound.
No kernel may reach another device: no remote copies, remote signals or barrier semaphores. Data moves between devices by JAX's collectives and lax.ppermute only.
A program may use at most 256 MiB of HBM per device.

```python
import math
import jax
import jax.numpy as jnp
from jax import lax

D = 768
HEADS = 12
HEAD = 64
FF = 3072
BUCKETS = 32
SEQ = 512
EXPERTS = 32
SEQS = 64
CAP = 20


def with_ends(drawn, own_key, least, top_value):
    index_at = [jax.random.randint(jax.random.fold_in(own_key, axis), (), 0, length) for axis, length in enumerate(drawn.shape)]
    longest = drawn.shape.index(max(drawn.shape))
    neighbour = index_at[:longest] + [(index_at[longest] + 1) % drawn.shape[longest]] + index_at[longest + 1:]
    return drawn.at[tuple(index_at)].set(least).at[tuple(neighbour)].set(top_value)


def block_scale(key, dims, shards, low, largest):
    def one(axis_at, parts):
        steps = jax.random.uniform(jax.random.fold_in(jax.random.fold_in(key, 6), axis_at), (parts,), jnp.float32, low / len(shards), largest / len(shards))
        return jnp.repeat(jnp.exp(steps), dims[axis_at] // parts).reshape((-1,) + (1,) * (len(dims) - axis_at - 1))

    factor_of = one(*shards[0])
    for cut in shards[1:]:
        factor_of = factor_of * one(*cut)
    return factor_of


def different_ones(key, rows, amount, top, lift):
    ranking = jax.random.permutation(jax.random.fold_in(key, 1), amount)
    favour = ranking
    for power in range(3):
        favour = favour * favour // amount
    favour = favour * lift // amount
    lots = jax.random.randint(jax.random.fold_in(key, 2), (rows, amount), 0, 4096) + favour
    sure = jax.random.permutation(jax.random.fold_in(key, 3), rows)[jnp.arange(amount) % rows]
    lots = jnp.where(jnp.arange(rows)[:, None] == sure[None, :], 1 << 14, lots)
    score = lots * amount + jnp.arange(amount)
    return lax.top_k(score.astype(jnp.int32), top)[1].astype(jnp.int32)


def noise(rng, shape, width, reach, pieces=(), kind=jnp.bfloat16):
    drawn = width * jax.random.normal(rng, shape, jnp.float32)
    if pieces:
        drawn = drawn * block_scale(rng, shape, pieces, -0.22, 0.18)
    return jnp.clip(drawn, -reach, reach).astype(kind)


def setup_inputs(seed: int = 0) -> dict:
    streams_of = jax.random.split(jax.random.key(seed), 17)
    return {
        "tokens": noise(streams_of[0], (SEQS, SEQ, D), 1.0, 6.0, ((0, 32),)),
        "w_query": noise(streams_of[1], (D, D), (4 * D) ** -0.5, 0.109375, ((0, 32),)),
        "w_key": noise(streams_of[2], (D, D), (4 * D) ** -0.5, 0.109375, ((0, 32),)),
        "w_value": noise(streams_of[3], (D, D), D ** -0.5, 0.21875, ((0, 32),)),
        "w_output": noise(streams_of[4], (D, D), (D // 8) ** -0.5, 0.625, ((0, 32),)),
        "w_router": noise(streams_of[5], (D, EXPERTS), (2 * D) ** -0.5, 0.15625, ((0, 32),)),
        "gain_attn": jnp.clip(1.0 + 0.15 * jax.random.normal(streams_of[6], (D,), jnp.float32), 0.25, 1.75).astype(jnp.bfloat16),
        "gain_ffn": jnp.clip(1.0 + 0.15 * jax.random.normal(streams_of[7], (D,), jnp.float32), 0.25, 1.75).astype(jnp.bfloat16),
        "rel_bias": noise(streams_of[8], (BUCKETS * HEADS,), 1.0, 4.0, ((0, 32),)),
        "router_bias": noise(streams_of[9], (EXPERTS,), 0.1, 0.59765625, ((0, 32),)),
        "w_in": noise(streams_of[10], (EXPERTS, D, FF), D ** -0.5, 0.21875, ((0, 32),)),
        "w_out": noise(streams_of[11], (EXPERTS, FF, D), (0.026 * EXPERTS), 4.96875, ((0, 32),)),
        "routes": different_ones(streams_of[12], SEQS * SEQ, EXPERTS, 1, 256).reshape((SEQS, SEQ, 1)),
        "fill_rank": jax.vmap(lambda own: jax.random.permutation(own, SEQ))(jax.random.split(streams_of[13], SEQS)).reshape((SEQS, SEQ)).astype(jnp.int32),
        "bucket_map": with_ends(jax.random.randint(streams_of[14], (2 * SEQ - 1,), 0, BUCKETS), jax.random.fold_in(streams_of[14], 1), 0, BUCKETS - 1).astype(jnp.int32),
        "upstream_grad": noise(streams_of[15], (SEQS, SEQ, D), 1.0, 6.0, ((0, 32),)),
    }


epsilon = 1e-06
precise = lax.Precision.HIGHEST

@jax.custom_vjp
def low(v):
    return lax.optimization_barrier(v.astype(jnp.bfloat16)).astype(jnp.float32)

@jax.custom_vjp
def low_back(v):
    return v

def low_keep(v):
    return (low(v), None)

def low_pass(kept, grad):
    return (grad,)

def back_keep(v):
    return (v, None)

def back_low(kept, grad):
    return (low(grad),)
low.defvjp(low_keep, low_pass)
low_back.defvjp(back_keep, back_low)

def rms_scale(values, gain):
    return values * lax.rsqrt(lax.optimization_barrier(jnp.mean(values * values, axis=-1, keepdims=True)) + epsilon) * gain

def slot_of(pair):
    route, order = pair
    same = route[:, None] == route[None, :]
    before = order[None, :] < order[:, None]
    return lax.optimization_barrier(jnp.sum((same & before).astype(jnp.int32), axis=1, dtype=jnp.int32)).astype(jnp.int32)

def reference(tokens, w_query, w_key, w_value, w_output, w_router, gain_attn, gain_ffn, rel_bias, router_bias, w_in, w_out, routes, fill_rank, bucket_map, upstream_grad):
    route = routes[..., 0].astype(jnp.int32)
    slot = lax.map(slot_of, (route, fill_rank.astype(jnp.int32))).astype(jnp.int32)
    keep = (slot < jnp.int32(CAP)).astype(jnp.float32)
    places = jnp.arange(SEQ, dtype=jnp.int32)
    distance = (places[None, :] - places[:, None] + jnp.int32(SEQ - 1)).astype(jnp.int32)
    bucket_mat = bucket_map.astype(jnp.int32)[distance].astype(jnp.int32)
    count_all = SEQS * SEQ
    seq_range = jnp.arange(SEQS, dtype=jnp.int32)
    expert_range = jnp.arange(EXPERTS, dtype=jnp.int32)
    cap_range = jnp.arange(CAP, dtype=jnp.int32)

    def index_of(args):
        route_row, slot_row, seq_number = args
        hit = (route_row[None, None, :] == expert_range[:, None, None]) & (slot_row[None, None, :] == cap_range[None, :, None])
        found = lax.optimization_barrier(jnp.sum(hit.astype(jnp.int32), axis=2, dtype=jnp.int32))
        flat_pos = (places + seq_number * jnp.int32(SEQ)).astype(jnp.int32)
        where_pos = lax.optimization_barrier(jnp.sum(jnp.where(hit, flat_pos[None, None, :], jnp.int32(0)), axis=2, dtype=jnp.int32))
        return jnp.where(found > 0, where_pos, jnp.int32(count_all)).astype(jnp.int32)
    index = jnp.transpose(lax.map(index_of, (route, slot, seq_range)), (1, 0, 2)).astype(jnp.int32)
    seq_id = jnp.broadcast_to(seq_range[:, None], (SEQS, SEQ)).astype(jnp.int32)
    safe_slot = jnp.minimum(slot, jnp.int32(CAP - 1)).astype(jnp.int32)
    gather_pos = (seq_id * jnp.int32(CAP) + safe_slot).astype(jnp.int32)
    route_hot = jax.nn.one_hot(route, EXPERTS, dtype=jnp.float32)
    group = math.gcd(SEQS, max(1, 4096 // SEQ))

    def forward(acts, wq, wk, wv, wo, wr, gone, gtwo, relb, rbias, win, wout):
        table = relb.reshape(BUCKETS, HEADS)
        bias = jnp.transpose(table[bucket_mat], (2, 0, 1))

        def attend(block):
            normed = low(rms_scale(block, gone))
            queries = low_back(low(jnp.einsum('gsd,de->gse', normed, wq, precision=precise))).reshape(group, SEQ, HEADS, HEAD)
            keys = low_back(low(jnp.einsum('gsd,de->gse', normed, wk, precision=precise))).reshape(group, SEQ, HEADS, HEAD)
            values = low_back(low(jnp.einsum('gsd,de->gse', normed, wv, precision=precise))).reshape(group, SEQ, HEADS, HEAD)
            scores = low_back(jnp.einsum('gqhd,gkhd->ghqk', queries, keys, precision=precise) + bias[None])
            probs = low(jax.nn.softmax(scores, axis=-1))
            mixed = jnp.einsum('ghqk,gkhd->gqhd', probs, values, precision=precise).reshape(group, SEQ, D)
            mixed = low_back(low(mixed))
            branch = low_back(jnp.einsum('gsd,de->gse', mixed, wo, precision=precise))
            return block + branch
        resid = lax.map(jax.checkpoint(attend), acts.reshape(SEQS // group, group, SEQ, D)).reshape(SEQS, SEQ, D)
        normed_two = low(rms_scale(resid, gtwo))
        logits = low_back(jnp.einsum('tsd,de->tse', normed_two, wr, precision=precise) + rbias)
        router_probs = jax.nn.softmax(logits, axis=-1)
        gate = lax.optimization_barrier(jnp.sum(router_probs * route_hot, axis=-1))
        padded = jnp.concatenate([normed_two.reshape(count_all, D), jnp.zeros((1, D), dtype=normed_two.dtype)], axis=0)

        def expert(args):
            idx, weight_in, weight_out = args
            rows = low_back(padded[idx.reshape(-1).astype(jnp.int32)])
            inner = low_back(jnp.dot(rows, weight_in, precision=precise))
            active = low(jax.nn.gelu(inner, approximate=False))
            return low_back(low(jnp.dot(active, weight_out, precision=precise)))
        produced = lax.map(jax.checkpoint(expert), (index, win, wout))
        result = produced[route, gather_pos]
        return resid + (keep * gate)[..., None] * result
    prims = tuple((a.astype(jnp.float32) for a in (tokens, w_query, w_key, w_value, w_output, w_router, gain_attn, gain_ffn, rel_bias, router_bias, w_in, w_out)))
    output, pull = jax.vjp(forward, *prims)
    grads = pull(upstream_grad.astype(jnp.float32))
    return (output.astype(jnp.bfloat16), grads[0].astype(jnp.bfloat16), grads[1], grads[2], grads[3], grads[4], grads[5], grads[6], grads[7], grads[8], grads[9], grads[10], grads[11])
```

```python
import jax
import jax.numpy as jnp
from jax import lax
from jax.experimental import pallas as pl
from jax.experimental.pallas import tpu as pltpu
from jax.sharding import PartitionSpec as P

HEADS = 12
HEAD = 64
BUCKETS = 32
AXES = ("narrow", "wide")

epsilon = 1e-06
f32 = jnp.float32
bf16 = jnp.bfloat16


def smooth_unit(values):
    return jax.nn.gelu(values, approximate=False)


def norm_forward(values, gain):
    scale = lax.rsqrt(jnp.mean(values * values, axis=-1, keepdims=True) + epsilon)
    return (values * scale * gain, scale)


def norm_backward(values, scale, gain, grad):
    weighted = grad * gain
    grad_values = scale * weighted - values * scale**3 * jnp.mean(
        weighted * values, axis=-1, keepdims=True
    )
    return (grad_values, jnp.sum(grad * values * scale, axis=0))


def exchange(buffer):
    return lax.all_to_all(buffer, AXES, split_axis=0, concat_axis=0, tiled=True)


def pack_rows(parts, width):
    lead = parts[0].shape[0]
    flat = jnp.concatenate([part.reshape(lead, -1) for part in parts], axis=1)
    short = -flat.shape[1] % width
    return jnp.pad(flat, ((0, 0), (0, short))).reshape(lead, -1, width)


def unpack_rows(packed, sizes):
    flat = packed.reshape(packed.shape[0], -1)
    out, at = [], 0
    for size in sizes:
        out.append(flat[:, at : at + size])
        at += size
    return out


def skew_kernel(lines_ref, out_ref):
    heads, block, span = out_ref.shape
    for head in range(heads):
        row = jnp.broadcast_to(lines_ref[head : head + 1, :], (block, span))
        out_ref[head] = pltpu.roll(row, span - (block - 1), 1, stride=1, stride_axis=0)


def skew_bias(lines, block):
    heads, span = lines.shape
    return pl.pallas_call(
        skew_kernel,
        out_shape=jax.ShapeDtypeStruct((heads, block, span), f32),
    )(lines)


def body(
    tokens,
    w_query,
    w_key,
    w_value,
    w_output,
    w_router,
    gain_attn,
    gain_ffn,
    rel_bias,
    router_bias,
    w_in,
    w_out,
    routes,
    fill_rank,
    bucket_map,
    upstream_grad,
):
    batches, length, width = tokens.shape
    devices = lax.axis_size(AXES)
    narrow = lax.axis_size("narrow")
    wide = lax.axis_size("wide")
    local_experts = w_in.shape[0]
    experts = local_experts * devices
    capacity = max(2, 5 * length // (4 * experts))
    slots = experts * capacity
    slot_ids = jnp.arange(slots, dtype=jnp.int32)
    expert_ids = jnp.arange(experts, dtype=jnp.int32)
    block = 128
    blocks = length // block
    span = 2 * length

    small_parts = [w_router, gain_attn, gain_ffn, rel_bias, router_bias]
    small = pack_rows([part.reshape(1, -1) for part in small_parts], width)[0]
    square = jnp.concatenate([w_query, w_key, w_value, w_output, small], axis=0)
    shard = w_query.shape[0]
    everything = lax.all_gather(square, AXES, axis=0)
    wq_all, wk_all, wv_all, wo_all = (
        everything[:, i * shard : (i + 1) * shard].reshape(width, width) for i in range(4)
    )
    wr_all, gain_one, gain_two, rel_flat, bias_all = unpack_rows(
        everything[:, 4 * shard :], [part.size for part in small_parts]
    )
    wr_all = wr_all.reshape(width, experts)
    gain_one32 = gain_one.reshape(-1).astype(f32)
    gain_two32 = gain_two.reshape(-1).astype(f32)
    bias_all32 = bias_all.reshape(-1).astype(f32)
    table = rel_flat.reshape(BUCKETS, HEADS).T

    bucket_hot = (
        jnp.arange(BUCKETS, dtype=jnp.int32)[:, None]
        == jnp.pad(bucket_map, (0, 1), constant_values=-1)[None, :]
    ).astype(bf16)
    lines = jnp.dot(table, bucket_hot, preferred_element_type=f32)
    skewed = skew_bias(lines, block)
    bias = jnp.concatenate(
        [
            skewed[:, :, length - block * (at + 1) : 2 * length - block * (at + 1)]
            for at in range(blocks)
        ],
        axis=1,
    )

    def plan(at):
        route = routes[at, :, 0]
        order = fill_rank[at]
        route_hot = (route[:, None] == expert_ids[None, :]).astype(f32)
        earlier = (order[None, :] < order[:, None]).astype(bf16)
        counts = jnp.dot(earlier, route_hot.astype(bf16), preferred_element_type=f32)
        slot = jnp.sum(counts * route_hot, axis=-1).astype(jnp.int32)
        target = jnp.where(slot < capacity, route * capacity + slot, -1)
        sender = (slot_ids[:, None] == target[None, :]).astype(bf16)
        return route_hot, sender

    def dispatch(sender, rows):
        moved = jnp.dot(sender, rows, preferred_element_type=f32).astype(bf16)
        return exchange(moved.reshape(devices, local_experts * capacity, width))

    def front(at):
        acts32 = tokens[at].astype(f32)
        normed, scale_one = norm_forward(acts32, gain_one32)
        normed_b = normed.astype(bf16)

        def project(weight):
            return (
                jnp.dot(normed_b, weight, preferred_element_type=f32)
                .astype(bf16)
                .reshape(length, HEADS, HEAD)
            )

        queries, keys, values = project(wq_all), project(wk_all), project(wv_all)
        scores = jnp.einsum("qhd,khd->hqk", queries, keys, preferred_element_type=f32) + bias
        peak = jnp.max(scores, axis=-1, keepdims=True)
        total = jnp.log(jnp.sum(jnp.exp(scores - peak), axis=-1, keepdims=True)) + peak
        probs_b = jnp.exp(scores - total).astype(bf16)
        mixed = (
            jnp.einsum("hqk,khd->qhd", probs_b, values, preferred_element_type=f32)
            .astype(bf16)
            .reshape(length, width)
        )
        resid = acts32 + jnp.dot(mixed, wo_all, preferred_element_type=f32)
        normed_two, scale_two = norm_forward(resid, gain_two32)
        normed_two_b = normed_two.astype(bf16)
        logits = jnp.dot(normed_two_b, wr_all, preferred_element_type=f32) + bias_all32
        router_probs = jax.nn.softmax(logits, axis=-1)
        return dict(
            acts32=acts32, scale_one=scale_one, normed_b=normed_b, queries=queries, keys=keys,
            values=values, probs_b=probs_b, mixed=mixed, resid=resid, scale_two=scale_two,
            normed_two_b=normed_two_b, router_probs=router_probs,
        )

    own = lax.axis_index(AXES) * local_experts

    def expert(rows, raw, local):
        logits = jnp.dot(rows, wr_all, preferred_element_type=f32) + bias_all32
        probs = jax.nn.softmax(logits, axis=-1)
        gate = jnp.sum(jnp.where(expert_ids[None, :] == own + local, probs, 0.0), axis=-1)
        grad_result = (gate[:, None] * raw.astype(f32)).astype(bf16)
        inner = jnp.dot(rows, w_in[local], preferred_element_type=f32)
        active = smooth_unit(inner).astype(bf16)
        result = jnp.dot(active, w_out[local], preferred_element_type=f32).astype(bf16)
        grad_active = jnp.einsum("rd,fd->rf", grad_result, w_out[local], preferred_element_type=f32)
        unused, smooth_pull = jax.vjp(smooth_unit, inner)
        grad_inner = smooth_pull(grad_active)[0].astype(bf16)
        grad_rows = jnp.einsum(
            "rf,df->rd", grad_inner, w_in[local], preferred_element_type=f32
        ).astype(bf16)
        return result, grad_rows, (rows, grad_result, active, grad_inner)

    def back(at, kept, hot, sender, result, grad_back):
        expert_rows = jnp.einsum("ct,cd->td", sender, result, preferred_element_type=f32)
        resid, scale_two = kept["resid"], kept["scale_two"]
        router_probs, normed_two_b = kept["router_probs"], kept["normed_two_b"]
        gate = jnp.sum(router_probs * hot, axis=-1)
        output = (resid + gate[:, None] * expert_rows).astype(bf16)
        upstream32 = upstream_grad[at].astype(f32)
        grad_gate = jnp.sum(upstream32 * expert_rows, axis=-1)
        grad_from_experts = jnp.einsum("ct,cd->td", sender, grad_back, preferred_element_type=f32)
        grad_logits = (
            router_probs * (hot * grad_gate[:, None] - (gate * grad_gate)[:, None])
        ).astype(bf16)
        grad_router_bias = jnp.sum(grad_logits.astype(f32), axis=0)
        grad_router_w = jnp.einsum(
            "td,te->de", normed_two_b, grad_logits, preferred_element_type=f32
        )
        grad_normed_two = (
            jnp.einsum("te,de->td", grad_logits, wr_all, preferred_element_type=f32)
            + grad_from_experts
        )
        grad_resid_norm, grad_gain_two = norm_backward(
            resid, scale_two, gain_two32, grad_normed_two
        )
        grad_resid = upstream32 + grad_resid_norm
        grad_branch = grad_resid.astype(bf16)
        grad_output_w = jnp.einsum(
            "td,te->de", kept["mixed"], grad_branch, preferred_element_type=f32
        )
        grad_mixed = (
            jnp.einsum("te,de->td", grad_branch, wo_all, preferred_element_type=f32)
            .astype(bf16)
            .reshape(length, HEADS, HEAD)
        )
        probs_b = kept["probs_b"]
        probs = probs_b.astype(f32)
        queries, keys, values = kept["queries"], kept["keys"], kept["values"]
        grad_probs = jnp.einsum("qhd,khd->hqk", grad_mixed, values, preferred_element_type=f32)
        center = jnp.sum(probs * grad_probs, axis=-1, keepdims=True)
        grad_scores = (probs * (grad_probs - center)).astype(bf16)
        grad_values = (
            jnp.einsum("hqk,qhd->khd", probs_b, grad_mixed, preferred_element_type=f32)
            .astype(bf16)
            .reshape(length, width)
        )
        grad_queries = (
            jnp.einsum("hqk,khd->qhd", grad_scores, keys, preferred_element_type=f32)
            .astype(bf16)
            .reshape(length, width)
        )
        grad_keys = (
            jnp.einsum("hqk,qhd->khd", grad_scores, queries, preferred_element_type=f32)
            .astype(bf16)
            .reshape(length, width)
        )
        normed_b = kept["normed_b"]
        grad_weights = [
            jnp.einsum("td,te->de", normed_b, grad, preferred_element_type=f32)
            for grad in (grad_queries, grad_keys, grad_values)
        ]
        grad_normed = sum(
            jnp.einsum("te,de->td", grad, weight, preferred_element_type=f32)
            for grad, weight in (
                (grad_queries, wq_all),
                (grad_keys, wk_all),
                (grad_values, wv_all),
            )
        )
        grad_acts_norm, grad_gain_one = norm_backward(
            kept["acts32"], kept["scale_one"], gain_one32, grad_normed
        )
        grad_acts = (grad_resid + grad_acts_norm).astype(bf16)
        fold = jnp.zeros((HEADS, block, span), f32)
        for step in range(blocks):
            low = length - block * (step + 1)
            piece = grad_scores[:, block * step : block * (step + 1), :].astype(f32)
            fold = fold + jnp.pad(piece, ((0, 0), (0, 0), (low, span - length - low)))
        return (
            output,
            grad_acts,
            fold,
            (
                *grad_weights,
                grad_output_w,
                grad_router_w,
                grad_gain_one,
                grad_gain_two,
                grad_router_bias,
            ),
        )

    plans = [plan(at) for at in range(batches)]
    raw_arrived = [dispatch(plans[at][1], upstream_grad[at]) for at in range(batches)]
    fronts, returned, saved = [], [], []
    for at in range(batches):
        kept = front(at)
        fronts.append(kept)
        arrived = dispatch(plans[at][1], kept["normed_two_b"])
        arrived = arrived.reshape(devices, local_experts, capacity, width)
        raw = raw_arrived[at].reshape(devices, local_experts, capacity, width)
        results, grads, keep = [], [], []
        for local in range(local_experts):
            result, grad_rows, held = expert(
                arrived[:, local].reshape(devices * capacity, width),
                raw[:, local].reshape(devices * capacity, width),
                local,
            )
            results.append(result.reshape(devices, capacity, width))
            grads.append(grad_rows.reshape(devices, capacity, width))
            keep.append(held)
        saved.append(keep)
        both = jnp.concatenate(
            [
                jnp.stack(results, axis=1).reshape(devices, local_experts * capacity, width),
                jnp.stack(grads, axis=1).reshape(devices, local_experts * capacity, width),
            ],
            axis=2,
        )
        returned.append(exchange(both).reshape(slots, 2 * width))

    grad_in, grad_out = [], []
    for local in range(local_experts):
        rows, grad_result, active, grad_inner = (
            jnp.concatenate([saved[at][local][i] for at in range(batches)], axis=0)
            for i in range(4)
        )
        grad_in.append(jnp.einsum("rd,rf->df", rows, grad_inner, preferred_element_type=f32))
        grad_out.append(jnp.einsum("rf,rd->fd", active, grad_result, preferred_element_type=f32))

    outputs, grad_inputs, total, folded = [], [], None, None
    for at in range(batches):
        output, grad_acts, fold, update = back(
            at,
            fronts[at],
            plans[at][0],
            plans[at][1],
            returned[at][:, :width],
            returned[at][:, width:],
        )
        outputs.append(output)
        grad_inputs.append(grad_acts)
        folded = fold if folded is None else folded + fold
        total = update if total is None else tuple(a + b for a, b in zip(total, update))
    rows = block
    while rows > 1:
        rows //= 2
        folded = folded[:, :rows] + jnp.roll(folded[:, rows:], -rows, axis=2)
    diagonal = jnp.roll(folded[:, 0], block - 1, axis=1)
    grad_rel = jnp.einsum(
        "hn,bn->bh", diagonal, bucket_hot.astype(f32), precision=lax.Precision.HIGHEST
    ).reshape(-1)
    g_query, g_key, g_value, g_output, g_router, g_gain_one, g_gain_two, g_bias = total

    small_grads = [g_router, g_gain_one, g_gain_two, grad_rel, g_bias]
    small_pack = pack_rows([part.reshape(devices, -1) for part in small_grads], width)
    packed = jnp.concatenate(
        [part.reshape(devices, shard, width) for part in (g_query, g_key, g_value, g_output)]
        + [small_pack],
        axis=1,
    ).astype(bf16)
    depth = packed.shape[1]
    summed = lax.psum_scatter(
        packed.reshape(narrow, wide, depth, width), "wide", scatter_dimension=1, tiled=True
    )
    summed = lax.psum_scatter(
        summed.reshape(narrow, depth, width), "narrow", scatter_dimension=0, tiled=True
    )
    summed = summed.reshape(depth, width).astype(f32)
    r_query, r_key, r_value, r_output = (
        summed[i * shard : (i + 1) * shard] for i in range(4)
    )
    tail = unpack_rows(summed[None, 4 * shard :], [part.size // devices for part in small_grads])
    r_router, r_gain_one, r_gain_two, r_rel, r_bias = (
        part.reshape(shape)
        for part, shape in zip(
            tail,
            (w_router.shape, gain_attn.shape, gain_ffn.shape, rel_bias.shape, router_bias.shape),
        )
    )
    return (
        jnp.stack(outputs, axis=0),
        jnp.stack(grad_inputs, axis=0),
        r_query,
        r_key,
        r_value,
        r_output,
        r_router,
        r_gain_one,
        r_gain_two,
        r_rel,
        r_bias,
        jnp.stack(grad_in, axis=0),
        jnp.stack(grad_out, axis=0),
    )


def solution(mesh):
    both = P(AXES)
    in_specs = (both,) * 14 + (P(), both)
    out_specs = (both,) * 13
    return jax.shard_map(body, mesh=mesh, in_specs=in_specs, out_specs=out_specs, check_vma=False)
```

```python
import jax
import jax.numpy as jnp
from jax import lax
from jax.experimental import pallas as pl
from jax.experimental.pallas import tpu as pltpu
from jax.sharding import PartitionSpec as P

HEADS = 12
HEAD = 64
BUCKETS = 32
PAIR = 2 * HEAD
GROUP = 4
BLOCK = 128
AXES = ("narrow", "wide")
VMEM_BYTES = 60 * 1024 * 1024

epsilon = 1e-06
f32 = jnp.float32
bf16 = jnp.bfloat16


def mm(a, b):
    return lax.dot_general(a, b, (((1,), (0,)), ((), ())), preferred_element_type=f32)


def mm_nt(a, b):
    return lax.dot_general(a, b, (((1,), (1,)), ((), ())), preferred_element_type=f32)


def mm_tn(a, b):
    return lax.dot_general(a, b, (((0,), (0,)), ((), ())), preferred_element_type=f32)


def norm_scale(values):
    return lax.rsqrt(jnp.mean(values * values, axis=-1, keepdims=True) + epsilon)


def softmax_rows(logits):
    shifted = jnp.exp(logits - jnp.max(logits, axis=-1, keepdims=True))
    return shifted / jnp.sum(shifted, axis=-1, keepdims=True)


def pair_mask(shape, half):
    lane = lax.broadcasted_iota(jnp.int32, shape, 1)
    return (lane < HEAD) if half == 0 else (lane >= HEAD)


def params():
    return pltpu.CompilerParams(vmem_limit_bytes=VMEM_BYTES)


def front_kernel(
    tokens_ref, wq_ref, wk_ref, wv_ref, wo_ref, skew_ref, gain_one_ref, gain_two_ref, wr_ref,
    rbias_ref, spots_ref, q_ref, k_ref, v_ref, probs_ref, mixed_ref, resid_ref, normed_two_ref,
    router_ref, sent_ref, normed_ref,
):
    step = pl.program_id(0)
    length, width = tokens_ref.shape

    @pl.when(step == 0)
    def start():
        acts = tokens_ref[...].astype(f32)
        normed_ref[...] = (acts * norm_scale(acts) * gain_one_ref[...]).astype(bf16)
        resid_ref[...] = acts

    normed = normed_ref[...]
    q_ref[...] = mm(normed, wq_ref[...]).astype(bf16)
    k_ref[...] = mm(normed, wk_ref[...]).astype(bf16)
    v_ref[...] = mm(normed, wv_ref[...]).astype(bf16)
    for pair in range(GROUP // 2):
        cols = slice(PAIR * pair, PAIR * (pair + 1))
        query, key, value = q_ref[:, cols], k_ref[:, cols], v_ref[:, cols]
        out = None
        for half in range(2):
            head = 2 * pair + half
            mask = pair_mask(query.shape, half)
            scores = mm_nt(jnp.where(mask, query, jnp.zeros_like(query)), key)
            parts = []
            for at in range(length // BLOCK):
                low = length - BLOCK * (at + 1)
                part = scores[BLOCK * at : BLOCK * (at + 1), :] + skew_ref[head, :, low : low + length]
                part = jnp.exp(part - jnp.max(part, axis=-1, keepdims=True))
                total = jnp.sum(part, axis=-1, keepdims=True)
                parts.append((part * (1.0 / total)).astype(bf16))
            probs = jnp.concatenate(parts, axis=0)
            probs_ref[head] = probs
            term = mm(probs, jnp.where(mask, value, jnp.zeros_like(value)))
            out = term if out is None else out + term
        mixed_ref[:, cols] = out.astype(bf16)
    resid_ref[...] += mm(mixed_ref[...], wo_ref[...])

    @pl.when(step == pl.num_programs(0) - 1)
    def finish():
        resid = resid_ref[...]
        normed_two = (resid * norm_scale(resid) * gain_two_ref[...]).astype(bf16)
        normed_two_ref[...] = normed_two
        router_ref[...] = softmax_rows(mm(normed_two, wr_ref[...]) + rbias_ref[...])
        rows = lax.broadcasted_iota(jnp.int32, (sent_ref.shape[0], length), 0)
        left = mm((rows == spots_ref[0:1, :]).astype(bf16), normed_two[:, : width // 2])
        right = mm((rows == spots_ref[1:2, :]).astype(bf16), normed_two[:, width // 2 :])
        sent_ref[...] = (left + right).astype(bf16)


def front_call(tokens, wq, wk, wv, wo, skewed, gain_one, gain_two, wr, rbias, spots, slots):
    length, width = tokens.shape
    experts = wr.shape[1]
    part = GROUP * HEAD
    whole = lambda *shape: pl.BlockSpec(shape, lambda g: (0,) * len(shape))
    columns = lambda size: pl.BlockSpec((size, part), lambda g: (0, g))
    return pl.pallas_call(
        front_kernel,
        grid=(HEADS // GROUP,),
        in_specs=[
            whole(length, width), columns(width), columns(width), columns(width),
            pl.BlockSpec((part, width), lambda g: (g, 0)),
            pl.BlockSpec((GROUP, BLOCK, 2 * length), lambda g: (g, 0, 0)),
            whole(1, width), whole(1, width), whole(width, experts), whole(1, experts),
            whole(2, length),
        ],
        out_specs=[
            columns(length), columns(length), columns(length),
            pl.BlockSpec((GROUP, length, length), lambda g: (g, 0, 0)),
            columns(length), whole(length, width), whole(length, width), whole(length, experts),
            whole(2 * slots, width // 2),
        ],
        out_shape=[
            jax.ShapeDtypeStruct((length, width), bf16),
            jax.ShapeDtypeStruct((length, width), bf16),
            jax.ShapeDtypeStruct((length, width), bf16),
            jax.ShapeDtypeStruct((HEADS, length, length), bf16),
            jax.ShapeDtypeStruct((length, width), bf16),
            jax.ShapeDtypeStruct((length, width), f32),
            jax.ShapeDtypeStruct((length, width), bf16),
            jax.ShapeDtypeStruct((length, experts), f32),
            jax.ShapeDtypeStruct((2 * slots, width // 2), bf16),
        ],
        scratch_shapes=[pltpu.VMEM((length, width), bf16)],
        compiler_params=params(),
        cost_estimate=pl.CostEstimate(
            flops=2 * length * width * width * 4 + 4 * length * length * width * 4,
            bytes_accessed=25 * 1024 * 1024, transcendentals=HEADS * length * length,
        ),
        name="front",
    )(tokens, wq, wk, wv, wo, skewed, gain_one, gain_two, wr, rbias, spots)


def bell(values):
    size = jnp.abs(values)
    t = 1.0 / (1.0 + (0.3275911 * 0.7071067811865476) * size)
    falling = jnp.exp(-0.5 * values * values)
    poly = t * (
        0.127414796
        + t * (-0.142248368 + t * (0.7107068705 + t * (-0.7265760135 + t * 0.5307027145)))
    )
    tail = poly * falling
    return jnp.where(values < 0, tail, 1.0 - tail), falling * 0.3989422804014327


def expert_kernel(
    own_ref, arrived_ref, raw_ref, wr_ref, rbias_ref, place_ref, placed_ref, win_ref, wout_ref,
    sent_ref, rows_ref, active_ref, gradinner_ref, gradresult_ref, result_acc, rows_acc,
):
    step = pl.program_id(0)
    last = pl.num_programs(0) - 1
    count = rows_ref.shape[0]

    @pl.when(step == 0)
    def start():
        arrived = arrived_ref[...]
        ids = lax.broadcasted_iota(jnp.int32, (count, 2 * count), 1)
        half = arrived.shape[1]
        for side in range(2):
            pick = (ids == place_ref[:, side : side + 1]).astype(bf16)
            rows_ref[:, half * side : half * (side + 1)] = mm(pick, arrived).astype(bf16)
        probs = softmax_rows(mm(rows_ref[...], wr_ref[...]) + rbias_ref[...])
        mine = lax.broadcasted_iota(jnp.int32, probs.shape, 1) == own_ref[0]
        gate = jnp.sum(jnp.where(mine, probs, 0.0), axis=-1, keepdims=True)
        gradresult_ref[...] = (gate * raw_ref[...].astype(f32)).astype(bf16)

    inner = mm(rows_ref[...], win_ref[...])
    grad_active = mm_nt(gradresult_ref[...], wout_ref[...])
    share, density = bell(inner)
    active = (inner * share).astype(bf16)
    grad_inner = (grad_active * (share + inner * density)).astype(bf16)
    active_ref[...] = active
    gradinner_ref[...] = grad_inner
    result = mm(active, wout_ref[...])
    grad_rows = mm_nt(grad_inner, win_ref[...])

    @pl.when(step == 0)
    def first():
        result_acc[...] = result
        rows_acc[...] = grad_rows

    @pl.when(step > 0)
    def more():
        result_acc[...] += result
        rows_acc[...] += grad_rows

    @pl.when(step == last)
    def finish():
        ids = lax.broadcasted_iota(jnp.int32, (2 * count, count), 0)
        sent_ref[...] = (
            mm((ids == placed_ref[0:1, :]).astype(bf16), result_acc[...].astype(bf16))
            + mm((ids == placed_ref[1:2, :]).astype(bf16), rows_acc[...].astype(bf16))
        ).astype(bf16)


def expert_call(own, arrived, raw, wr, rbias, place, w_in, w_out, part=1024):
    count, width = raw.shape
    hidden = w_in.shape[1]
    experts = wr.shape[1]
    whole = lambda *shape: pl.BlockSpec(shape, lambda g, own: (0,) * len(shape))
    columns = lambda n: pl.BlockSpec((n, part), lambda g, own: (0, g))
    return pl.pallas_call(
        expert_kernel,
        grid_spec=pltpu.PrefetchScalarGridSpec(
            num_scalar_prefetch=1,
            grid=(hidden // part,),
            in_specs=[
                whole(2 * count, width // 2), whole(count, width), whole(width, experts),
                whole(1, experts), whole(count, 2), whole(2, count),
                columns(width), pl.BlockSpec((part, width), lambda g, own: (g, 0)),
            ],
            out_specs=[
                whole(2 * count, width), whole(count, width), columns(count), columns(count),
                whole(count, width),
            ],
            scratch_shapes=[pltpu.VMEM((count, width), f32), pltpu.VMEM((count, width), f32)],
        ),
        out_shape=[
            jax.ShapeDtypeStruct((2 * count, width), bf16),
            jax.ShapeDtypeStruct((count, width), bf16),
            jax.ShapeDtypeStruct((count, hidden), bf16),
            jax.ShapeDtypeStruct((count, hidden), bf16),
            jax.ShapeDtypeStruct((count, width), bf16),
        ],
        compiler_params=params(),
        cost_estimate=pl.CostEstimate(
            flops=8 * count * width * hidden, bytes_accessed=20 * 1024 * 1024,
            transcendentals=count * hidden,
        ),
        name="expert",
    )(own, arrived, raw, wr, rbias, place, place.T, w_in, w_out)


def back_kernel(
    target_ref, route_ref, returned_ref, up_ref, resid_ref, router_ref, normed_two_ref,
    mixed_ref, tokens_ref, gain_one_ref, gain_two_ref, wr_ref, wo_ref, wq_ref, wk_ref, wv_ref,
    q_ref, k_ref, v_ref, probs_ref,
    output_ref, gradacts_ref, fold_ref, gq_ref, gk_ref, gv_ref, go_ref, grw_ref, small_ref,
    gbias_ref,
    gradmixed_ref, gradresid_ref, normedt_ref, acc_ref, center_ref,
):
    step = pl.program_id(0)
    last = pl.num_programs(0) - 1
    length, width = tokens_ref.shape
    experts = wr_ref.shape[1]
    part = GROUP * HEAD

    @pl.when(step == 0)
    def start():
        returned = returned_ref[...]
        ids = lax.broadcasted_iota(jnp.int32, (length, returned.shape[0]), 1)
        expert_rows = mm((ids == target_ref[:, 0:1]).astype(bf16), returned)
        grad_back = mm((ids == target_ref[:, 1:2]).astype(bf16), returned)
        up = up_ref[...].astype(f32)
        resid = resid_ref[...]
        router = router_ref[...]
        hot = lax.broadcasted_iota(jnp.int32, (length, experts), 1) == route_ref[...]
        gate = jnp.sum(jnp.where(hot, router, 0.0), axis=-1, keepdims=True)
        output_ref[...] = (resid + gate * expert_rows).astype(bf16)
        grad_gate = jnp.sum(up * expert_rows, axis=-1, keepdims=True)
        grad_logits = (router * (jnp.where(hot, grad_gate, 0.0) - gate * grad_gate)).astype(bf16)
        gbias_ref[...] = jnp.sum(grad_logits.astype(f32), axis=0, keepdims=True)
        grw_ref[...] = mm_tn(normed_two_ref[...], grad_logits)
        grad_normed = mm_nt(grad_logits, wr_ref[...]) + grad_back
        gain = gain_two_ref[...]
        scale = norm_scale(resid)
        small_ref[1:2, :] = jnp.sum(grad_normed * resid * scale, axis=0, keepdims=True)
        weighted = grad_normed * gain
        slope = scale * scale * scale * jnp.mean(weighted * resid, axis=-1, keepdims=True)
        grad_resid = up + (scale * weighted - resid * slope)
        gradresid_ref[...] = grad_resid
        grad_branch = grad_resid.astype(bf16)
        go_ref[...] = mm_tn(mixed_ref[...], grad_branch)
        grad_mixed = mm_nt(grad_branch, wo_ref[...]).astype(bf16)
        products = (grad_mixed.astype(f32) * mixed_ref[...].astype(f32)).astype(f32)
        for g in range(width // part):
            gradmixed_ref[g] = grad_mixed[:, g * part : (g + 1) * part]
            center_ref[g] = products[:, g * part : (g + 1) * part]
        acts = tokens_ref[...].astype(f32)
        normed = (acts * norm_scale(acts) * gain_one_ref[...]).astype(bf16)
        normedt_ref[...] = normed.T

    grad_mixed = gradmixed_ref[step]
    products = center_ref[step]
    dq, dk, dv = [], [], []
    for pair in range(GROUP // 2):
        cols = slice(PAIR * pair, PAIR * (pair + 1))
        query, key, value = q_ref[:, cols], k_ref[:, cols], v_ref[:, cols]
        grad = grad_mixed[:, cols]
        product = products[:, cols]
        gq = gk = gv = None
        for half in range(2):
            head = 2 * pair + half
            mask = pair_mask(query.shape, half)
            clear = lambda a: jnp.where(mask, a, jnp.zeros_like(a))
            own = clear(grad)
            center = jnp.sum(clear(product), axis=-1, keepdims=True)
            probs = probs_ref[head]
            grad_probs = mm_nt(own, value)
            grad_scores = probs.astype(f32) * (grad_probs - center)
            for at in range(length // BLOCK):
                low = length - BLOCK * (at + 1)
                piece = grad_scores[BLOCK * at : BLOCK * (at + 1), :]
                if at == 0:
                    fold_ref[head, :, :low] = jnp.zeros((BLOCK, low), f32)
                    fold_ref[head, :, low : low + length] = piece
                    fold_ref[head, :, low + length :] = jnp.zeros((BLOCK, length - low), f32)
                else:
                    fold_ref[head, :, low : low + length] += piece
            grad_scores = grad_scores.astype(bf16)
            a = mm(grad_scores, clear(key))
            b = mm_tn(grad_scores, clear(query))
            c = mm_tn(probs, own)
            gq = a if gq is None else gq + a
            gk = b if gk is None else gk + b
            gv = c if gv is None else gv + c
        dq.append(gq.astype(bf16))
        dk.append(gk.astype(bf16))
        dv.append(gv.astype(bf16))
    dq, dk, dv = (jnp.concatenate(x, axis=1) for x in (dq, dk, dv))
    normedt = normedt_ref[...]
    gq_ref[...] = mm(normedt, dq)
    gk_ref[...] = mm(normedt, dk)
    gv_ref[...] = mm(normedt, dv)
    total = mm_nt(dq, wq_ref[...]) + mm_nt(dk, wk_ref[...]) + mm_nt(dv, wv_ref[...])

    @pl.when(step == 0)
    def first():
        acc_ref[...] = total

    @pl.when(step > 0)
    def more():
        acc_ref[...] += total

    @pl.when(step == last)
    def finish():
        grad_normed = acc_ref[...]
        acts = tokens_ref[...].astype(f32)
        scale = norm_scale(acts)
        small_ref[0:1, :] = jnp.sum(grad_normed * acts * scale, axis=0, keepdims=True)
        weighted = grad_normed * gain_one_ref[...]
        slope = scale * scale * scale * jnp.mean(weighted * acts, axis=-1, keepdims=True)
        gradacts_ref[...] = (gradresid_ref[...] + (scale * weighted - acts * slope)).astype(bf16)


def back_call(
    target, route, returned, up, resid, router, normed_two, mixed, tokens, gain_one,
    gain_two, wr, wo, wq, wk, wv, q, k, v, probs,
):
    length, width = tokens.shape
    rows = returned.shape[0]
    experts = wr.shape[1]
    part = GROUP * HEAD
    whole = lambda *shape: pl.BlockSpec(shape, lambda g: (0,) * len(shape))
    columns = lambda size: pl.BlockSpec((size, part), lambda g: (0, g))
    shape = jax.ShapeDtypeStruct
    return pl.pallas_call(
        back_kernel,
        grid=(HEADS // GROUP,),
        in_specs=[
            whole(length, 2), whole(length, 1), whole(rows, width),
            whole(length, width), whole(length, width), whole(length, experts),
            whole(length, width), whole(length, width), whole(length, width),
            whole(1, width), whole(1, width), whole(width, experts), whole(width, width),
            columns(width), columns(width), columns(width),
            columns(length), columns(length), columns(length),
            pl.BlockSpec((GROUP, length, length), lambda g: (g, 0, 0)),
        ],
        out_specs=[
            whole(length, width), whole(length, width),
            pl.BlockSpec((GROUP, BLOCK, 2 * length), lambda g: (g, 0, 0)),
            columns(width), columns(width), columns(width), whole(width, width),
            whole(width, experts), whole(2, width), whole(1, experts),
        ],
        out_shape=[
            shape((length, width), bf16), shape((length, width), bf16),
            shape((HEADS, BLOCK, 2 * length), f32),
            shape((width, width), f32), shape((width, width), f32), shape((width, width), f32),
            shape((width, width), f32), shape((width, experts), f32), shape((2, width), f32),
            shape((1, experts), f32),
        ],
        scratch_shapes=[
            pltpu.VMEM((width // part, length, part), bf16),
            pltpu.VMEM((length, width), f32),
            pltpu.VMEM((width, length), bf16),
            pltpu.VMEM((length, width), f32),
            pltpu.VMEM((width // part, length, part), f32),
        ],
        compiler_params=params(),
        cost_estimate=pl.CostEstimate(
            flops=2 * length * width * width * 8 + 8 * length * length * width * 4,
            bytes_accessed=30 * 1024 * 1024, transcendentals=0,
        ),
        name="back",
    )(
        target, route, returned, up, resid, router, normed_two, mixed, tokens, gain_one,
        gain_two, wr, wo, wq, wk, wv, q, k, v, probs,
    )


def skew_kernel(lines_ref, out_ref):
    heads, block, span = out_ref.shape
    for head in range(heads):
        row = jnp.broadcast_to(lines_ref[head : head + 1, :], (block, span))
        out_ref[head] = pltpu.roll(row, span - (block - 1), 1, stride=1, stride_axis=0)


def skew_call(lines, block):
    heads, span = lines.shape
    return pl.pallas_call(
        skew_kernel,
        out_shape=jax.ShapeDtypeStruct((heads, block, span), f32),
        compiler_params=params(),
        name="skew",
    )(lines)


def exchange(buffer):
    return lax.all_to_all(buffer, AXES, split_axis=0, concat_axis=0, tiled=True)


def swap(value, bit):
    devices = lax.axis_size(AXES)
    return lax.ppermute(value, AXES, [(at, at ^ (1 << bit)) for at in range(devices)])


def own_bit(bit):
    return ((lax.axis_index(AXES) >> bit) & 1) == 1


def gather_step(held, bit):
    value, done = held
    theirs = swap(value, bit)
    upper = own_bit(bit)
    place = sum(1 for other in done if other > bit)
    value = jnp.stack(
        [jnp.where(upper, theirs, value), jnp.where(upper, value, theirs)], axis=place
    )
    return value, done + [bit]


def gather_all(value, order):
    held = (value, [])
    for bit in order:
        held = gather_step(held, bit)
    return held[0].reshape((-1,) + value.shape)


def scatter_all(parts, order):
    bits = len(order)
    held = parts.reshape((2,) * bits + parts.shape[1:])
    left = list(range(bits))[::-1]
    for bit in order:
        place = left.index(bit)
        low = lax.index_in_dim(held, 0, place, keepdims=False)
        high = lax.index_in_dim(held, 1, place, keepdims=False)
        upper = own_bit(bit)
        sent = jnp.where(upper, low, high).astype(bf16)
        held = jnp.where(upper, high, low) + swap(sent, bit).astype(f32)
        left.remove(bit)
    return held


def pack_rows(parts, width):
    lead = parts[0].shape[0]
    flat = jnp.concatenate([part.reshape(lead, -1) for part in parts], axis=1)
    short = -flat.shape[1] % width
    return jnp.pad(flat, ((0, 0), (0, short))).reshape(lead, -1, width)


def unpack_rows(packed, sizes):
    flat = packed.reshape(packed.shape[0], -1)
    out, at = [], 0
    for size in sizes:
        out.append(flat[:, at : at + size])
        at += size
    return out


def body(
    tokens,
    w_query,
    w_key,
    w_value,
    w_output,
    w_router,
    gain_attn,
    gain_ffn,
    rel_bias,
    router_bias,
    w_in,
    w_out,
    routes,
    fill_rank,
    bucket_map,
    upstream_grad,
):
    batches, length, width = tokens.shape
    devices = lax.axis_size(AXES)
    wide_bits = lax.axis_size("wide").bit_length() - 1
    bits = devices.bit_length() - 1
    local_experts = w_in.shape[0]
    experts = local_experts * devices
    capacity = max(2, 5 * length // (4 * experts))
    slots = experts * capacity
    span = 2 * length
    far = list(range(wide_bits, bits))
    near = list(range(1, wide_bits))
    turned = near[1:] + near[:1]

    expert_ids = jnp.arange(experts, dtype=jnp.int32)

    def plan(at):
        route = routes[at, :, 0]
        order = fill_rank[at]
        route_hot = (route[:, None] == expert_ids[None, :]).astype(f32)
        earlier = (order[None, :] < order[:, None]).astype(bf16)
        counts = jnp.dot(earlier, route_hot.astype(bf16), preferred_element_type=f32)
        slot = jnp.sum(counts * route_hot, axis=-1).astype(jnp.int32)
        first = jnp.where(slot < capacity, route * (2 * capacity) + slot, -1)
        second = jnp.where(first >= 0, first + capacity, -1)
        return jnp.stack([first, second], axis=0)

    spots = [plan(at) for at in range(batches)]
    raw_spots = jnp.concatenate([spots[at][at] for at in range(batches)], axis=0)
    raw_ids = jnp.arange(2 * slots, dtype=jnp.int32)
    raw_sent = jnp.dot(
        (raw_ids[:, None] == raw_spots[None, :]).astype(bf16),
        upstream_grad.reshape(batches * length, width),
        preferred_element_type=f32,
    ).astype(bf16)

    small_parts = [w_router, gain_attn, gain_ffn, rel_bias, router_bias]
    small = pack_rows([part.reshape(1, -1) for part in small_parts], width)[0]
    small_all = gather_all(small, far[::-1] + near[::-1] + [0])
    wr_all, gain_one, gain_two, rel_flat, bias_all = unpack_rows(
        small_all, [part.size for part in small_parts]
    )
    wr_all = wr_all.reshape(width, experts)
    gain_one = gain_one.reshape(1, width).astype(f32)
    gain_two = gain_two.reshape(1, width).astype(f32)
    bias_all = bias_all.reshape(1, experts).astype(f32)
    table = rel_flat.reshape(BUCKETS, HEADS).T
    bucket_hot = (
        jnp.arange(BUCKETS, dtype=jnp.int32)[:, None]
        == jnp.pad(bucket_map, (0, 1), constant_values=-1)[None, :]
    ).astype(bf16)
    skewed = skew_call(jnp.dot(table, bucket_hot, preferred_element_type=f32), BLOCK)

    shard = w_query.shape[0]
    first_half = gather_all(
        jnp.concatenate([w_query, w_key], axis=0), far[::-1] + near[::-1] + [0]
    )
    second_half = gather_all(
        jnp.concatenate([w_value, w_output], axis=0), far[::-1] + turned[::-1] + [0]
    )
    wq, wk = (first_half[:, i * shard : (i + 1) * shard].reshape(width, width) for i in range(2))
    wv, wo = (second_half[:, i * shard : (i + 1) * shard].reshape(width, width) for i in range(2))

    raw_arrived = exchange(raw_sent.reshape(devices, 2 * capacity, width))

    own = lax.axis_index(AXES).astype(jnp.int32).reshape(1)
    row = jnp.arange(slots, dtype=jnp.int32)
    place = row + (row // capacity) * capacity
    place = jnp.stack([place, place + capacity], axis=1)

    fronts, arrived, returned, saved = [], [], [], []
    for at in range(batches):
        acts = tokens[at]
        if at == 1:
            acts, raw_arrived = lax.optimization_barrier((acts, raw_arrived))
        front = front_call(
            acts, wq, wk, wv, wo, skewed, gain_one, gain_two, wr_all, bias_all, spots[at], slots
        )
        fronts.append(front)
        arrived.append(exchange(front[-1].reshape(devices, 2 * capacity, width // 2)))
    raw = raw_arrived.reshape(devices, 2, capacity, width)
    for at in range(batches):
        held = expert_call(
            own,
            arrived[at].reshape(2 * slots, width // 2),
            raw[:, at].reshape(slots, width),
            wr_all,
            bias_all,
            place,
            w_in[0],
            w_out[0],
        )
        returned.append(exchange(held[0].reshape(devices, 2 * capacity, width)))
        saved.append(held[1:])

    grad_in = sum(
        jnp.einsum("rd,rf->df", rows, grad_inner, preferred_element_type=f32)
        for rows, active, grad_inner, grad_result in saved
    )
    grad_out = sum(
        jnp.einsum("rf,rd->fd", active, grad_result, preferred_element_type=f32)
        for rows, active, grad_inner, grad_result in saved
    )

    backs = []
    for at in range(batches):
        q, k, v, probs, mixed, resid, normed_two, router, sent = fronts[at]
        backs.append(
            back_call(
                spots[at].T,
                routes[at],
                returned[at].reshape(2 * slots, width),
                upstream_grad[at],
                resid,
                router,
                normed_two,
                mixed,
                tokens[at],
                gain_one,
                gain_two,
                wr_all,
                wo,
                wq,
                wk,
                wv,
                q,
                k,
                v,
                probs,
            )
        )
    folded, g_query, g_key, g_value, g_output, g_router, g_gains, g_bias = (
        sum(back[i] for back in backs) for i in range(2, 10)
    )
    rows = BLOCK
    while rows > 1:
        rows //= 2
        folded = folded[:, :rows] + jnp.roll(folded[:, rows:], -rows, axis=2)
    diagonal = jnp.roll(folded[:, 0], BLOCK - 1, axis=1)
    g_rel = jnp.einsum(
        "hn,bn->bh", diagonal, bucket_hot.astype(f32), precision=lax.Precision.HIGHEST
    )

    def parted(value):
        return value.reshape(devices, -1, width)

    small_grads = [g_router, g_gains[0], g_gains[1], g_rel, g_bias]
    small_pack = pack_rows([part.reshape(devices, -1) for part in small_grads], width)
    low = scatter_all(
        jnp.concatenate([parted(g_query), parted(g_key)], axis=1), [0] + near + far
    )
    high = scatter_all(
        jnp.concatenate([parted(g_value), parted(g_output)], axis=1), [0] + turned + far
    )
    small_sum = scatter_all(small_pack, [0] + near + far)
    tail = unpack_rows(small_sum[None], [part.size // devices for part in small_grads])
    r_router, r_gain_one, r_gain_two, r_rel, r_bias = (
        part.reshape(shape)
        for part, shape in zip(
            tail,
            (w_router.shape, gain_attn.shape, gain_ffn.shape, rel_bias.shape, router_bias.shape),
        )
    )
    return (
        jnp.stack([back[0] for back in backs], axis=0),
        jnp.stack([back[1] for back in backs], axis=0),
        low[:shard],
        low[shard:],
        high[:shard],
        high[shard:],
        r_router,
        r_gain_one,
        r_gain_two,
        r_rel,
        r_bias,
        grad_in[None],
        grad_out[None],
    )


def solution(mesh):
    both = P(AXES)
    in_specs = (both,) * 14 + (P(), both)
    out_specs = (both,) * 13
    return jax.shard_map(body, mesh=mesh, in_specs=in_specs, out_specs=out_specs, check_vma=False)
```

```python
import functools
import jax
import jax.numpy as jnp
from jax import lax
from jax.experimental import pallas as pl
from jax.experimental.pallas import tpu as pltpu
from jax.sharding import PartitionSpec as P

HEADS = 12
HEAD = 64
BUCKETS = 32
PAIR = 2 * HEAD
GROUP = 4
BLOCK = 128
LANES = 128
AXES = ("narrow", "wide")
VMEM_BYTES = 60 * 1024 * 1024

epsilon = 1e-06
f32 = jnp.float32
bf16 = jnp.bfloat16


def mm(a, b):
    return lax.dot_general(a, b, (((1,), (0,)), ((), ())), preferred_element_type=f32)


def mm_nt(a, b):
    return lax.dot_general(a, b, (((1,), (1,)), ((), ())), preferred_element_type=f32)


def mm_tn(a, b):
    return lax.dot_general(a, b, (((0,), (0,)), ((), ())), preferred_element_type=f32)


def norm_scale(values):
    return lax.rsqrt(jnp.mean(values * values, axis=-1, keepdims=True) + epsilon)


def softmax_rows(logits):
    shifted = jnp.exp(logits - jnp.max(logits, axis=-1, keepdims=True))
    return shifted / jnp.sum(shifted, axis=-1, keepdims=True)


def pair_mask(shape, half):
    lane = lax.broadcasted_iota(jnp.int32, shape, 1)
    return (lane < HEAD) if half == 0 else (lane >= HEAD)


def params():
    return pltpu.CompilerParams(vmem_limit_bytes=VMEM_BYTES)


def front_kernel(
    tokens_ref, wq_ref, wk_ref, wv_ref, wo_ref, skew_ref, gain_one_ref, gain_two_ref, wr_ref,
    rbias_ref, spots_ref, q_ref, k_ref, v_ref, probs_ref, mixed_ref, resid_ref, normed_two_ref,
    router_ref, sent_ref, normed_ref,
):
    step = pl.program_id(0)
    length, width = tokens_ref.shape

    @pl.when(step == 0)
    def start():
        acts = tokens_ref[...].astype(f32)
        normed_ref[...] = (acts * norm_scale(acts) * gain_one_ref[...]).astype(bf16)
        resid_ref[...] = acts

    normed = normed_ref[...]
    q_ref[...] = mm(normed, wq_ref[...]).astype(bf16)
    k_ref[...] = mm(normed, wk_ref[...]).astype(bf16)
    v_ref[...] = mm(normed, wv_ref[...]).astype(bf16)
    for pair in range(GROUP // 2):
        cols = slice(PAIR * pair, PAIR * (pair + 1))
        query, key, value = q_ref[:, cols], k_ref[:, cols], v_ref[:, cols]
        out = None
        for half in range(2):
            head = 2 * pair + half
            mask = pair_mask(query.shape, half)
            scores = mm_nt(jnp.where(mask, query, jnp.zeros_like(query)), key)
            parts = []
            for at in range(length // BLOCK):
                low = length - BLOCK * (at + 1)
                part = scores[BLOCK * at : BLOCK * (at + 1), :] + skew_ref[head, :, low : low + length]
                part = jnp.exp(part - jnp.max(part, axis=-1, keepdims=True))
                total = jnp.sum(part, axis=-1, keepdims=True)
                parts.append((part * (1.0 / total)).astype(bf16))
            probs = jnp.concatenate(parts, axis=0)
            probs_ref[head] = probs
            term = mm(probs, jnp.where(mask, value, jnp.zeros_like(value)))
            out = term if out is None else out + term
        mixed_ref[:, cols] = out.astype(bf16)
    resid_ref[...] += mm(mixed_ref[...], wo_ref[...])

    @pl.when(step == pl.num_programs(0) - 1)
    def finish():
        resid = resid_ref[...]
        normed_two = (resid * norm_scale(resid) * gain_two_ref[...]).astype(bf16)
        normed_two_ref[...] = normed_two
        router_ref[...] = softmax_rows(mm(normed_two, wr_ref[...]) + rbias_ref[...])
        rows = lax.broadcasted_iota(jnp.int32, (sent_ref.shape[0], length), 0)
        left = mm((rows == spots_ref[0:1, :]).astype(bf16), normed_two[:, : width // 2])
        right = mm((rows == spots_ref[1:2, :]).astype(bf16), normed_two[:, width // 2 :])
        sent_ref[...] = (left + right).astype(bf16)


def front_call(tokens, wq, wk, wv, wo, skewed, gain_one, gain_two, wr, rbias, spots, slots):
    length, width = tokens.shape
    experts = wr.shape[1]
    part = GROUP * HEAD
    whole = lambda *shape: pl.BlockSpec(shape, lambda g: (0,) * len(shape))
    columns = lambda size: pl.BlockSpec((size, part), lambda g: (0, g))
    return pl.pallas_call(
        front_kernel,
        grid=(HEADS // GROUP,),
        in_specs=[
            whole(length, width), columns(width), columns(width), columns(width),
            pl.BlockSpec((part, width), lambda g: (g, 0)),
            pl.BlockSpec((GROUP, BLOCK, 2 * length), lambda g: (g, 0, 0)),
            whole(1, width), whole(1, width), whole(width, experts), whole(1, experts),
            whole(2, length),
        ],
        out_specs=[
            columns(length), columns(length), columns(length),
            pl.BlockSpec((GROUP, length, length), lambda g: (g, 0, 0)),
            columns(length), whole(length, width), whole(length, width), whole(length, experts),
            whole(2 * slots, width // 2),
        ],
        out_shape=[
            jax.ShapeDtypeStruct((length, width), bf16),
            jax.ShapeDtypeStruct((length, width), bf16),
            jax.ShapeDtypeStruct((length, width), bf16),
            jax.ShapeDtypeStruct((HEADS, length, length), bf16),
            jax.ShapeDtypeStruct((length, width), bf16),
            jax.ShapeDtypeStruct((length, width), f32),
            jax.ShapeDtypeStruct((length, width), bf16),
            jax.ShapeDtypeStruct((length, experts), f32),
            jax.ShapeDtypeStruct((2 * slots, width // 2), bf16),
        ],
        scratch_shapes=[pltpu.VMEM((length, width), bf16)],
        compiler_params=params(),
        cost_estimate=pl.CostEstimate(
            flops=2 * length * width * width * 4 + 4 * length * length * width * 4,
            bytes_accessed=25 * 1024 * 1024, transcendentals=HEADS * length * length,
        ),
        name="front",
    )(tokens, wq, wk, wv, wo, skewed, gain_one, gain_two, wr, rbias, spots)


def bell(values):
    size = jnp.abs(values)
    t = 1.0 / (1.0 + (0.3275911 * 0.7071067811865476) * size)
    falling = jnp.exp(-0.5 * values * values)
    poly = t * (
        0.127414796
        + t * (-0.142248368 + t * (0.7107068705 + t * (-0.7265760135 + t * 0.5307027145)))
    )
    tail = poly * falling
    return jnp.where(values < 0, tail, 1.0 - tail), falling * 0.3989422804014327


def expert_kernel(
    own_ref, arrived_ref, raw_ref, wr_ref, rbias_ref, place_ref, placed_ref, win_ref, wout_ref,
    sent_ref, rows_ref, active_ref, gradinner_ref, gradresult_ref, result_acc, rows_acc,
):
    step = pl.program_id(0)
    last = pl.num_programs(0) - 1
    count = rows_ref.shape[0]

    @pl.when(step == 0)
    def start():
        arrived = arrived_ref[...]
        ids = lax.broadcasted_iota(jnp.int32, (count, 2 * count), 1)
        half = arrived.shape[1]
        for side in range(2):
            pick = (ids == place_ref[:, side : side + 1]).astype(bf16)
            rows_ref[:, half * side : half * (side + 1)] = mm(pick, arrived).astype(bf16)
        probs = softmax_rows(mm(rows_ref[...], wr_ref[...]) + rbias_ref[...])
        mine = lax.broadcasted_iota(jnp.int32, probs.shape, 1) == own_ref[0]
        gate = jnp.sum(jnp.where(mine, probs, 0.0), axis=-1, keepdims=True)
        gradresult_ref[...] = (gate * raw_ref[...].astype(f32)).astype(bf16)

    inner = mm(rows_ref[...], win_ref[...])
    grad_active = mm_nt(gradresult_ref[...], wout_ref[...])
    share, density = bell(inner)
    active = (inner * share).astype(bf16)
    grad_inner = (grad_active * (share + inner * density)).astype(bf16)
    active_ref[...] = active
    gradinner_ref[...] = grad_inner
    result = mm(active, wout_ref[...])
    grad_rows = mm_nt(grad_inner, win_ref[...])

    @pl.when(step == 0)
    def first():
        result_acc[...] = result
        rows_acc[...] = grad_rows

    @pl.when(step > 0)
    def more():
        result_acc[...] += result
        rows_acc[...] += grad_rows

    @pl.when(step == last)
    def finish():
        ids = lax.broadcasted_iota(jnp.int32, (2 * count, count), 0)
        sent_ref[...] = (
            mm((ids == placed_ref[0:1, :]).astype(bf16), result_acc[...].astype(bf16))
            + mm((ids == placed_ref[1:2, :]).astype(bf16), rows_acc[...].astype(bf16))
        ).astype(bf16)


def expert_call(own, arrived, raw, wr, rbias, place, w_in, w_out, part=1024):
    count, width = raw.shape
    hidden = w_in.shape[1]
    experts = wr.shape[1]
    whole = lambda *shape: pl.BlockSpec(shape, lambda g, own: (0,) * len(shape))
    columns = lambda n: pl.BlockSpec((n, part), lambda g, own: (0, g))
    return pl.pallas_call(
        expert_kernel,
        grid_spec=pltpu.PrefetchScalarGridSpec(
            num_scalar_prefetch=1,
            grid=(hidden // part,),
            in_specs=[
                whole(2 * count, width // 2), whole(count, width), whole(width, experts),
                whole(1, experts), whole(count, 2), whole(2, count),
                columns(width), pl.BlockSpec((part, width), lambda g, own: (g, 0)),
            ],
            out_specs=[
                whole(2 * count, width), whole(count, width), columns(count), columns(count),
                whole(count, width),
            ],
            scratch_shapes=[pltpu.VMEM((count, width), f32), pltpu.VMEM((count, width), f32)],
        ),
        out_shape=[
            jax.ShapeDtypeStruct((2 * count, width), bf16),
            jax.ShapeDtypeStruct((count, width), bf16),
            jax.ShapeDtypeStruct((count, hidden), bf16),
            jax.ShapeDtypeStruct((count, hidden), bf16),
            jax.ShapeDtypeStruct((count, width), bf16),
        ],
        compiler_params=params(),
        cost_estimate=pl.CostEstimate(
            flops=8 * count * width * hidden, bytes_accessed=20 * 1024 * 1024,
            transcendentals=count * hidden,
        ),
        name="expert",
    )(own, arrived, raw, wr, rbias, place, place.T, w_in, w_out)


def back_rows_kernel(
    target_ref, route_ref, returned_ref, up_ref, resid_ref, router_ref, normed_two_ref, mixed_ref,
    gain_two_ref, wr_ref, wo_ref, *refs,
):
    output_ref, gradresid_ref, gradmixed_ref, product_ref = refs[-8:-4]
    go_ref, grw_ref, ggain_ref, gbias_ref = refs[-4:]
    length, experts = router_ref.shape
    returned = returned_ref[...]
    ids = lax.broadcasted_iota(jnp.int32, (length, returned.shape[0]), 1)
    expert_rows = mm((ids == target_ref[:, 0:1]).astype(bf16), returned)
    grad_back = mm((ids == target_ref[:, 1:2]).astype(bf16), returned)
    up = up_ref[...].astype(f32)
    resid = resid_ref[...]
    router = router_ref[...]
    hot = lax.broadcasted_iota(jnp.int32, (length, experts), 1) == route_ref[...]
    gate = jnp.sum(jnp.where(hot, router, 0.0), axis=-1, keepdims=True)
    output_ref[...] = (resid + gate * expert_rows).astype(bf16)
    grad_gate = jnp.sum(up * expert_rows, axis=-1, keepdims=True)
    grad_logits = (router * (jnp.where(hot, grad_gate, 0.0) - gate * grad_gate)).astype(bf16)
    gbias_ref[...] = jnp.sum(grad_logits.astype(f32), axis=0, keepdims=True)
    grw_ref[...] = mm_tn(normed_two_ref[...], grad_logits)
    grad_normed = mm_nt(grad_logits, wr_ref[...]) + grad_back
    scale = norm_scale(resid)
    ggain_ref[...] = jnp.sum(grad_normed * resid * scale, axis=0, keepdims=True)
    weighted = grad_normed * gain_two_ref[...]
    slope = scale * scale * scale * jnp.mean(weighted * resid, axis=-1, keepdims=True)
    grad_resid = up + (scale * weighted - resid * slope)
    gradresid_ref[...] = grad_resid
    grad_branch = grad_resid.astype(bf16)
    mixed = mixed_ref[...]
    go = mm_tn(mixed, grad_branch)
    if len(refs) > 8:
        go = go + refs[0][...]
    go_ref[...] = go.astype(go_ref.dtype)
    grad_mixed = mm_nt(grad_branch, wo_ref[...]).astype(bf16)
    gradmixed_ref[...] = grad_mixed
    product_ref[...] = grad_mixed.astype(f32) * mixed.astype(f32)


def back_rows_call(
    target, route, returned, up, resid, router, normed_two, mixed, gain_two, wr, wo, prior
):
    length, width = up.shape
    experts = wr.shape[1]
    shape = jax.ShapeDtypeStruct
    return pl.pallas_call(
        back_rows_kernel,
        out_shape=[
            shape((length, width), bf16), shape((length, width), f32),
            shape((length, width), bf16), shape((length, width), f32),
            shape((width, width), f32 if prior is None else bf16),
            shape((width, experts), f32), shape((1, width), f32), shape((1, experts), f32),
        ],
        compiler_params=params(),
        cost_estimate=pl.CostEstimate(
            flops=2 * length * width * (2 * width + 2 * returned.shape[0]),
            bytes_accessed=18 * 1024 * 1024, transcendentals=0,
        ),
        name="back_rows",
    )(
        target, route, returned, up, resid, router, normed_two, mixed, gain_two, wr, wo,
        *([] if prior is None else [prior]),
    )


def back_heads_kernel(
    tokens_ref, gain_ref, gradmixed_ref, product_ref, wq_ref, wk_ref, wv_ref, q_ref, k_ref, v_ref,
    probs_ref, gradresid_ref, *refs,
):
    prior_ref = refs[0] if len(refs) > 7 else None
    line_ref, gw_ref, gradacts_ref, ggain_ref, normedt_ref, acc_ref, fold_ref = refs[-7:]
    step = pl.program_id(0)
    last = pl.num_programs(0) - 1
    length, width = tokens_ref.shape
    span = 2 * length

    @pl.when(step == 0)
    def start():
        acts = tokens_ref[...].astype(f32)
        normed = (acts * norm_scale(acts) * gain_ref[...]).astype(bf16)
        normedt_ref[...] = normed.T
        acc_ref[...] = jnp.zeros_like(acc_ref)

    dq, dk, dv = [], [], []
    for pair in range(GROUP // 2):
        cols = slice(PAIR * pair, PAIR * (pair + 1))
        query, key, value = q_ref[:, cols], k_ref[:, cols], v_ref[:, cols]
        grad = gradmixed_ref[:, cols]
        product = product_ref[:, cols]
        gq = gk = gv = None
        for half in range(2):
            head = 2 * pair + half
            mask = pair_mask(query.shape, half)
            clear = lambda a: jnp.where(mask, a, jnp.zeros_like(a))
            own = clear(grad)
            center = jnp.sum(clear(product), axis=-1, keepdims=True)
            probs = probs_ref[head]
            grad_probs = mm_nt(own, value)
            grad_scores = probs.astype(f32) * (grad_probs - center)
            for at in range(length // BLOCK):
                low = length - BLOCK * (at + 1)
                piece = grad_scores[BLOCK * at : BLOCK * (at + 1), :]
                if at == 0:
                    fold_ref[:, :low] = jnp.zeros((BLOCK, low), f32)
                    fold_ref[:, low : low + length] = piece
                    fold_ref[:, low + length :] = jnp.zeros((BLOCK, length - low), f32)
                else:
                    fold_ref[:, low : low + length] += piece
            rows = fold_ref[...]
            size = BLOCK
            while size > 1:
                size //= 2
                rows = rows[:size] + pltpu.roll(rows[size:], span - size, 1)
            line_ref[0, head : head + 1, :] = pltpu.roll(rows, BLOCK - 1, 1)
            grad_scores = grad_scores.astype(bf16)
            a = mm(grad_scores, clear(key))
            b = mm_tn(grad_scores, clear(query))
            c = mm_tn(probs, own)
            gq = a if gq is None else gq + a
            gk = b if gk is None else gk + b
            gv = c if gv is None else gv + c
        dq.append(gq.astype(bf16))
        dk.append(gk.astype(bf16))
        dv.append(gv.astype(bf16))
    dq, dk, dv = (jnp.concatenate(x, axis=1) for x in (dq, dk, dv))
    normedt = normedt_ref[...]
    for i, grad in enumerate((dq, dk, dv)):
        total = mm(normedt, grad)
        if prior_ref is not None:
            total = total + prior_ref[i]
        gw_ref[i] = total.astype(gw_ref.dtype)
    acc_ref[...] += mm_nt(dq, wq_ref[...]) + mm_nt(dk, wk_ref[...]) + mm_nt(dv, wv_ref[...])

    @pl.when(step == last)
    def finish():
        grad_normed = acc_ref[...]
        acts = tokens_ref[...].astype(f32)
        scale = norm_scale(acts)
        ggain_ref[...] = jnp.sum(grad_normed * acts * scale, axis=0, keepdims=True)
        weighted = grad_normed * gain_ref[...]
        slope = scale * scale * scale * jnp.mean(weighted * acts, axis=-1, keepdims=True)
        grad_acts = gradresid_ref[...] + (scale * weighted - acts * slope)
        gradacts_ref[...] = grad_acts.astype(bf16)


def back_heads_call(
    tokens, gain, grad_mixed, product, wq, wk, wv, q, k, v, probs, grad_resid, prior
):
    length, width = tokens.shape
    part = GROUP * HEAD
    groups = HEADS // GROUP
    whole = lambda *shape: pl.BlockSpec(shape, lambda g: (0,) * len(shape))
    columns = lambda size: pl.BlockSpec((size, part), lambda g: (0, g))
    shape = jax.ShapeDtypeStruct
    weights = pl.BlockSpec((3, width, part), lambda g: (0, 0, g))
    return pl.pallas_call(
        back_heads_kernel,
        grid=(groups,),
        in_specs=[
            whole(length, width), whole(1, width), columns(length), columns(length),
            columns(width), columns(width), columns(width),
            columns(length), columns(length), columns(length),
            pl.BlockSpec((GROUP, length, length), lambda g: (g, 0, 0)), whole(length, width),
            *([] if prior is None else [weights]),
        ],
        out_specs=[
            pl.BlockSpec((1, GROUP, 2 * length), lambda g: (g, 0, 0)), weights,
            whole(length, width), whole(1, width),
        ],
        out_shape=[
            shape((groups, GROUP, 2 * length), f32),
            shape((3, width, width), f32 if prior is None else bf16),
            shape((length, width), bf16), shape((1, width), f32),
        ],
        scratch_shapes=[
            pltpu.VMEM((width, length), bf16), pltpu.VMEM((length, width), f32),
            pltpu.VMEM((BLOCK, 2 * length), f32),
        ],
        compiler_params=params(),
        cost_estimate=pl.CostEstimate(
            flops=groups * (2 * length * width * part * 6 + 8 * length * length * part * 4),
            bytes_accessed=groups * 8 * 1024 * 1024, transcendentals=0,
        ),
        name="back_heads",
    )(
        tokens, gain, grad_mixed, product, wq, wk, wv, q, k, v, probs, grad_resid,
        *([] if prior is None else [prior]),
    )


def pack_kernel(*refs):
    for at, ref in enumerate(refs[:-1]):
        refs[-1][at] = ref[...]


def pack_call(*parts):
    return pl.pallas_call(
        pack_kernel,
        out_shape=jax.ShapeDtypeStruct((len(parts), *parts[0].shape), parts[0].dtype),
        compiler_params=params(),
        name="pack",
    )(*parts)


def skew_kernel(lines_ref, out_ref):
    heads, block, span = out_ref.shape
    for head in range(heads):
        row = jnp.broadcast_to(lines_ref[head : head + 1, :], (8, span))
        base = pltpu.roll(row, span - (block - 1), 1, stride=1, stride_axis=0)
        for at in range(0, block, 8):
            out_ref[head, at : at + 8, :] = base if at == 0 else pltpu.roll(base, at, 1)


def skew_call(lines, block):
    heads, span = lines.shape
    return pl.pallas_call(
        skew_kernel,
        out_shape=jax.ShapeDtypeStruct((heads, block, span), f32),
        compiler_params=params(),
        name="skew",
    )(lines)


def exchange(buffer):
    return lax.all_to_all(buffer, AXES, split_axis=0, concat_axis=0, tiled=True)


def swap(value, bit):
    devices = lax.axis_size(AXES)
    return lax.ppermute(value, AXES, [(at, at ^ (1 << bit)) for at in range(devices)])


def own_bit(bit):
    return ((lax.axis_index(AXES) >> bit) & 1) == 1


def gather_step(held, bit):
    value, done = held
    theirs = swap(value, bit)
    upper = own_bit(bit)
    place = sum(1 for other in done if other > bit)
    value = jnp.stack(
        [jnp.where(upper, theirs, value), jnp.where(upper, value, theirs)], axis=place
    )
    return value, done + [bit]


def gather_all(value, order):
    held = (value, [])
    for bit in order:
        held = gather_step(held, bit)
    return held[0].reshape((-1,) + value.shape)


def scatter_step(held, bit):
    value, left = held
    place = 1 + left.index(bit)
    low = lax.index_in_dim(value, 0, place, keepdims=False)
    high = lax.index_in_dim(value, 1, place, keepdims=False)
    upper = own_bit(bit)
    sent = jnp.where(upper, low, high).astype(bf16)
    value = jnp.where(upper, high, low).astype(f32) + swap(sent, bit).astype(f32)
    return value, [other for other in left if other != bit]


def pack_rows(parts, width):
    lead = parts[0].shape[0]
    flat = jnp.concatenate([part.reshape(lead, -1) for part in parts], axis=1)
    short = -flat.shape[1] % width
    return jnp.pad(flat, ((0, 0), (0, short))).reshape(lead, -1, width)


def unpack_rows(packed, sizes):
    flat = packed.reshape(packed.shape[0], -1)
    out, at = [], 0
    for size in sizes:
        out.append(flat[:, at : at + size])
        at += size
    return out


def body(
    tokens,
    w_query,
    w_key,
    w_value,
    w_output,
    w_router,
    gain_attn,
    gain_ffn,
    rel_bias,
    router_bias,
    w_in,
    w_out,
    routes,
    fill_rank,
    bucket_map,
    upstream_grad,
):
    batches, length, width = tokens.shape
    devices = lax.axis_size(AXES)
    wide_bits = lax.axis_size("wide").bit_length() - 1
    bits = devices.bit_length() - 1
    local_experts = w_in.shape[0]
    experts = local_experts * devices
    capacity = max(2, 5 * length // (4 * experts))
    slots = experts * capacity
    span = 2 * length
    far = list(range(wide_bits, bits))
    near = list(range(1, wide_bits))
    turned = near[1:] + near[:1]

    expert_ids = jnp.arange(experts, dtype=jnp.int32)

    def plan(at):
        route = routes[at, :, 0]
        order = fill_rank[at]
        route_hot = (route[:, None] == expert_ids[None, :]).astype(f32)
        earlier = (order[None, :] < order[:, None]).astype(bf16)
        counts = jnp.dot(earlier, route_hot.astype(bf16), preferred_element_type=f32)
        slot = jnp.sum(counts * route_hot, axis=-1).astype(jnp.int32)
        first = jnp.where(slot < capacity, route * (2 * capacity) + slot, -1)
        second = jnp.where(first >= 0, first + capacity, -1)
        return jnp.stack([first, second], axis=0)

    spots = [plan(at) for at in range(batches)]
    raw_spots = jnp.concatenate([spots[at][at] for at in range(batches)], axis=0)
    raw_ids = jnp.arange(2 * slots, dtype=jnp.int32)
    raw_sent = jnp.dot(
        (raw_ids[:, None] == raw_spots[None, :]).astype(bf16),
        upstream_grad.reshape(batches * length, width),
        preferred_element_type=f32,
    ).astype(bf16)

    small_parts = [w_router, gain_attn, gain_ffn, rel_bias, router_bias]
    small = pack_rows([part.reshape(1, -1) for part in small_parts], 8 * LANES)
    square = (pack_call(w_query, w_key, w_value, w_output), [])
    small = (small.reshape(8, LANES), [])
    for bit in far[::-1]:
        square, small = gather_step(square, bit), gather_step(small, bit)
    square, small, raw_sent = lax.optimization_barrier((square[0], small[0], raw_sent))
    raw_arrived = exchange(raw_sent.reshape(devices, 2 * capacity, width))
    small, done = (small, far[::-1]), far[::-1]
    square = square.reshape((2,) * len(far) + (4, -1, width))
    low, high = ((lax.slice_in_dim(square, i, i + 2, axis=len(far)), done) for i in (0, 2))
    for one, two in zip(near[::-1] + [0], turned[::-1] + [0]):
        small = gather_step(small, one)
        low, high = gather_step(low, one), gather_step(high, two)
    wq, wk, wv, wo = (
        lax.index_in_dim(part[0].reshape(devices, 2, -1, width), i, 1).reshape(width, width)
        for part in (low, high)
        for i in range(2)
    )
    small_all = small[0]

    wr_all, gain_one, gain_two, rel_flat, bias_all = unpack_rows(
        small_all.reshape(devices, 1, -1), [part.size for part in small_parts]
    )
    wr_all = wr_all.reshape(width, experts)
    gain_one = gain_one.reshape(1, width).astype(f32)
    gain_two = gain_two.reshape(1, width).astype(f32)
    bias_all = bias_all.reshape(1, experts).astype(f32)
    table = rel_flat.reshape(BUCKETS, HEADS).T
    bucket_hot = (
        jnp.arange(BUCKETS, dtype=jnp.int32)[:, None]
        == jnp.pad(bucket_map, (0, 1), constant_values=-1)[None, :]
    ).astype(bf16)
    skewed = skew_call(jnp.dot(table, bucket_hot, preferred_element_type=f32), BLOCK)

    own = lax.axis_index(AXES).astype(jnp.int32).reshape(1)
    row = jnp.arange(slots, dtype=jnp.int32)
    place = row + (row // capacity) * capacity
    place = jnp.stack([place, place + capacity], axis=1)

    fronts, arrived, returned, saved = [], [], [], []
    for at in range(batches):
        acts = tokens[at]
        if at == 1:
            acts, raw_arrived = lax.optimization_barrier((acts, raw_arrived))
        front = front_call(
            acts, wq, wk, wv, wo, skewed, gain_one, gain_two, wr_all, bias_all, spots[at], slots
        )
        fronts.append(front)
        arrived.append(exchange(front[-1].reshape(devices, 2 * capacity, width // 2)))
    raw = raw_arrived.reshape(devices, 2, capacity, width)
    for at in range(batches):
        held = expert_call(
            own,
            arrived[at].reshape(2 * slots, width // 2),
            raw[:, at].reshape(slots, width),
            wr_all,
            bias_all,
            place,
            w_in[0],
            w_out[0],
        )
        returned.append(exchange(held[0].reshape(devices, 2 * capacity, width)))
        saved.append(held[1:])

    grad_in = sum(
        jnp.einsum("rd,rf->df", rows, grad_inner, preferred_element_type=f32)
        for rows, active, grad_inner, grad_result in saved
    )
    grad_out = sum(
        jnp.einsum("rf,rd->fd", active, grad_result, preferred_element_type=f32)
        for rows, active, grad_inner, grad_result in saved
    )

    row_parts, head_parts = [], []
    g_output = g_heads = None
    for at in range(batches):
        q, k, v, probs, mixed, resid, normed_two, router, sent = fronts[at]
        row_part = back_rows_call(
            spots[at].T, routes[at], returned[at].reshape(2 * slots, width), upstream_grad[at],
            resid, router, normed_two, mixed, gain_two, wr_all, wo, g_output,
        )
        g_output = row_part[4]
        head_part = back_heads_call(
            tokens[at], gain_one, row_part[2], row_part[3], wq, wk, wv, q, k, v, probs,
            row_part[1], g_heads,
        )
        g_heads = head_part[1]
        row_parts.append(row_part)
        head_parts.append(head_part)

    parts = jnp.concatenate([g_heads, g_output[None]], axis=0)
    held = scatter_step((parts.reshape((4,) + (2,) * bits + (-1, width)), list(range(bits))[::-1]), 0)
    low, high = ((held[0][i : i + 2], held[1]) for i in (0, 2))
    for one, two in zip(near, turned):
        low, high = scatter_step(low, one), scatter_step(high, two)
    held = (jnp.concatenate([low[0], high[0]], axis=0), low[1])
    for bit in far:
        held = scatter_step(held, bit)
    r_query, r_key, r_value, r_output = (held[0][i] for i in range(4))

    g_router, g_gain_two, g_bias = (
        sum(row_part[i] for row_part in row_parts) for i in range(5, 8)
    )
    lines, g_gain_one = (sum(part[i] for part in head_parts) for i in (0, 3))
    g_rel = jnp.einsum(
        "hn,bn->bh",
        lines.reshape(HEADS, span),
        bucket_hot.astype(f32),
        precision=lax.Precision.HIGHEST,
    )
    small_grads = [g_router, g_gain_one, g_gain_two, g_rel, g_bias]
    small_pack = pack_rows([part.reshape(devices, -1) for part in small_grads], 8 * LANES)
    held = (
        small_pack.reshape((1,) + (2,) * bits + (-1, LANES)), list(range(bits))[::-1]
    )
    for bit in [0] + near + far:
        held = scatter_step(held, bit)
    small_sum = held[0]
    tail = unpack_rows(small_sum.reshape(1, 1, -1), [part.size // devices for part in small_grads])
    r_router, r_gain_one, r_gain_two, r_rel, r_bias = (
        part.reshape(shape)
        for part, shape in zip(
            tail,
            (w_router.shape, gain_attn.shape, gain_ffn.shape, rel_bias.shape, router_bias.shape),
        )
    )
    return (
        jnp.stack([row_part[0] for row_part in row_parts], axis=0),
        jnp.stack([part[2] for part in head_parts], axis=0),
        r_query,
        r_key,
        r_value,
        r_output,
        r_router,
        r_gain_one,
        r_gain_two,
        r_rel,
        r_bias,
        grad_in[None],
        grad_out[None],
    )


def solution(mesh):
    both = P(AXES)
    in_specs = (both,) * 14 + (P(), both)
    out_specs = (both,) * 13
    return jax.shard_map(body, mesh=mesh, in_specs=in_specs, out_specs=out_specs, check_vma=False)
```

```python
import functools
import jax
import jax.numpy as jnp
from jax import lax
from jax.experimental import pallas as pl
from jax.experimental.pallas import tpu as pltpu
from jax.sharding import PartitionSpec as P

HEADS = 12
HEAD = 64
BUCKETS = 32
PAIR = 2 * HEAD
GROUP = 4
BLOCK = 128
LANES = 128
AXES = ("narrow", "wide")
MIB = 1024 * 1024

epsilon = 1e-06
f32 = jnp.float32
bf16 = jnp.bfloat16


def mm(a, b):
    return lax.dot_general(a, b, (((1,), (0,)), ((), ())), preferred_element_type=f32)


def mm_nt(a, b):
    return lax.dot_general(a, b, (((1,), (1,)), ((), ())), preferred_element_type=f32)


def mm_tn(a, b):
    return lax.dot_general(a, b, (((0,), (0,)), ((), ())), preferred_element_type=f32)


def norm_scale(values):
    return lax.rsqrt(jnp.mean(values * values, axis=-1, keepdims=True) + epsilon)


def softmax_rows(logits):
    shifted = jnp.exp(logits - jnp.max(logits, axis=-1, keepdims=True))
    return shifted / jnp.sum(shifted, axis=-1, keepdims=True)


def pair_mask(shape, half):
    lane = lax.broadcasted_iota(jnp.int32, shape, 1)
    return (lane < HEAD) if half == 0 else (lane >= HEAD)


def params(size):
    return pltpu.CompilerParams(vmem_limit_bytes=size * MIB)


def front_kernel(
    tokens_ref, wq_ref, wk_ref, wv_ref, wo_ref, skew_ref, gain_one_ref, gain_two_ref, spots_ref,
    q_ref, k_ref, v_ref, mixed_ref, lse_ref, sent_ref, normed_ref, resid_ref,
):
    step = pl.program_id(0)
    length, width = tokens_ref.shape

    @pl.when(step == 0)
    def start():
        acts = tokens_ref[...].astype(f32)
        normed_ref[...] = (acts * norm_scale(acts) * gain_one_ref[...]).astype(bf16)
        resid_ref[...] = acts

    normed = normed_ref[...]
    q_ref[...] = mm(normed, wq_ref[...]).astype(bf16)
    k_ref[...] = mm(normed, wk_ref[...]).astype(bf16)
    v_ref[...] = mm(normed, wv_ref[...]).astype(bf16)
    for pair in range(GROUP // 2):
        cols = slice(PAIR * pair, PAIR * (pair + 1))
        query, key, value = q_ref[:, cols], k_ref[:, cols], v_ref[:, cols]
        out = None
        for half in range(2):
            head = 2 * pair + half
            mask = pair_mask(query.shape, half)
            scores = mm_nt(jnp.where(mask, query, jnp.zeros_like(query)), key)
            parts = []
            for at in range(length // BLOCK):
                rows = slice(BLOCK * at, BLOCK * (at + 1))
                low = length - BLOCK * (at + 1)
                part = scores[rows, :] + skew_ref[head, :, low : low + length].astype(f32)
                peak = jnp.max(part, axis=-1, keepdims=True)
                part = jnp.exp(part - peak)
                total = jnp.sum(part, axis=-1, keepdims=True)
                lse_ref[0, rows, head : head + 1] = peak + jnp.log(total)
                parts.append((part * (1.0 / total)).astype(bf16))
            probs = jnp.concatenate(parts, axis=0)
            term = mm(probs, jnp.where(mask, value, jnp.zeros_like(value)))
            out = term if out is None else out + term
        mixed_ref[:, cols] = out.astype(bf16)
    resid_ref[...] += mm(mixed_ref[...], wo_ref[...])

    @pl.when(step == pl.num_programs(0) - 1)
    def finish():
        resid = resid_ref[...]
        normed_two = (resid * norm_scale(resid) * gain_two_ref[...]).astype(bf16)
        rows = lax.broadcasted_iota(jnp.int32, (sent_ref.shape[0], length), 0)
        left = mm((rows == spots_ref[0:1, :]).astype(bf16), normed_two[:, : width // 2])
        right = mm((rows == spots_ref[1:2, :]).astype(bf16), normed_two[:, width // 2 :])
        sent_ref[...] = (left + right).astype(bf16)


def front_call(tokens, wq, wk, wv, wo, skewed, gain_one, gain_two, spots, slots):
    length, width = tokens.shape
    part = GROUP * HEAD
    groups = HEADS // GROUP
    whole = lambda *shape: pl.BlockSpec(shape, lambda g: (0,) * len(shape))
    columns = lambda rows: pl.BlockSpec((rows, part), lambda g: (0, g))
    shape = jax.ShapeDtypeStruct
    return pl.pallas_call(
        front_kernel,
        grid=(groups,),
        in_specs=[
            whole(length, width), columns(width), columns(width), columns(width),
            pl.BlockSpec((part, width), lambda g: (g, 0)),
            pl.BlockSpec((GROUP, BLOCK, skewed.shape[2]), lambda g: (g, 0, 0)),
            whole(1, width), whole(1, width), whole(2, length),
        ],
        out_specs=[
            columns(length), columns(length), columns(length), columns(length),
            pl.BlockSpec((1, length, GROUP), lambda g: (g, 0, 0)),
            whole(2 * slots, width // 2),
        ],
        out_shape=[
            *(4 * [shape((length, width), bf16)]), shape((groups, length, GROUP), f32),
            shape((2 * slots, width // 2), bf16),
        ],
        scratch_shapes=[pltpu.VMEM((length, width), bf16), pltpu.VMEM((length, width), f32)],
        compiler_params=params(60),
        cost_estimate=pl.CostEstimate(
            flops=2 * length * width * width * 4 + 4 * length * length * width * 4,
            bytes_accessed=14 * MIB, transcendentals=HEADS * length * length,
        ),
        name="front",
    )(tokens, wq, wk, wv, wo, skewed, gain_one, gain_two, spots)


def bell(values):
    size = jnp.abs(values)
    t = 1.0 / (1.0 + (0.3275911 * 0.7071067811865476) * size)
    falling = jnp.exp(-0.5 * values * values)
    poly = t * (
        0.127414796
        + t * (-0.142248368 + t * (0.7107068705 + t * (-0.7265760135 + t * 0.5307027145)))
    )
    tail = poly * falling
    return jnp.where(values < 0, tail, 1.0 - tail), falling * 0.3989422804014327


def expert_kernel(
    own_ref, arrived_ref, raw_ref, wr_ref, rbias_ref, place_ref, placed_ref, win_ref, wout_ref,
    sent_ref, rows_ref, active_ref, gradinner_ref, gradresult_ref, result_acc, rows_acc,
):
    step = pl.program_id(0)
    last = pl.num_programs(0) - 1
    count = rows_ref.shape[0]
    unit = place_ref.shape[0]

    @pl.when(step == 0)
    def start():
        half = arrived_ref.shape[1]
        ids = lax.broadcasted_iota(jnp.int32, (unit, 2 * unit), 1)
        for side in range(2):
            pick = (ids == place_ref[:, side : side + 1]).astype(bf16)
            for at in range(0, count, unit):
                rows_ref[at : at + unit, half * side : half * (side + 1)] = mm(
                    pick, arrived_ref[2 * at : 2 * (at + unit), :]
                ).astype(bf16)
        probs = softmax_rows(mm(rows_ref[...], wr_ref[...]) + rbias_ref[...])
        mine = lax.broadcasted_iota(jnp.int32, probs.shape, 1) == own_ref[0]
        gate = jnp.sum(jnp.where(mine, probs, 0.0), axis=-1, keepdims=True)
        gradresult_ref[...] = (gate * raw_ref[...].astype(f32)).astype(bf16)

    inner = mm(rows_ref[...], win_ref[...])
    grad_active = mm_nt(gradresult_ref[...], wout_ref[...])
    share, density = bell(inner)
    active = (inner * share).astype(bf16)
    grad_inner = (grad_active * (share + inner * density)).astype(bf16)
    active_ref[...] = active
    gradinner_ref[...] = grad_inner
    result = mm(active, wout_ref[...])
    grad_rows = mm_nt(grad_inner, win_ref[...])

    @pl.when(step == 0)
    def first():
        result_acc[...] = result
        rows_acc[...] = grad_rows

    @pl.when(step > 0)
    def more():
        result_acc[...] += result
        rows_acc[...] += grad_rows

    @pl.when(step == last)
    def finish():
        ids = lax.broadcasted_iota(jnp.int32, (2 * unit, unit), 0)
        picks = [(ids == placed_ref[side : side + 1, :]).astype(bf16) for side in range(2)]
        for at in range(0, count, unit):
            sent_ref[2 * at : 2 * (at + unit), :] = (
                mm(picks[0], result_acc[at : at + unit, :].astype(bf16))
                + mm(picks[1], rows_acc[at : at + unit, :].astype(bf16))
            ).astype(bf16)


def expert_call(own, arrived, raw, wr, rbias, place, w_in, w_out, part=1024):
    count, width = raw.shape
    hidden = w_in.shape[1]
    experts = wr.shape[1]
    whole = lambda *shape: pl.BlockSpec(shape, lambda g, own: (0,) * len(shape))
    columns = lambda n: pl.BlockSpec((n, part), lambda g, own: (0, g))
    return pl.pallas_call(
        expert_kernel,
        grid_spec=pltpu.PrefetchScalarGridSpec(
            num_scalar_prefetch=1,
            grid=(hidden // part,),
            in_specs=[
                whole(2 * count, width // 2), whole(count, width), whole(width, experts),
                whole(1, experts), whole(*place.shape), whole(*place.shape[::-1]),
                columns(width), pl.BlockSpec((part, width), lambda g, own: (g, 0)),
            ],
            out_specs=[
                whole(2 * count, width), whole(count, width), columns(count), columns(count),
                whole(count, width),
            ],
            scratch_shapes=[pltpu.VMEM((count, width), f32), pltpu.VMEM((count, width), f32)],
        ),
        out_shape=[
            jax.ShapeDtypeStruct((2 * count, width), bf16),
            jax.ShapeDtypeStruct((count, width), bf16),
            jax.ShapeDtypeStruct((count, hidden), bf16),
            jax.ShapeDtypeStruct((count, hidden), bf16),
            jax.ShapeDtypeStruct((count, width), bf16),
        ],
        compiler_params=params(60),
        cost_estimate=pl.CostEstimate(
            flops=8 * count * width * hidden, bytes_accessed=20 * MIB,
            transcendentals=count * hidden,
        ),
        name="expert",
    )(own, arrived, raw, wr, rbias, place, place.T, w_in, w_out)


def back_rows_kernel(
    target_ref, route_ref, returned_ref, up_ref, tokens_ref, mixed_ref, gain_ref, wr_ref,
    rbias_ref, wo_ref, *refs,
):
    output_ref, gradresid_ref, gradmixed_ref, go_ref, grw_ref, ggain_ref, gbias_ref = refs[-7:]
    length = up_ref.shape[0]
    experts = wr_ref.shape[1]
    mixed = mixed_ref[...]
    resid = tokens_ref[...].astype(f32) + mm(mixed, wo_ref[...])
    scale = norm_scale(resid)
    normed_two = (resid * scale * gain_ref[...]).astype(bf16)
    router = softmax_rows(mm(normed_two, wr_ref[...]) + rbias_ref[...])
    returned = returned_ref[...]
    ids = lax.broadcasted_iota(jnp.int32, (length, returned.shape[0]), 1)
    expert_rows = mm((ids == target_ref[:, 0:1]).astype(bf16), returned)
    grad_back = mm((ids == target_ref[:, 1:2]).astype(bf16), returned)
    up = up_ref[...].astype(f32)
    hot = lax.broadcasted_iota(jnp.int32, (length, experts), 1) == route_ref[...]
    gate = jnp.sum(jnp.where(hot, router, 0.0), axis=-1, keepdims=True)
    output_ref[...] = (resid + gate * expert_rows).astype(bf16)
    grad_gate = jnp.sum(up * expert_rows, axis=-1, keepdims=True)
    grad_logits = (router * (jnp.where(hot, grad_gate, 0.0) - gate * grad_gate)).astype(bf16)
    gbias_ref[...] = jnp.sum(grad_logits.astype(f32), axis=0, keepdims=True)
    grw_ref[...] = mm_tn(normed_two, grad_logits)
    grad_normed = mm_nt(grad_logits, wr_ref[...]) + grad_back
    ggain_ref[...] = jnp.sum(grad_normed * resid * scale, axis=0, keepdims=True)
    weighted = grad_normed * gain_ref[...]
    slope = scale * scale * scale * jnp.mean(weighted * resid, axis=-1, keepdims=True)
    grad_resid = up + (scale * weighted - resid * slope)
    gradresid_ref[...] = grad_resid
    grad_branch = grad_resid.astype(bf16)
    go = mm_tn(mixed, grad_branch)
    if len(refs) > 7:
        go = go + refs[0][...].astype(f32)
    go_ref[...] = go.astype(bf16)
    gradmixed_ref[...] = mm_nt(grad_branch, wo_ref[...]).astype(bf16)


def back_rows_call(target, route, returned, up, tokens, mixed, gain, wr, rbias, wo, prior):
    length, width = up.shape
    experts = wr.shape[1]
    shape = jax.ShapeDtypeStruct
    return pl.pallas_call(
        back_rows_kernel,
        out_shape=[
            shape((length, width), bf16), shape((length, width), f32),
            shape((length, width), bf16), shape((width, width), bf16),
            shape((width, experts), f32), shape((1, width), f32), shape((1, experts), f32),
        ],
        compiler_params=params(60),
        cost_estimate=pl.CostEstimate(
            flops=2 * length * width * (3 * width + 2 * returned.shape[0]),
            bytes_accessed=12 * MIB, transcendentals=0,
        ),
        name="back_rows",
    )(
        target, route, returned, up, tokens, mixed, gain, wr, rbias, wo,
        *([] if prior is None else [prior]),
    )


def back_heads_kernel(
    tokens_ref, gain_ref, gradmixed_ref, mixed_ref, wq_ref, wk_ref, wv_ref, q_ref, k_ref, v_ref,
    skew_ref, lse_ref, gradresid_ref, *refs,
):
    prior_ref = refs[0] if len(refs) > 7 else None
    line_ref, gw_ref, gradacts_ref, ggain_ref, normedt_ref, acc_ref, fold_ref = refs[-7:]
    step = pl.program_id(0)
    last = pl.num_programs(0) - 1
    length, width = tokens_ref.shape
    span = 2 * length

    @pl.when(step == 0)
    def start():
        acts = tokens_ref[...].astype(f32)
        normed = (acts * norm_scale(acts) * gain_ref[...]).astype(bf16)
        normedt_ref[...] = normed.T
        acc_ref[...] = jnp.zeros_like(acc_ref)

    dq, dk, dv = [], [], []
    for pair in range(GROUP // 2):
        cols = slice(PAIR * pair, PAIR * (pair + 1))
        query, key, value = q_ref[:, cols], k_ref[:, cols], v_ref[:, cols]
        grad = gradmixed_ref[:, cols]
        product = grad.astype(f32) * mixed_ref[:, cols].astype(f32)
        gq = gk = gv = None
        for half in range(2):
            head = 2 * pair + half
            mask = pair_mask(query.shape, half)
            clear = lambda a: jnp.where(mask, a, jnp.zeros_like(a))
            own, asked = clear(grad), clear(query)
            center = jnp.sum(clear(product), axis=-1, keepdims=True)
            scores = mm_nt(asked, key)
            grad_probs = mm_nt(own, value)
            all_probs, all_grads = [], []
            for at in range(length // BLOCK):
                rows = slice(BLOCK * at, BLOCK * (at + 1))
                low = length - BLOCK * (at + 1)
                part = scores[rows, :] + skew_ref[head, :, low : low + length].astype(f32)
                probs = jnp.exp(part - lse_ref[0, rows, head : head + 1])
                piece = probs * (grad_probs[rows, :] - center[rows, :])
                if at == 0:
                    fold_ref[:, :low] = jnp.zeros((BLOCK, low), f32)
                    fold_ref[:, low : low + length] = piece
                    fold_ref[:, low + length :] = jnp.zeros((BLOCK, length - low), f32)
                else:
                    fold_ref[:, low : low + length] += piece
                all_probs.append(probs.astype(bf16))
                all_grads.append(piece.astype(bf16))
            rows = fold_ref[...]
            size = BLOCK
            while size > 1:
                size //= 2
                rows = rows[:size] + pltpu.roll(rows[size:], span - size, 1)
            line_ref[0, head : head + 1, :] = pltpu.roll(rows, BLOCK - 1, 1)
            probs = jnp.concatenate(all_probs, axis=0)
            grad_scores = jnp.concatenate(all_grads, axis=0)
            a = mm(grad_scores, clear(key))
            b = mm_tn(grad_scores, asked)
            c = mm_tn(probs, own)
            gq = a if gq is None else gq + a
            gk = b if gk is None else gk + b
            gv = c if gv is None else gv + c
        dq.append(gq.astype(bf16))
        dk.append(gk.astype(bf16))
        dv.append(gv.astype(bf16))
    dq, dk, dv = (jnp.concatenate(x, axis=1) for x in (dq, dk, dv))
    normedt = normedt_ref[...]
    for i, grad in enumerate((dq, dk, dv)):
        total = mm(normedt, grad)
        if prior_ref is not None:
            total = total + prior_ref[i].astype(f32)
        gw_ref[i] = total.astype(bf16)
    acc_ref[...] += mm_nt(dq, wq_ref[...]) + mm_nt(dk, wk_ref[...]) + mm_nt(dv, wv_ref[...])

    @pl.when(step == last)
    def finish():
        grad_normed = acc_ref[...]
        acts = tokens_ref[...].astype(f32)
        scale = norm_scale(acts)
        ggain_ref[...] = jnp.sum(grad_normed * acts * scale, axis=0, keepdims=True)
        weighted = grad_normed * gain_ref[...]
        slope = scale * scale * scale * jnp.mean(weighted * acts, axis=-1, keepdims=True)
        grad_acts = gradresid_ref[...] + (scale * weighted - acts * slope)
        gradacts_ref[...] = grad_acts.astype(bf16)


def back_heads_call(
    tokens, gain, grad_mixed, mixed, wq, wk, wv, q, k, v, skewed, lse, grad_resid, prior
):
    length, width = tokens.shape
    part = GROUP * HEAD
    groups = HEADS // GROUP
    whole = lambda *shape: pl.BlockSpec(shape, lambda g: (0,) * len(shape))
    columns = lambda size: pl.BlockSpec((size, part), lambda g: (0, g))
    shape = jax.ShapeDtypeStruct
    weights = pl.BlockSpec((3, width, part), lambda g: (0, 0, g))
    return pl.pallas_call(
        back_heads_kernel,
        grid=(groups,),
        in_specs=[
            whole(length, width), whole(1, width), columns(length), columns(length),
            columns(width), columns(width), columns(width),
            columns(length), columns(length), columns(length),
            pl.BlockSpec((GROUP, BLOCK, skewed.shape[2]), lambda g: (g, 0, 0)),
            pl.BlockSpec((1, length, GROUP), lambda g: (g, 0, 0)), whole(length, width),
            *([] if prior is None else [weights]),
        ],
        out_specs=[
            pl.BlockSpec((1, GROUP, 2 * length), lambda g: (g, 0, 0)), weights,
            whole(length, width), whole(1, width),
        ],
        out_shape=[
            shape((groups, GROUP, 2 * length), f32), shape((3, width, width), bf16),
            shape((length, width), bf16), shape((1, width), f32),
        ],
        scratch_shapes=[
            pltpu.VMEM((width, length), bf16), pltpu.VMEM((length, width), f32),
            pltpu.VMEM((BLOCK, 2 * length), f32),
        ],
        compiler_params=params(60),
        cost_estimate=pl.CostEstimate(
            flops=groups * (2 * length * width * part * 6 + 8 * length * length * part * 4),
            bytes_accessed=21 * MIB, transcendentals=HEADS * length * length,
        ),
        name="back_heads",
    )(
        tokens, gain, grad_mixed, mixed, wq, wk, wv, q, k, v, skewed, lse, grad_resid,
        *([] if prior is None else [prior]),
    )


def pack_kernel(*refs):
    for at, ref in enumerate(refs[:-1]):
        refs[-1][at] = ref[...]


def pack_call(*parts):
    return pl.pallas_call(
        pack_kernel,
        out_shape=jax.ShapeDtypeStruct((len(parts), *parts[0].shape), parts[0].dtype),
        compiler_params=params(8),
        name="pack",
    )(*parts)


def skew_kernel(lines_ref, out_ref):
    heads, block, span = out_ref.shape
    full = lines_ref.shape[1]
    for head in range(heads):
        row = jnp.broadcast_to(lines_ref[head : head + 1, :], (16, full))
        base = pltpu.roll(row, full - (block - 1), 1, stride=1, stride_axis=0)
        for at in range(0, block, 16):
            turned = base if at == 0 else pltpu.roll(base, at, 1)
            out_ref[head, at : at + 16, :] = turned[:, :span].astype(bf16)


def skew_call(lines, block):
    heads, span = lines.shape
    return pl.pallas_call(
        skew_kernel,
        out_shape=jax.ShapeDtypeStruct((heads, block, span - block), bf16),
        compiler_params=params(16),
        name="skew",
    )(lines)


def exchange(buffer):
    return lax.all_to_all(buffer, AXES, split_axis=0, concat_axis=0, tiled=True)


def swap(value, bit):
    devices = lax.axis_size(AXES)
    return lax.ppermute(value, AXES, [(at, at ^ (1 << bit)) for at in range(devices)])


def own_bit(bit):
    return ((lax.axis_index(AXES) >> bit) & 1) == 1


def gather_step(held, bit):
    value, done = held
    theirs = swap(value, bit)
    upper = own_bit(bit)
    place = sum(1 for other in done if other > bit)
    value = jnp.stack(
        [jnp.where(upper, theirs, value), jnp.where(upper, value, theirs)], axis=place
    )
    return value, done + [bit]


def gather_all(value, order):
    held = (value, [])
    for bit in order:
        held = gather_step(held, bit)
    return held[0].reshape((-1,) + value.shape)


def scatter_step(held, bit):
    value, left = held
    place = 1 + left.index(bit)
    low = lax.index_in_dim(value, 0, place, keepdims=False)
    high = lax.index_in_dim(value, 1, place, keepdims=False)
    upper = own_bit(bit)
    sent = jnp.where(upper, low, high).astype(bf16)
    value = jnp.where(upper, high, low).astype(f32) + swap(sent, bit).astype(f32)
    return value, [other for other in left if other != bit]


def pack_rows(parts, width):
    lead = parts[0].shape[0]
    flat = jnp.concatenate([part.reshape(lead, -1) for part in parts], axis=1)
    short = -flat.shape[1] % width
    return jnp.pad(flat, ((0, 0), (0, short))).reshape(lead, -1, width)


def unpack_rows(packed, sizes):
    flat = packed.reshape(packed.shape[0], -1)
    out, at = [], 0
    for size in sizes:
        out.append(flat[:, at : at + size])
        at += size
    return out


def body(
    tokens,
    w_query,
    w_key,
    w_value,
    w_output,
    w_router,
    gain_attn,
    gain_ffn,
    rel_bias,
    router_bias,
    w_in,
    w_out,
    routes,
    fill_rank,
    bucket_map,
    upstream_grad,
):
    batches, length, width = tokens.shape
    devices = lax.axis_size(AXES)
    wide_bits = lax.axis_size("wide").bit_length() - 1
    bits = devices.bit_length() - 1
    local_experts = w_in.shape[0]
    experts = local_experts * devices
    capacity = max(2, 5 * length // (4 * experts))
    slots = experts * capacity
    span = 2 * length
    far = list(range(wide_bits, bits))
    near = list(range(1, wide_bits))
    turned = near[1:] + near[:1]

    expert_ids = jnp.arange(experts, dtype=jnp.int32)

    def plan(route, order):
        route_hot = (route[:, None] == expert_ids[None, :]).astype(f32)
        earlier = (order[None, :] < order[:, None]).astype(bf16)
        counts = jnp.dot(earlier, route_hot.astype(bf16), preferred_element_type=f32)
        slot = jnp.sum(counts * route_hot, axis=-1).astype(jnp.int32)
        first = jnp.where(slot < capacity, route * (2 * capacity) + slot, -1)
        second = jnp.where(first >= 0, first + capacity, -1)
        return jnp.stack([first, second], axis=0)

    small_parts = [w_router, gain_attn, gain_ffn, rel_bias, router_bias]
    small = pack_rows([part.reshape(1, -1) for part in small_parts], 8 * LANES)
    square = (pack_call(w_query, w_key, w_value, w_output), [])
    small = (small.reshape(8, LANES), [])
    for bit in far[::-1]:
        square, small = gather_step(square, bit), gather_step(small, bit)
    value, ahead = lax.optimization_barrier((square[0], small[0]))
    small = (ahead, small[1])
    done = far[::-1]
    value = value.reshape((2,) * len(far) + (4, -1, width))
    low, high = ((lax.slice_in_dim(value, i, i + 2, axis=len(far)), done) for i in (0, 2))
    raw_inputs = (routes, fill_rank, upstream_grad)
    for number, (one, two) in enumerate(zip(near[::-1], turned[::-1])):
        low, high = gather_step(low, one), gather_step(high, two)
        if number == 0:
            for bit in near[::-1]:
                small = gather_step(small, bit)
            first, second, ahead = lax.optimization_barrier((low[0], high[0], small[0]))
            low, high = (first, low[1]), (second, high[1])
            small_all = gather_step((ahead, small[1]), 0)[0]
            small_all, *raw_inputs = lax.optimization_barrier((small_all, *raw_inputs))

    raw_routes, raw_ranks, raw_upstream = raw_inputs
    spots = [plan(raw_routes[at, :, 0], raw_ranks[at]) for at in range(batches)]
    raw_spots = jnp.concatenate([spots[at][at] for at in range(batches)], axis=0)
    raw_ids = jnp.arange(2 * slots, dtype=jnp.int32)
    raw_sent = jnp.dot(
        (raw_ids[:, None] == raw_spots[None, :]).astype(bf16),
        raw_upstream.reshape(batches * length, width),
        preferred_element_type=f32,
    ).astype(bf16)
    raw_arrived = exchange(raw_sent.reshape(devices, 2 * capacity, width))

    wr_all, gain_one, gain_two, rel_flat, bias_all = unpack_rows(
        small_all.reshape(devices, 1, -1), [part.size for part in small_parts]
    )
    wr_all = wr_all.reshape(width, experts)
    gain_one = gain_one.reshape(1, width).astype(f32)
    gain_two = gain_two.reshape(1, width).astype(f32)
    bias_all = bias_all.reshape(1, experts).astype(f32)
    table = rel_flat.reshape(BUCKETS, HEADS).T
    bucket_hot = (
        jnp.arange(BUCKETS, dtype=jnp.int32)[:, None]
        == jnp.pad(bucket_map, (0, 1), constant_values=-1)[None, :]
    ).astype(bf16)
    skewed = skew_call(jnp.dot(table, bucket_hot, preferred_element_type=f32), BLOCK)
    first, second, skewed = lax.optimization_barrier((low[0], high[0], skewed))
    low, high = gather_step((first, low[1]), 0), gather_step((second, high[1]), 0)
    wq, wk, wv, wo = (
        lax.index_in_dim(part[0].reshape(devices, 2, -1, width), i, 1).reshape(width, width)
        for part in (low, high)
        for i in range(2)
    )

    own = lax.axis_index(AXES).astype(jnp.int32).reshape(1)
    count = 8 if 8 * capacity % 16 == 0 else 16
    row = jnp.arange(count * capacity, dtype=jnp.int32)
    place = row + (row // capacity) * capacity
    place = jnp.stack([place, place + capacity], axis=1)

    fronts, arrived, returned = [], [], []
    for at in range(batches):
        acts = tokens[at]
        if at == 1:
            acts, raw_arrived = lax.optimization_barrier((acts, raw_arrived))
        front = front_call(
            acts, wq, wk, wv, wo, skewed, gain_one, gain_two, spots[at], slots
        )
        fronts.append(front)
        arrived.append(exchange(front[-1].reshape(devices, 2 * capacity, width // 2)))
    raw = raw_arrived.reshape(devices, 2, capacity, width)
    grad_in = grad_out = 0.0
    for at in range(batches):
        sent, rows, active, grad_inner, grad_result = expert_call(
            own,
            arrived[at].reshape(2 * slots, width // 2),
            raw[:, at].reshape(slots, width),
            wr_all,
            bias_all,
            place,
            w_in[0],
            w_out[0],
        )
        grad_in += jnp.einsum("rd,rf->df", rows, grad_inner, preferred_element_type=f32)
        grad_out += jnp.einsum("rf,rd->fd", active, grad_result, preferred_element_type=f32)
        back = exchange(sent.reshape(devices, 2 * capacity, width))
        back, grad_in, grad_out = lax.optimization_barrier((back, grad_in, grad_out))
        returned.append(back)

    row_parts, head_parts = [], []
    g_output = g_heads = None
    for at in range(batches):
        q, k, v, mixed, lse, sent = fronts[at]
        row_part = back_rows_call(
            spots[at].T, routes[at], returned[at].reshape(2 * slots, width), upstream_grad[at],
            tokens[at], mixed, gain_two, wr_all, bias_all, wo, g_output,
        )
        g_output = row_part[3]
        head_part = back_heads_call(
            tokens[at], gain_one, row_part[2], mixed, wq, wk, wv, q, k, v, skewed, lse,
            row_part[1], g_heads,
        )
        g_heads = head_part[1]
        row_parts.append(row_part)
        head_parts.append(head_part)

    parts = jnp.concatenate([g_heads, g_output[None]], axis=0)
    held = scatter_step((parts.reshape((4,) + (2,) * bits + (-1, width)), list(range(bits))[::-1]), 0)
    low, high = ((held[0][i : i + 2], held[1]) for i in (0, 2))
    for one, two in zip(near, turned):
        low, high = scatter_step(low, one), scatter_step(high, two)
    held = (jnp.concatenate([low[0], high[0]], axis=0), low[1])
    for bit in far:
        held = scatter_step(held, bit)
    r_query, r_key, r_value, r_output = (held[0][i] for i in range(4))

    g_router, g_gain_two, g_bias = (
        sum(row_part[i] for row_part in row_parts) for i in range(4, 7)
    )
    lines, g_gain_one = (sum(part[i] for part in head_parts) for i in (0, 3))
    g_rel = jnp.einsum(
        "hn,bn->bh",
        lines.reshape(HEADS, span),
        bucket_hot.astype(f32),
        precision=lax.Precision.HIGHEST,
    )
    small_grads = [g_router, g_gain_one, g_gain_two, g_rel, g_bias]
    small_pack = pack_rows([part.reshape(devices, -1) for part in small_grads], 8 * LANES)
    held = (
        small_pack.reshape((1,) + (2,) * bits + (-1, LANES)), list(range(bits))[::-1]
    )
    for bit in [0] + near + far:
        held = scatter_step(held, bit)
    small_sum = held[0]
    tail = unpack_rows(small_sum.reshape(1, 1, -1), [part.size // devices for part in small_grads])
    r_router, r_gain_one, r_gain_two, r_rel, r_bias = (
        part.reshape(shape)
        for part, shape in zip(
            tail,
            (w_router.shape, gain_attn.shape, gain_ffn.shape, rel_bias.shape, router_bias.shape),
        )
    )
    return (
        jnp.stack([row_part[0] for row_part in row_parts], axis=0),
        jnp.stack([part[2] for part in head_parts], axis=0),
        r_query,
        r_key,
        r_value,
        r_output,
        r_router,
        r_gain_one,
        r_gain_two,
        r_rel,
        r_bias,
        grad_in[None],
        grad_out[None],
    )


def solution(mesh):
    both = P(AXES)
    in_specs = (both,) * 14 + (P(), both)
    out_specs = (both,) * 13
    return jax.shard_map(body, mesh=mesh, in_specs=in_specs, out_specs=out_specs, check_vma=False)
```

```python
import functools
import jax
import jax.numpy as jnp
import numpy as np
from jax import lax
from jax.experimental import pallas as pl
from jax.experimental.pallas import tpu as pltpu
from jax.sharding import PartitionSpec as P

HEADS = 12
HEAD = 64
BUCKETS = 32
PAIR = 2 * HEAD
GROUP = 4
BLOCK = 128
LANES = 128
AXES = ("narrow", "wide")
MIB = 1024 * 1024

epsilon = 1e-06
f32 = jnp.float32
bf16 = jnp.bfloat16


def mm(a, b):
    return lax.dot_general(a, b, (((1,), (0,)), ((), ())), preferred_element_type=f32)


def mm_nt(a, b):
    return lax.dot_general(a, b, (((1,), (1,)), ((), ())), preferred_element_type=f32)


def mm_tn(a, b):
    return lax.dot_general(a, b, (((0,), (0,)), ((), ())), preferred_element_type=f32)


def norm_scale(values):
    return lax.rsqrt(jnp.mean(values * values, axis=-1, keepdims=True) + epsilon)


def softmax_rows(logits):
    shifted = jnp.exp(logits - jnp.max(logits, axis=-1, keepdims=True))
    return shifted / jnp.sum(shifted, axis=-1, keepdims=True)


def pair_mask(shape, half):
    lane = lax.broadcasted_iota(jnp.int32, shape, 1)
    return (lane < HEAD) if half == 0 else (lane >= HEAD)


def params(size):
    return pltpu.CompilerParams(vmem_limit_bytes=size * MIB)


def front_kernel(
    tokens_ref, wq_ref, wk_ref, wv_ref, wo_ref, skew_ref, gain_one_ref, gain_two_ref, spots_ref,
    q_ref, k_ref, v_ref, mixed_ref, lse_ref, sent_ref, normed_ref, resid_ref,
):
    step = pl.program_id(0)
    length, width = tokens_ref.shape

    @pl.when(step == 0)
    def start():
        acts = tokens_ref[...].astype(f32)
        normed_ref[...] = (acts * norm_scale(acts) * gain_one_ref[...]).astype(bf16)
        resid_ref[...] = acts

    normed = normed_ref[...]
    q_ref[...] = mm(normed, wq_ref[...]).astype(bf16)
    k_ref[...] = mm(normed, wk_ref[...]).astype(bf16)
    v_ref[...] = mm(normed, wv_ref[...]).astype(bf16)
    for pair in range(GROUP // 2):
        cols = slice(PAIR * pair, PAIR * (pair + 1))
        query, key, value = q_ref[:, cols], k_ref[:, cols], v_ref[:, cols]
        out = None
        for half in range(2):
            head = 2 * pair + half
            mask = pair_mask(query.shape, half)
            scores = mm_nt(jnp.where(mask, query, jnp.zeros_like(query)), key)
            parts = []
            for at in range(length // BLOCK):
                rows = slice(BLOCK * at, BLOCK * (at + 1))
                low = length - BLOCK * (at + 1)
                part = scores[rows, :] + skew_ref[head, :, low : low + length].astype(f32)
                peak = jnp.max(part, axis=-1, keepdims=True)
                part = jnp.exp(part - peak)
                total = jnp.sum(part, axis=-1, keepdims=True)
                lse_ref[0, rows, head : head + 1] = peak + jnp.log(total)
                parts.append((part * (1.0 / total)).astype(bf16))
            probs = jnp.concatenate(parts, axis=0)
            term = mm(probs, jnp.where(mask, value, jnp.zeros_like(value)))
            out = term if out is None else out + term
        mixed_ref[:, cols] = out.astype(bf16)
    resid_ref[...] += mm(mixed_ref[...], wo_ref[...])

    @pl.when(step == pl.num_programs(0) - 1)
    def finish():
        resid = resid_ref[...]
        normed_two = (resid * norm_scale(resid) * gain_two_ref[...]).astype(bf16)
        rows = lax.broadcasted_iota(jnp.int32, (sent_ref.shape[0], length), 0)
        left = mm((rows == spots_ref[0:1, :]).astype(bf16), normed_two[:, : width // 2])
        right = mm((rows == spots_ref[1:2, :]).astype(bf16), normed_two[:, width // 2 :])
        sent_ref[...] = (left + right).astype(bf16)


def front_call(tokens, wq, wk, wv, wo, skewed, gain_one, gain_two, spots, slots):
    length, width = tokens.shape
    part = GROUP * HEAD
    groups = HEADS // GROUP
    whole = lambda *shape: pl.BlockSpec(shape, lambda g: (0,) * len(shape))
    columns = lambda rows: pl.BlockSpec((rows, part), lambda g: (0, g))
    shape = jax.ShapeDtypeStruct
    return pl.pallas_call(
        front_kernel,
        grid=(groups,),
        in_specs=[
            whole(length, width), columns(width), columns(width), columns(width),
            pl.BlockSpec((part, width), lambda g: (g, 0)),
            pl.BlockSpec((GROUP, BLOCK, skewed.shape[2]), lambda g: (g, 0, 0)),
            whole(1, width), whole(1, width), whole(2, length),
        ],
        out_specs=[
            columns(length), columns(length), columns(length), columns(length),
            pl.BlockSpec((1, length, GROUP), lambda g: (g, 0, 0)),
            whole(2 * slots, width // 2),
        ],
        out_shape=[
            *(4 * [shape((length, width), bf16)]), shape((groups, length, GROUP), f32),
            shape((2 * slots, width // 2), bf16),
        ],
        scratch_shapes=[pltpu.VMEM((length, width), bf16), pltpu.VMEM((length, width), f32)],
        compiler_params=params(60),
        cost_estimate=pl.CostEstimate(
            flops=2 * length * width * width * 4 + 4 * length * length * width * 4,
            bytes_accessed=14 * MIB, transcendentals=HEADS * length * length,
        ),
        name="front",
    )(tokens, wq, wk, wv, wo, skewed, gain_one, gain_two, spots)


def bell(values):
    size = jnp.abs(values)
    t = 1.0 / (1.0 + (0.3275911 * 0.7071067811865476) * size)
    falling = jnp.exp(-0.5 * values * values)
    poly = t * (
        0.127414796
        + t * (-0.142248368 + t * (0.7107068705 + t * (-0.7265760135 + t * 0.5307027145)))
    )
    tail = poly * falling
    return jnp.where(values < 0, tail, 1.0 - tail), falling * 0.3989422804014327


def expert_kernel(
    own_ref, arrived_ref, raw_ref, wr_ref, rbias_ref, place_ref, placed_ref, win_ref, wout_ref,
    sent_ref, rows_ref, active_ref, gradinner_ref, gradresult_ref, result_acc, rows_acc,
):
    step = pl.program_id(0)
    last = pl.num_programs(0) - 1
    count = rows_ref.shape[0]
    unit = place_ref.shape[0]

    @pl.when(step == 0)
    def start():
        half = arrived_ref.shape[1]
        ids = lax.broadcasted_iota(jnp.int32, (unit, 2 * unit), 1)
        for side in range(2):
            pick = (ids == place_ref[:, side : side + 1]).astype(bf16)
            for at in range(0, count, unit):
                rows_ref[at : at + unit, half * side : half * (side + 1)] = mm(
                    pick, arrived_ref[2 * at : 2 * (at + unit), :]
                ).astype(bf16)
        probs = softmax_rows(mm(rows_ref[...], wr_ref[...]) + rbias_ref[...])
        mine = lax.broadcasted_iota(jnp.int32, probs.shape, 1) == own_ref[0]
        gate = jnp.sum(jnp.where(mine, probs, 0.0), axis=-1, keepdims=True)
        gradresult_ref[...] = (gate * raw_ref[...].astype(f32)).astype(bf16)

    inner = mm(rows_ref[...], win_ref[...])
    grad_active = mm_nt(gradresult_ref[...], wout_ref[...])
    share, density = bell(inner)
    active = (inner * share).astype(bf16)
    grad_inner = (grad_active * (share + inner * density)).astype(bf16)
    active_ref[...] = active
    gradinner_ref[...] = grad_inner
    result = mm(active, wout_ref[...])
    grad_rows = mm_nt(grad_inner, win_ref[...])

    @pl.when(step == 0)
    def first():
        result_acc[...] = result
        rows_acc[...] = grad_rows

    @pl.when(step > 0)
    def more():
        result_acc[...] += result
        rows_acc[...] += grad_rows

    @pl.when(step == last)
    def finish():
        ids = lax.broadcasted_iota(jnp.int32, (2 * unit, unit), 0)
        picks = [(ids == placed_ref[side : side + 1, :]).astype(bf16) for side in range(2)]
        for at in range(0, count, unit):
            sent_ref[2 * at : 2 * (at + unit), :] = (
                mm(picks[0], result_acc[at : at + unit, :].astype(bf16))
                + mm(picks[1], rows_acc[at : at + unit, :].astype(bf16))
            ).astype(bf16)


def expert_call(own, arrived, raw, wr, rbias, place, w_in, w_out, part=1024):
    count, width = raw.shape
    hidden = w_in.shape[1]
    experts = wr.shape[1]
    whole = lambda *shape: pl.BlockSpec(shape, lambda g, own: (0,) * len(shape))
    columns = lambda n: pl.BlockSpec((n, part), lambda g, own: (0, g))
    return pl.pallas_call(
        expert_kernel,
        grid_spec=pltpu.PrefetchScalarGridSpec(
            num_scalar_prefetch=1,
            grid=(hidden // part,),
            in_specs=[
                whole(2 * count, width // 2), whole(count, width), whole(width, experts),
                whole(1, experts), whole(*place.shape), whole(*place.shape[::-1]),
                columns(width), pl.BlockSpec((part, width), lambda g, own: (g, 0)),
            ],
            out_specs=[
                whole(2 * count, width), whole(count, width), columns(count), columns(count),
                whole(count, width),
            ],
            scratch_shapes=[pltpu.VMEM((count, width), f32), pltpu.VMEM((count, width), f32)],
        ),
        out_shape=[
            jax.ShapeDtypeStruct((2 * count, width), bf16),
            jax.ShapeDtypeStruct((count, width), bf16),
            jax.ShapeDtypeStruct((count, hidden), bf16),
            jax.ShapeDtypeStruct((count, hidden), bf16),
            jax.ShapeDtypeStruct((count, width), bf16),
        ],
        compiler_params=params(60),
        cost_estimate=pl.CostEstimate(
            flops=8 * count * width * hidden, bytes_accessed=20 * MIB,
            transcendentals=count * hidden,
        ),
        name="expert",
    )(own, arrived, raw, wr, rbias, place, place.T, w_in, w_out)


def back_rows_kernel(
    target_ref, route_ref, returned_ref, up_ref, tokens_ref, mixed_ref, gain_ref, wr_ref,
    rbias_ref, wo_ref, *refs,
):
    output_ref, gradresid_ref, gradmixed_ref, go_ref, grw_ref, ggain_ref, gbias_ref = refs[-7:]
    length = up_ref.shape[0]
    experts = wr_ref.shape[1]
    mixed = mixed_ref[...]
    resid = tokens_ref[...].astype(f32) + mm(mixed, wo_ref[...])
    scale = norm_scale(resid)
    normed_two = (resid * scale * gain_ref[...]).astype(bf16)
    router = softmax_rows(mm(normed_two, wr_ref[...]) + rbias_ref[...])
    returned = returned_ref[...]
    ids = lax.broadcasted_iota(jnp.int32, (length, returned.shape[0]), 1)
    expert_rows = mm((ids == target_ref[:, 0:1]).astype(bf16), returned)
    grad_back = mm((ids == target_ref[:, 1:2]).astype(bf16), returned)
    up = up_ref[...].astype(f32)
    hot = lax.broadcasted_iota(jnp.int32, (length, experts), 1) == route_ref[...]
    gate = jnp.sum(jnp.where(hot, router, 0.0), axis=-1, keepdims=True)
    output_ref[...] = (resid + gate * expert_rows).astype(bf16)
    grad_gate = jnp.sum(up * expert_rows, axis=-1, keepdims=True)
    grad_logits = (router * (jnp.where(hot, grad_gate, 0.0) - gate * grad_gate)).astype(bf16)
    grad_normed = mm_nt(grad_logits, wr_ref[...]) + grad_back
    gbias = jnp.sum(grad_logits.astype(f32), axis=0, keepdims=True)
    grw = mm_tn(normed_two, grad_logits)
    ggain = jnp.sum(grad_normed * resid * scale, axis=0, keepdims=True)
    weighted = grad_normed * gain_ref[...]
    slope = scale * scale * scale * jnp.mean(weighted * resid, axis=-1, keepdims=True)
    grad_resid = up + (scale * weighted - resid * slope)
    gradresid_ref[...] = grad_resid
    grad_branch = grad_resid.astype(bf16)
    go = mm_tn(mixed, grad_branch)
    sums = [go, grw, ggain, gbias]
    if len(refs) > 7:
        sums = [one + prior[...].astype(f32) for one, prior in zip(sums, refs)]
    for ref, one in zip((go_ref, grw_ref, ggain_ref, gbias_ref), sums):
        ref[...] = one.astype(ref.dtype)
    gradmixed_ref[...] = mm_nt(grad_branch, wo_ref[...]).astype(bf16)


def back_rows_call(target, route, returned, up, tokens, mixed, gain, wr, rbias, wo, prior):
    length, width = up.shape
    experts = wr.shape[1]
    shape = jax.ShapeDtypeStruct
    return pl.pallas_call(
        back_rows_kernel,
        out_shape=[
            shape((length, width), bf16), shape((length, width), f32),
            shape((length, width), bf16), shape((width, width), bf16),
            shape((width, experts), f32), shape((1, width), f32), shape((1, experts), f32),
        ],
        compiler_params=params(60),
        cost_estimate=pl.CostEstimate(
            flops=2 * length * width * (3 * width + 2 * returned.shape[0]),
            bytes_accessed=12 * MIB, transcendentals=0,
        ),
        name="back_rows",
    )(
        target, route, returned, up, tokens, mixed, gain, wr, rbias, wo, *prior
    )


def back_heads_kernel(
    tokens_ref, gain_ref, gradmixed_ref, mixed_ref, wq_ref, wk_ref, wv_ref, q_ref, k_ref, v_ref,
    skew_ref, lse_ref, gradresid_ref, *refs,
):
    prior_refs = refs[:-7]
    line_ref, gw_ref, gradacts_ref, ggain_ref, normedt_ref, acc_ref, fold_ref = refs[-7:]
    step = pl.program_id(0)
    last = pl.num_programs(0) - 1
    length, width = tokens_ref.shape
    span = 2 * length

    @pl.when(step == 0)
    def start():
        acts = tokens_ref[...].astype(f32)
        normed = (acts * norm_scale(acts) * gain_ref[...]).astype(bf16)
        normedt_ref[...] = normed.T
        acc_ref[...] = jnp.zeros_like(acc_ref)

    dq, dk, dv = [], [], []
    for pair in range(GROUP // 2):
        cols = slice(PAIR * pair, PAIR * (pair + 1))
        query, key, value = q_ref[:, cols], k_ref[:, cols], v_ref[:, cols]
        grad = gradmixed_ref[:, cols]
        product = grad.astype(f32) * mixed_ref[:, cols].astype(f32)
        gq = gk = gv = None
        for half in range(2):
            head = 2 * pair + half
            mask = pair_mask(query.shape, half)
            clear = lambda a: jnp.where(mask, a, jnp.zeros_like(a))
            own, asked = clear(grad), clear(query)
            center = jnp.sum(clear(product), axis=-1, keepdims=True)
            scores = mm_nt(asked, key)
            grad_probs = mm_nt(own, value)
            all_probs, all_grads = [], []
            for at in range(length // BLOCK):
                rows = slice(BLOCK * at, BLOCK * (at + 1))
                low = length - BLOCK * (at + 1)
                part = scores[rows, :] + skew_ref[head, :, low : low + length].astype(f32)
                probs = jnp.exp(part - lse_ref[0, rows, head : head + 1])
                piece = probs * (grad_probs[rows, :] - center[rows, :])
                if at == 0:
                    fold_ref[:, :low] = jnp.zeros((BLOCK, low), f32)
                    fold_ref[:, low : low + length] = piece
                    fold_ref[:, low + length :] = jnp.zeros((BLOCK, length - low), f32)
                else:
                    fold_ref[:, low : low + length] += piece
                all_probs.append(probs.astype(bf16))
                all_grads.append(piece.astype(bf16))
            rows = fold_ref[...]
            size = BLOCK
            while size > 1:
                size //= 2
                rows = rows[:size] + pltpu.roll(rows[size:], span - size, 1)
            line = pltpu.roll(rows, BLOCK - 1, 1)
            if prior_refs:
                line = line + prior_refs[1][0, head : head + 1, :]
            line_ref[0, head : head + 1, :] = line
            probs = jnp.concatenate(all_probs, axis=0)
            grad_scores = jnp.concatenate(all_grads, axis=0)
            a = mm(grad_scores, clear(key))
            b = mm(asked.T, grad_scores)
            c = mm(own.T, probs)
            gq = a if gq is None else gq + a
            gk = b if gk is None else gk + b
            gv = c if gv is None else gv + c
        dq.append(gq.astype(bf16))
        dk.append(gk.T.astype(bf16))
        dv.append(gv.T.astype(bf16))
    dq, dk, dv = (jnp.concatenate(x, axis=1) for x in (dq, dk, dv))
    normedt = normedt_ref[...]
    for i, grad in enumerate((dq, dk, dv)):
        total = mm(normedt, grad)
        if prior_refs:
            total = total + prior_refs[0][i].astype(f32)
        gw_ref[i] = total.astype(bf16)
    acc_ref[...] += mm_nt(dq, wq_ref[...]) + mm_nt(dk, wk_ref[...]) + mm_nt(dv, wv_ref[...])

    @pl.when(step == last)
    def finish():
        grad_normed = acc_ref[...]
        acts = tokens_ref[...].astype(f32)
        scale = norm_scale(acts)
        ggain = jnp.sum(grad_normed * acts * scale, axis=0, keepdims=True)
        if prior_refs:
            ggain = ggain + prior_refs[2][...]
        ggain_ref[...] = ggain
        weighted = grad_normed * gain_ref[...]
        slope = scale * scale * scale * jnp.mean(weighted * acts, axis=-1, keepdims=True)
        grad_acts = gradresid_ref[...] + (scale * weighted - acts * slope)
        gradacts_ref[...] = grad_acts.astype(bf16)


def back_heads_call(
    tokens, gain, grad_mixed, mixed, wq, wk, wv, q, k, v, skewed, lse, grad_resid, prior
):
    length, width = tokens.shape
    part = GROUP * HEAD
    groups = HEADS // GROUP
    whole = lambda *shape: pl.BlockSpec(shape, lambda g: (0,) * len(shape))
    columns = lambda size: pl.BlockSpec((size, part), lambda g: (0, g))
    shape = jax.ShapeDtypeStruct
    weights = pl.BlockSpec((3, width, part), lambda g: (0, 0, g))
    lines = pl.BlockSpec((1, GROUP, 2 * length), lambda g: (g, 0, 0))
    return pl.pallas_call(
        back_heads_kernel,
        grid=(groups,),
        in_specs=[
            whole(length, width), whole(1, width), columns(length), columns(length),
            columns(width), columns(width), columns(width),
            columns(length), columns(length), columns(length),
            pl.BlockSpec((GROUP, BLOCK, skewed.shape[2]), lambda g: (g, 0, 0)),
            pl.BlockSpec((1, length, GROUP), lambda g: (g, 0, 0)), whole(length, width),
            *([weights, lines, whole(1, width)] if prior else []),
        ],
        out_specs=[
            lines, weights,
            whole(length, width), whole(1, width),
        ],
        out_shape=[
            shape((groups, GROUP, 2 * length), f32), shape((3, width, width), bf16),
            shape((length, width), bf16), shape((1, width), f32),
        ],
        scratch_shapes=[
            pltpu.VMEM((width, length), bf16), pltpu.VMEM((length, width), f32),
            pltpu.VMEM((BLOCK, 2 * length), f32),
        ],
        compiler_params=params(60),
        cost_estimate=pl.CostEstimate(
            flops=groups * (2 * length * width * part * 6 + 8 * length * length * part * 4),
            bytes_accessed=21 * MIB, transcendentals=HEADS * length * length,
        ),
        name="back_heads",
    )(
        tokens, gain, grad_mixed, mixed, wq, wk, wv, q, k, v, skewed, lse, grad_resid,
        *prior,
    )


def pack_kernel(*refs):
    for at, ref in enumerate(refs[:-1]):
        refs[-1][at] = ref[...]


def pack_call(*parts):
    return pl.pallas_call(
        pack_kernel,
        out_shape=jax.ShapeDtypeStruct((len(parts), *parts[0].shape), parts[0].dtype),
        compiler_params=params(60),
        name="pack",
    )(*parts)


def skew_kernel(lines_ref, out_ref):
    heads, block, span = out_ref.shape
    full = lines_ref.shape[1]
    for head in range(heads):
        row = jnp.broadcast_to(lines_ref[head : head + 1, :], (16, full))
        base = pltpu.roll(row, full - (block - 1), 1, stride=1, stride_axis=0)
        for at in range(0, block, 16):
            turned = base if at == 0 else pltpu.roll(base, at, 1)
            out_ref[head, at : at + 16, :] = turned[:, :span].astype(bf16)


def skew_call(lines, block):
    heads, span = lines.shape
    return pl.pallas_call(
        skew_kernel,
        out_shape=jax.ShapeDtypeStruct((heads, block, span - block), bf16),
        compiler_params=params(16),
        name="skew",
    )(lines)


def exchange(buffer):
    return lax.all_to_all(buffer, AXES, split_axis=0, concat_axis=0, tiled=True)


def swap(value, bit):
    devices = lax.axis_size(AXES)
    return lax.ppermute(value, AXES, [(at, at ^ (1 << bit)) for at in range(devices)])


def own_bit(bit):
    return ((lax.axis_index(AXES) >> bit) & 1) == 1


def gather_step(held, bit):
    value, done = held
    theirs = swap(value, bit)
    upper = own_bit(bit)
    place = sum(1 for other in done if other > bit)
    value = jnp.stack(
        [jnp.where(upper, theirs, value), jnp.where(upper, value, theirs)], axis=place
    )
    return value, done + [bit]


def gather_all(value, order):
    held = (value, [])
    for bit in order:
        held = gather_step(held, bit)
    return held[0].reshape((-1,) + value.shape)


def scatter_step(held, bit):
    value, left = held
    place = 1 + left.index(bit)
    low = lax.index_in_dim(value, 0, place, keepdims=False)
    high = lax.index_in_dim(value, 1, place, keepdims=False)
    upper = own_bit(bit)
    sent = jnp.where(upper, low, high).astype(bf16)
    value = jnp.where(upper, high, low).astype(f32) + swap(sent, bit).astype(f32)
    return value, [other for other in left if other != bit]


def pack_rows(parts, width):
    lead = parts[0].shape[0]
    flat = jnp.concatenate([part.reshape(lead, -1) for part in parts], axis=1)
    short = -flat.shape[1] % width
    return jnp.pad(flat, ((0, 0), (0, short))).reshape(lead, -1, width)


def unpack_rows(packed, sizes):
    flat = packed.reshape(packed.shape[0], -1)
    out, at = [], 0
    for size in sizes:
        out.append(flat[:, at : at + size])
        at += size
    return out


def body(
    tokens,
    w_query,
    w_key,
    w_value,
    w_output,
    w_router,
    gain_attn,
    gain_ffn,
    rel_bias,
    router_bias,
    w_in,
    w_out,
    routes,
    fill_rank,
    bucket_map,
    upstream_grad,
):
    batches, length, width = tokens.shape
    devices = lax.axis_size(AXES)
    wide_bits = lax.axis_size("wide").bit_length() - 1
    bits = devices.bit_length() - 1
    local_experts = w_in.shape[0]
    experts = local_experts * devices
    capacity = max(2, 5 * length // (4 * experts))
    slots = experts * capacity
    span = 2 * length
    shard = w_query.shape[0]
    far = list(range(wide_bits, bits))
    near = list(range(1, wide_bits))
    turned = near[1:] + near[:1]

    expert_ids = jnp.arange(experts, dtype=jnp.int32)

    def plan(route, order):
        route_hot = (route[:, None] == expert_ids[None, :]).astype(f32)
        earlier = (order[None, :] < order[:, None]).astype(bf16)
        counts = jnp.dot(earlier, route_hot.astype(bf16), preferred_element_type=f32)
        slot = jnp.sum(counts * route_hot, axis=-1).astype(jnp.int32)
        first = jnp.where(slot < capacity, route * (2 * capacity) + slot, -1)
        second = jnp.where(first >= 0, first + capacity, -1)
        return jnp.stack([first, second], axis=0)

    small_parts = [w_router, gain_attn, gain_ffn, rel_bias, router_bias]
    small = pack_rows([part.reshape(1, -1) for part in small_parts], 8 * LANES)
    packed, small = lax.optimization_barrier(
        (pack_call(w_query, w_key, w_value, w_output), small)
    )
    square, small = (packed, []), (small.reshape(8, LANES), [])
    for bit in far[::-1]:
        square, small = gather_step(square, bit), gather_step(small, bit)
    value, ahead = lax.optimization_barrier((square[0], small[0]))
    small = (ahead, small[1])
    done = far[::-1]
    value = value.reshape((2,) * len(far) + (4, -1, width))
    low, high = ((lax.slice_in_dim(value, i, i + 2, axis=len(far)), done) for i in (0, 2))
    for number, (one, two) in enumerate(zip(near[::-1], turned[::-1])):
        low, high = gather_step(low, one), gather_step(high, two)
        if number == 0:
            for bit in near[::-1]:
                small = gather_step(small, bit)
            first, second, ahead = lax.optimization_barrier((low[0], high[0], small[0]))
            low, high = (first, low[1]), (second, high[1])
            small_all = gather_step((ahead, small[1]), 0)[0]

    spots = [plan(routes[at, :, 0], fill_rank[at]) for at in range(batches)]
    raw_spots = jnp.concatenate([spots[at][at] for at in range(batches)], axis=0)
    raw_ids = jnp.arange(2 * slots, dtype=jnp.int32)
    raw_sent = jnp.dot(
        (raw_ids[:, None] == raw_spots[None, :]).astype(bf16),
        upstream_grad.reshape(batches * length, width),
        preferred_element_type=f32,
    ).astype(bf16)
    small_all, raw_sent = lax.optimization_barrier((small_all, raw_sent))
    raw_arrived = exchange(raw_sent.reshape(devices, 2 * capacity, width))

    wr_all, gain_one, gain_two, rel_flat, bias_all = unpack_rows(
        small_all.reshape(devices, 1, -1), [part.size for part in small_parts]
    )
    wr_all = wr_all.reshape(width, experts)
    gain_one = gain_one.reshape(1, width).astype(f32)
    gain_two = gain_two.reshape(1, width).astype(f32)
    bias_all = bias_all.reshape(1, experts).astype(f32)
    table = rel_flat.reshape(BUCKETS, HEADS).T
    bucket_hot = (
        jnp.arange(BUCKETS, dtype=jnp.int32)[:, None]
        == jnp.pad(bucket_map, (0, 1), constant_values=-1)[None, :]
    ).astype(bf16)
    skewed = skew_call(jnp.dot(table, bucket_hot, preferred_element_type=f32), BLOCK)
    own = lax.axis_index(AXES).astype(jnp.int32).reshape(1)
    count = 8 if 8 * capacity % 16 == 0 else 16
    row = np.arange(count * capacity, dtype=np.int32)
    row = row + (row // capacity) * capacity
    place = jnp.asarray(np.stack([row, row + capacity], axis=1))
    first, second, skewed, wr_all, gain_one, gain_two, bias_all = lax.optimization_barrier(
        (low[0], high[0], skewed, wr_all, gain_one, gain_two, bias_all)
    )
    low, high = gather_step((first, low[1]), 0), gather_step((second, high[1]), 0)
    wq, wk, wv, wo = (
        lax.index_in_dim(part[0].reshape(devices, 2, -1, width), i, 1).reshape(width, width)
        for part in (low, high)
        for i in range(2)
    )

    fronts, arrived, returned = [], [], []
    for at in range(batches):
        acts = tokens[at]
        if at == 1:
            raw = raw_arrived.reshape(devices, batches, capacity, width)
            raw = [raw[:, i].reshape(slots, width) for i in range(batches)]
            acts, raw, targets = lax.optimization_barrier(
                (acts, raw, [(spots[i].T, routes[i]) for i in range(batches)])
            )
        front = front_call(
            acts, wq, wk, wv, wo, skewed, gain_one, gain_two, spots[at], slots
        )
        fronts.append(front)
        arrived.append(exchange(front[-1].reshape(devices, 2 * capacity, width // 2)))
    grad_in = grad_out = 0.0
    for at in range(batches):
        sent, rows, active, grad_inner, grad_result = expert_call(
            own,
            arrived[at].reshape(2 * slots, width // 2),
            raw[at],
            wr_all,
            bias_all,
            place,
            w_in[0],
            w_out[0],
        )
        if at == batches - 1:
            sent, grad_in, grad_out = lax.optimization_barrier((sent, grad_in, grad_out))
        grad_in += jnp.einsum("rd,rf->df", rows, grad_inner, preferred_element_type=f32)
        grad_out += jnp.einsum("rf,rd->fd", active, grad_result, preferred_element_type=f32)
        back = exchange(sent.reshape(devices, 2 * capacity, width))
        back, grad_in, grad_out = lax.optimization_barrier((back, grad_in, grad_out))
        returned.append(back)

    row_parts, head_parts = [], []
    row_prior, head_prior = [], []
    for at in range(batches):
        q, k, v, mixed, lse, sent = fronts[at]
        row_part = back_rows_call(
            *targets[at], returned[at].reshape(2 * slots, width), upstream_grad[at],
            tokens[at], mixed, gain_two, wr_all, bias_all, wo, row_prior,
        )
        row_prior = row_part[3:]
        head_part = back_heads_call(
            tokens[at], gain_one, row_part[2], mixed, wq, wk, wv, q, k, v, skewed, lse,
            row_part[1], head_prior,
        )
        head_prior = [head_part[1], head_part[0], head_part[3]]
        row_parts.append(row_part)
        head_parts.append(head_part)

    def halved(value):
        value = value.reshape((-1,) + (2,) * bits + (shard, width))
        return scatter_step((value, list(range(bits))[::-1]), 0)

    g_output, g_router, g_gain_two, g_bias = row_prior
    g_heads, lines, g_gain_one = head_prior
    outer, inner = halved(g_output[None]), halved(g_heads)
    low, high = inner[0][:2], jnp.concatenate([inner[0][2:], outer[0]], axis=0)
    low, high, g_router, g_gain_two, g_bias, lines, g_gain_one = lax.optimization_barrier(
        (low, high, g_router, g_gain_two, g_bias, lines, g_gain_one)
    )
    low, high = (low, inner[1]), (high, inner[1])
    g_rel = jnp.einsum(
        "hn,bn->bh",
        lines.reshape(HEADS, span),
        bucket_hot.astype(f32),
        precision=lax.Precision.HIGHEST,
    )
    short = [part.reshape(devices, -1) for part in (g_gain_one, g_gain_two, g_rel, g_bias)]
    sizes = [part.shape[1] for part in short]
    short_pack = pack_rows(short, 8 * LANES).reshape(devices, -1, LANES).astype(bf16)
    lanes = -(-experts // LANES) * LANES
    router_pack = jnp.pad(g_router.astype(bf16), ((0, 0), (0, lanes - experts)))
    router_pack = router_pack.reshape(devices, -1, LANES)
    small = jnp.concatenate([router_pack, short_pack], axis=1)
    small = (small.reshape((1,) + (2,) * bits + small.shape[1:]), list(range(bits))[::-1])
    small_bits = [0] + near + far
    for one, two in zip(near, turned):
        low, high = scatter_step(low, one), scatter_step(high, two)
    held = (jnp.concatenate([low[0], high[0]], axis=0), low[1])
    for bit in far:
        held = scatter_step(held, bit)
    for bit in small_bits:
        small = scatter_step(small, bit)
    r_query, r_key, r_value, r_output = (held[0][i] for i in range(4))
    cut = router_pack.shape[1]
    r_router = small[0][0, :cut].reshape(shard, lanes)[:, :experts]
    tail = unpack_rows(small[0][:, cut:], sizes)
    r_gain_one, r_gain_two, r_rel, r_bias = (
        part.reshape(shape)
        for part, shape in zip(
            tail,
            (gain_attn.shape, gain_ffn.shape, rel_bias.shape, router_bias.shape),
        )
    )
    return (
        jnp.stack([row_part[0] for row_part in row_parts], axis=0),
        jnp.stack([part[2] for part in head_parts], axis=0),
        r_query,
        r_key,
        r_value,
        r_output,
        r_router,
        r_gain_one,
        r_gain_two,
        r_rel,
        r_bias,
        grad_in[None],
        grad_out[None],
    )


def solution(mesh):
    both = P(AXES)
    in_specs = (both,) * 14 + (P(), both)
    out_specs = (both,) * 13
    return jax.shard_map(body, mesh=mesh, in_specs=in_specs, out_specs=out_specs, check_vma=False)
```

```python
import functools
import jax
import jax.numpy as jnp
import numpy as np
from jax import lax
from jax.experimental import pallas as pl
from jax.experimental.pallas import tpu as pltpu
from jax.sharding import PartitionSpec as P

HEADS = 12
HEAD = 64
BUCKETS = 32
PAIR = 2 * HEAD
GROUP = 4
BLOCK = 128
LANES = 128
AXES = ("narrow", "wide")
MIB = 1024 * 1024

epsilon = 1e-06
f32 = jnp.float32
bf16 = jnp.bfloat16


def mm(a, b):
    return lax.dot_general(a, b, (((1,), (0,)), ((), ())), preferred_element_type=f32)


def mm_nt(a, b):
    return lax.dot_general(a, b, (((1,), (1,)), ((), ())), preferred_element_type=f32)


def mm_tn(a, b):
    return lax.dot_general(a, b, (((0,), (0,)), ((), ())), preferred_element_type=f32)


def norm_scale(values):
    return lax.rsqrt(jnp.mean(values * values, axis=-1, keepdims=True) + epsilon)


def softmax_rows(logits):
    shifted = jnp.exp(logits - jnp.max(logits, axis=-1, keepdims=True))
    return shifted / jnp.sum(shifted, axis=-1, keepdims=True)


def pair_mask(shape, half):
    lane = lax.broadcasted_iota(jnp.int32, shape, 1)
    return (lane < HEAD) if half == 0 else (lane >= HEAD)


def params(size):
    return pltpu.CompilerParams(vmem_limit_bytes=size * MIB)


def front_kernel(
    tokens_ref, wq_ref, wk_ref, wv_ref, wo_ref, skew_ref, gain_one_ref, gain_two_ref, spots_ref,
    q_ref, k_ref, v_ref, mixed_ref, lse_ref, sent_ref, normed_ref, resid_ref,
):
    step = pl.program_id(0)
    length, width = tokens_ref.shape

    @pl.when(step == 0)
    def start():
        acts = tokens_ref[...].astype(f32)
        normed_ref[...] = (acts * norm_scale(acts) * gain_one_ref[...]).astype(bf16)
        resid_ref[...] = acts

    normed = normed_ref[...]
    q_ref[...] = mm(normed, wq_ref[...]).astype(bf16)
    k_ref[...] = mm(normed, wk_ref[...]).astype(bf16)
    v_ref[...] = mm(normed, wv_ref[...]).astype(bf16)
    for pair in range(GROUP // 2):
        cols = slice(PAIR * pair, PAIR * (pair + 1))
        query, key, value = q_ref[:, cols], k_ref[:, cols], v_ref[:, cols]
        out = None
        for half in range(2):
            head = 2 * pair + half
            mask = pair_mask(query.shape, half)
            scores = mm_nt(jnp.where(mask, query, jnp.zeros_like(query)), key)
            parts = []
            for at in range(length // BLOCK):
                rows = slice(BLOCK * at, BLOCK * (at + 1))
                low = length - BLOCK * (at + 1)
                part = scores[rows, :] + skew_ref[head, :, low : low + length].astype(f32)
                peak = jnp.max(part, axis=-1, keepdims=True)
                part = jnp.exp(part - peak)
                total = jnp.sum(part, axis=-1, keepdims=True)
                lse_ref[0, rows, head : head + 1] = peak + jnp.log(total)
                parts.append((part * (1.0 / total)).astype(bf16))
            probs = jnp.concatenate(parts, axis=0)
            term = mm(probs, jnp.where(mask, value, jnp.zeros_like(value)))
            out = term if out is None else out + term
        mixed_ref[:, cols] = out.astype(bf16)
    resid_ref[...] += mm(mixed_ref[...], wo_ref[...])

    @pl.when(step == pl.num_programs(0) - 1)
    def finish():
        resid = resid_ref[...]
        normed_two = (resid * norm_scale(resid) * gain_two_ref[...]).astype(bf16)
        rows = lax.broadcasted_iota(jnp.int32, (sent_ref.shape[0], length), 0)
        left = mm((rows == spots_ref[0:1, :]).astype(bf16), normed_two[:, : width // 2])
        right = mm((rows == spots_ref[1:2, :]).astype(bf16), normed_two[:, width // 2 :])
        sent_ref[...] = (left + right).astype(bf16)


def one_in(at, length, width):
    return pl.BlockSpec((None, length, width), lambda *g: (at, 0, 0))


def front_call(at, tokens, wq, wk, wv, wo, skewed, gain_one, gain_two, spots, slots):
    length, width = tokens.shape[1:]
    part = GROUP * HEAD
    groups = HEADS // GROUP
    whole = lambda *shape: pl.BlockSpec(shape, lambda g: (0,) * len(shape))
    columns = lambda rows: pl.BlockSpec((rows, part), lambda g: (0, g))
    shape = jax.ShapeDtypeStruct
    return pl.pallas_call(
        front_kernel,
        grid=(groups,),
        in_specs=[
            one_in(at, length, width), columns(width), columns(width), columns(width),
            pl.BlockSpec((part, width), lambda g: (g, 0)),
            pl.BlockSpec((GROUP, BLOCK, skewed.shape[2]), lambda g: (g, 0, 0)),
            whole(1, width), whole(1, width), whole(2, length),
        ],
        out_specs=[
            columns(length), columns(length), columns(length), columns(length),
            pl.BlockSpec((1, length, GROUP), lambda g: (g, 0, 0)),
            whole(2 * slots, width // 2),
        ],
        out_shape=[
            *(4 * [shape((length, width), bf16)]), shape((groups, length, GROUP), f32),
            shape((2 * slots, width // 2), bf16),
        ],
        scratch_shapes=[pltpu.VMEM((length, width), bf16), pltpu.VMEM((length, width), f32)],
        compiler_params=params(60),
        cost_estimate=pl.CostEstimate(flops=1000000, bytes_accessed=MIB // 4, transcendentals=0),
        name="front",
    )(tokens, wq, wk, wv, wo, skewed, gain_one, gain_two, spots)


def bell(values):
    size = jnp.abs(values)
    t = 1.0 / (1.0 + (0.3275911 * 0.7071067811865476) * size)
    falling = jnp.exp(-0.5 * values * values)
    poly = t * (
        0.127414796
        + t * (-0.142248368 + t * (0.7107068705 + t * (-0.7265760135 + t * 0.5307027145)))
    )
    tail = poly * falling
    return jnp.where(values < 0, tail, 1.0 - tail), falling * 0.3989422804014327


def expert_kernel(
    mine_at, own_ref, arrived_ref, raw_ref, wr_ref, rbias_ref, place_ref, placed_ref, win_ref, wout_ref,
    sent_ref, rows_ref, active_ref, gradinner_ref, gradresult_ref, result_acc, rows_acc,
):
    step = pl.program_id(0)
    last = pl.num_programs(0) - 1
    count = rows_ref.shape[0]
    unit = place_ref.shape[0]

    @pl.when(step == 0)
    def start():
        half = arrived_ref.shape[1]
        ids = lax.broadcasted_iota(jnp.int32, (unit, 2 * unit), 1)
        for side in range(2):
            pick = (ids == place_ref[:, side : side + 1]).astype(bf16)
            for at in range(0, count, unit):
                rows_ref[at : at + unit, half * side : half * (side + 1)] = mm(
                    pick, arrived_ref[2 * at : 2 * (at + unit), :]
                ).astype(bf16)
        probs = softmax_rows(mm(rows_ref[...], wr_ref[...]) + rbias_ref[...])
        mine = lax.broadcasted_iota(jnp.int32, probs.shape, 1) == own_ref[0]
        gate = jnp.sum(jnp.where(mine, probs, 0.0), axis=-1, keepdims=True)
        pick = (ids == place_ref[:, mine_at : mine_at + 1]).astype(bf16)
        for at in range(0, count, unit):
            raw = mm(pick, raw_ref[2 * at : 2 * (at + unit), :])
            gradresult_ref[at : at + unit, :] = (gate[at : at + unit] * raw).astype(bf16)

    inner = mm(rows_ref[...], win_ref[...])
    grad_active = mm_nt(gradresult_ref[...], wout_ref[...])
    share, density = bell(inner)
    active = (inner * share).astype(bf16)
    grad_inner = (grad_active * (share + inner * density)).astype(bf16)
    active_ref[...] = active
    gradinner_ref[...] = grad_inner
    result = mm(active, wout_ref[...])
    grad_rows = mm_nt(grad_inner, win_ref[...])

    @pl.when(step == 0)
    def first():
        result_acc[...] = result
        rows_acc[...] = grad_rows

    @pl.when(step > 0)
    def more():
        result_acc[...] += result
        rows_acc[...] += grad_rows

    @pl.when(step == last)
    def finish():
        ids = lax.broadcasted_iota(jnp.int32, (2 * unit, unit), 0)
        picks = [(ids == placed_ref[side : side + 1, :]).astype(bf16) for side in range(2)]
        for at in range(0, count, unit):
            sent_ref[2 * at : 2 * (at + unit), :] = (
                mm(picks[0], result_acc[at : at + unit, :].astype(bf16))
                + mm(picks[1], rows_acc[at : at + unit, :].astype(bf16))
            ).astype(bf16)


def expert_call(mine_at, own, arrived, raw, wr, rbias, place, w_in, w_out, part=1024):
    count, width = raw.shape[0] // 2, raw.shape[1]
    hidden = w_in.shape[1]
    experts = wr.shape[1]
    whole = lambda *shape: pl.BlockSpec(shape, lambda g, own: (0,) * len(shape))
    columns = lambda n: pl.BlockSpec((n, part), lambda g, own: (0, g))
    return pl.pallas_call(
        functools.partial(expert_kernel, mine_at),
        grid_spec=pltpu.PrefetchScalarGridSpec(
            num_scalar_prefetch=1,
            grid=(hidden // part,),
            in_specs=[
                whole(2 * count, width // 2), whole(2 * count, width), whole(width, experts),
                whole(1, experts), whole(*place.shape), whole(*place.shape[::-1]),
                columns(width), pl.BlockSpec((part, width), lambda g, own: (g, 0)),
            ],
            out_specs=[
                whole(2 * count, width), whole(count, width), columns(count), columns(count),
                whole(count, width),
            ],
            scratch_shapes=[pltpu.VMEM((count, width), f32), pltpu.VMEM((count, width), f32)],
        ),
        out_shape=[
            jax.ShapeDtypeStruct((2 * count, width), bf16),
            jax.ShapeDtypeStruct((count, width), bf16),
            jax.ShapeDtypeStruct((count, hidden), bf16),
            jax.ShapeDtypeStruct((count, hidden), bf16),
            jax.ShapeDtypeStruct((count, width), bf16),
        ],
        compiler_params=params(60),
        cost_estimate=pl.CostEstimate(
            flops=8 * count * width * hidden, bytes_accessed=20 * MIB,
            transcendentals=count * hidden,
        ),
        name="expert",
    )(own, arrived, raw, wr, rbias, place, place.T, w_in, w_out)


def back_rows_kernel(
    target_ref, route_ref, returned_ref, up_ref, tokens_ref, mixed_ref, gain_ref, wr_ref,
    rbias_ref, wo_ref, *refs,
):
    output_ref, gradresid_ref, gradmixed_ref, go_ref, grw_ref, ggain_ref, gbias_ref = refs[-7:]
    length = up_ref.shape[0]
    experts = wr_ref.shape[1]
    mixed = mixed_ref[...]
    resid = tokens_ref[...].astype(f32) + mm(mixed, wo_ref[...])
    scale = norm_scale(resid)
    normed_two = (resid * scale * gain_ref[...]).astype(bf16)
    router = softmax_rows(mm(normed_two, wr_ref[...]) + rbias_ref[...])
    returned = returned_ref[...]
    ids = lax.broadcasted_iota(jnp.int32, (length, returned.shape[0]), 1)
    expert_rows = mm((ids == target_ref[:, 0:1]).astype(bf16), returned)
    grad_back = mm((ids == target_ref[:, 1:2]).astype(bf16), returned)
    up = up_ref[...].astype(f32)
    hot = lax.broadcasted_iota(jnp.int32, (length, experts), 1) == route_ref[...]
    gate = jnp.sum(jnp.where(hot, router, 0.0), axis=-1, keepdims=True)
    output_ref[0] = (resid + gate * expert_rows).astype(bf16)
    grad_gate = jnp.sum(up * expert_rows, axis=-1, keepdims=True)
    grad_logits = (router * (jnp.where(hot, grad_gate, 0.0) - gate * grad_gate)).astype(bf16)
    grad_normed = mm_nt(grad_logits, wr_ref[...]) + grad_back
    gbias = jnp.sum(grad_logits.astype(f32), axis=0, keepdims=True)
    grw = mm_tn(normed_two, grad_logits)
    ggain = jnp.sum(grad_normed * resid * scale, axis=0, keepdims=True)
    weighted = grad_normed * gain_ref[...]
    slope = scale * scale * scale * jnp.mean(weighted * resid, axis=-1, keepdims=True)
    grad_resid = up + (scale * weighted - resid * slope)
    gradresid_ref[...] = grad_resid
    grad_branch = grad_resid.astype(bf16)
    go = mm_tn(mixed, grad_branch)
    sums = [go, grw, ggain, gbias]
    if len(refs) > 7:
        sums = [one + prior[...].astype(f32) for one, prior in zip(sums, refs)]
    for ref, one in zip((go_ref, grw_ref, ggain_ref, gbias_ref), sums):
        ref[...] = one.astype(ref.dtype)
    gradmixed_ref[...] = mm_nt(grad_branch, wo_ref[...]).astype(bf16)


def one_of(count, at, length, width):
    spec = pl.BlockSpec((1, length, width), lambda *g: (at, 0, 0))
    return spec, jax.ShapeDtypeStruct((count, length, width), bf16)


def back_rows_call(
    at, count, target, route, returned, up, tokens, mixed, gain, wr, rbias, wo, prior, output
):
    length, width = up.shape[1:]
    experts = wr.shape[1]
    shape = jax.ShapeDtypeStruct
    spec, full = one_of(count, at, length, width)
    vmem = pl.BlockSpec(memory_space=pltpu.VMEM)
    inputs = 10 + len(prior)
    return pl.pallas_call(
        back_rows_kernel,
        grid=(1,),
        in_specs=[vmem] * 3
        + [one_in(at, length, width)] * 2
        + [vmem] * (inputs - 5)
        + [pl.BlockSpec(memory_space=pl.ANY)] * len(output),
        out_specs=[spec] + [vmem] * 6,
        input_output_aliases={inputs: 0} if output else {},
        out_shape=[
            full, shape((length, width), f32),
            shape((length, width), bf16), shape((width, width), bf16),
            shape((width, experts), f32), shape((1, width), f32), shape((1, experts), f32),
        ],
        compiler_params=params(60),
        cost_estimate=pl.CostEstimate(
            flops=2 * length * width * (3 * width + 2 * returned.shape[0]),
            bytes_accessed=12 * MIB, transcendentals=0,
        ),
        name="back_rows",
    )(
        target, route, returned, up, tokens, mixed, gain, wr, rbias, wo, *prior, *output
    )


def back_heads_kernel(
    tokens_ref, gain_ref, gradmixed_ref, mixed_ref, wq_ref, wk_ref, wv_ref, q_ref, k_ref, v_ref,
    skew_ref, lse_ref, gradresid_ref, *refs,
):
    prior_refs = refs[: (len(refs) - 7) // 3 * 3]
    line_ref, gw_ref, gradacts_ref, ggain_ref, normedt_ref, acc_ref, fold_ref = refs[-7:]
    step = pl.program_id(0)
    last = pl.num_programs(0) - 1
    length, width = tokens_ref.shape
    span = 2 * length

    @pl.when(step == 0)
    def start():
        acts = tokens_ref[...].astype(f32)
        normed = (acts * norm_scale(acts) * gain_ref[...]).astype(bf16)
        normedt_ref[...] = normed.T
        acc_ref[...] = jnp.zeros_like(acc_ref)

    dq, dk, dv = [], [], []
    for pair in range(GROUP // 2):
        cols = slice(PAIR * pair, PAIR * (pair + 1))
        query, key, value = q_ref[:, cols], k_ref[:, cols], v_ref[:, cols]
        grad = gradmixed_ref[:, cols]
        product = grad.astype(f32) * mixed_ref[:, cols].astype(f32)
        gq = gk = gv = None
        for half in range(2):
            head = 2 * pair + half
            mask = pair_mask(query.shape, half)
            clear = lambda a: jnp.where(mask, a, jnp.zeros_like(a))
            own, asked = clear(grad), clear(query)
            center = jnp.sum(clear(product), axis=-1, keepdims=True)
            scores = mm_nt(asked, key)
            grad_probs = mm_nt(own, value)
            all_probs, all_grads = [], []
            for at in range(length // BLOCK):
                rows = slice(BLOCK * at, BLOCK * (at + 1))
                low = length - BLOCK * (at + 1)
                part = scores[rows, :] + skew_ref[head, :, low : low + length].astype(f32)
                probs = jnp.exp(part - lse_ref[0, rows, head : head + 1])
                piece = probs * (grad_probs[rows, :] - center[rows, :])
                if at == 0:
                    fold_ref[:, :low] = jnp.zeros((BLOCK, low), f32)
                    fold_ref[:, low : low + length] = piece
                    fold_ref[:, low + length :] = jnp.zeros((BLOCK, length - low), f32)
                else:
                    fold_ref[:, low : low + length] += piece
                all_probs.append(probs.astype(bf16))
                all_grads.append(piece.astype(bf16))
            rows = fold_ref[...]
            size = BLOCK
            while size > 1:
                size //= 2
                rows = rows[:size] + pltpu.roll(rows[size:], span - size, 1)
            line = pltpu.roll(rows, BLOCK - 1, 1)
            if prior_refs:
                line = line + prior_refs[1][0, head : head + 1, :]
            line_ref[0, head : head + 1, :] = line
            probs = jnp.concatenate(all_probs, axis=0)
            grad_scores = jnp.concatenate(all_grads, axis=0)
            a = mm(grad_scores, clear(key))
            b = mm(asked.T, grad_scores)
            c = mm(own.T, probs)
            gq = a if gq is None else gq + a
            gk = b if gk is None else gk + b
            gv = c if gv is None else gv + c
        dq.append(gq.astype(bf16))
        dk.append(gk.T.astype(bf16))
        dv.append(gv.T.astype(bf16))
    dq, dk, dv = (jnp.concatenate(x, axis=1) for x in (dq, dk, dv))
    normedt = normedt_ref[...]
    for i, grad in enumerate((dq, dk, dv)):
        total = mm(normedt, grad)
        if prior_refs:
            total = total + prior_refs[0][i].astype(f32)
        gw_ref[i] = total.astype(bf16)
    acc_ref[...] += mm_nt(dq, wq_ref[...]) + mm_nt(dk, wk_ref[...]) + mm_nt(dv, wv_ref[...])

    @pl.when(step == last)
    def finish():
        grad_normed = acc_ref[...]
        acts = tokens_ref[...].astype(f32)
        scale = norm_scale(acts)
        ggain = jnp.sum(grad_normed * acts * scale, axis=0, keepdims=True)
        if prior_refs:
            ggain = ggain + prior_refs[2][...]
        ggain_ref[...] = ggain
        weighted = grad_normed * gain_ref[...]
        slope = scale * scale * scale * jnp.mean(weighted * acts, axis=-1, keepdims=True)
        grad_acts = gradresid_ref[...] + (scale * weighted - acts * slope)
        gradacts_ref[0] = grad_acts.astype(bf16)


def back_heads_call(
    at, count, tokens, gain, grad_mixed, mixed, wq, wk, wv, q, k, v, skewed, lse, grad_resid,
    prior, grads,
):
    length, width = tokens.shape[1:]
    part = GROUP * HEAD
    groups = HEADS // GROUP
    whole = lambda *shape: pl.BlockSpec(shape, lambda g: (0,) * len(shape))
    columns = lambda size: pl.BlockSpec((size, part), lambda g: (0, g))
    shape = jax.ShapeDtypeStruct
    spec, full = one_of(count, at, length, width)
    weights = pl.BlockSpec((3, width, part), lambda g: (0, 0, g))
    lines = pl.BlockSpec((1, GROUP, 2 * length), lambda g: (g, 0, 0))
    return pl.pallas_call(
        back_heads_kernel,
        grid=(groups,),
        in_specs=[
            one_in(at, length, width), whole(1, width), columns(length), columns(length),
            columns(width), columns(width), columns(width),
            columns(length), columns(length), columns(length),
            pl.BlockSpec((GROUP, BLOCK, skewed.shape[2]), lambda g: (g, 0, 0)),
            pl.BlockSpec((1, length, GROUP), lambda g: (g, 0, 0)), whole(length, width),
            *([weights, lines, whole(1, width)] if prior else []),
            *([pl.BlockSpec(memory_space=pl.ANY)] * len(grads)),
        ],
        out_specs=[
            lines, weights,
            spec, whole(1, width),
        ],
        input_output_aliases={13 + len(prior): 2} if grads else {},
        out_shape=[
            shape((groups, GROUP, 2 * length), f32), shape((3, width, width), bf16),
            full, shape((1, width), f32),
        ],
        scratch_shapes=[
            pltpu.VMEM((width, length), bf16), pltpu.VMEM((length, width), f32),
            pltpu.VMEM((BLOCK, 2 * length), f32),
        ],
        compiler_params=params(60),
        cost_estimate=pl.CostEstimate(
            flops=groups * (2 * length * width * part * 6 + 8 * length * length * part * 4),
            bytes_accessed=21 * MIB, transcendentals=HEADS * length * length,
        ),
        name="back_heads",
    )(
        tokens, gain, grad_mixed, mixed, wq, wk, wv, q, k, v, skewed, lse, grad_resid,
        *prior, *grads,
    )


def pack_kernel(*refs):
    for at, ref in enumerate(refs[:-1]):
        refs[-1][at] = ref[...]


def pack_call(*parts):
    return pl.pallas_call(
        pack_kernel,
        out_shape=jax.ShapeDtypeStruct((len(parts), *parts[0].shape), parts[0].dtype),
        compiler_params=params(60),
        name="pack",
    )(*parts)


def skew_kernel(lines_ref, out_ref):
    heads, block, span = out_ref.shape
    full = lines_ref.shape[1]
    for head in range(heads):
        row = jnp.broadcast_to(lines_ref[head : head + 1, :], (16, full))
        base = pltpu.roll(row, full - (block - 1), 1, stride=1, stride_axis=0)
        for at in range(0, block, 16):
            turned = base if at == 0 else pltpu.roll(base, at, 1)
            out_ref[head, at : at + 16, :] = turned[:, :span].astype(bf16)


def skew_call(lines, block):
    heads, span = lines.shape
    return pl.pallas_call(
        skew_kernel,
        out_shape=jax.ShapeDtypeStruct((heads, block, span - block), bf16),
        compiler_params=params(16),
        name="skew",
    )(lines)


def exchange(buffer):
    return lax.all_to_all(buffer, AXES, split_axis=0, concat_axis=0, tiled=True)


def swap(value, bit):
    devices = lax.axis_size(AXES)
    return lax.ppermute(value, AXES, [(at, at ^ (1 << bit)) for at in range(devices)])


def own_bit(bit):
    return ((lax.axis_index(AXES) >> bit) & 1) == 1


def gather_step(held, bit):
    value, done = held
    theirs = swap(value, bit)
    upper = own_bit(bit)
    place = sum(1 for other in done if other > bit)
    value = jnp.stack(
        [jnp.where(upper, theirs, value), jnp.where(upper, value, theirs)], axis=place
    )
    return value, done + [bit]


def gather_all(value, order):
    held = (value, [])
    for bit in order:
        held = gather_step(held, bit)
    return held[0].reshape((-1,) + value.shape)


def scatter_step(held, bit):
    value, left = held
    place = 1 + left.index(bit)
    low = lax.index_in_dim(value, 0, place, keepdims=False)
    high = lax.index_in_dim(value, 1, place, keepdims=False)
    upper = own_bit(bit)
    sent = jnp.where(upper, low, high).astype(bf16)
    value = jnp.where(upper, high, low).astype(f32) + swap(sent, bit).astype(f32)
    return value, [other for other in left if other != bit]


def pack_rows(parts, width):
    lead = parts[0].shape[0]
    flat = jnp.concatenate([part.reshape(lead, -1) for part in parts], axis=1)
    short = -flat.shape[1] % width
    return jnp.pad(flat, ((0, 0), (0, short))).reshape(lead, -1, width)


def unpack_rows(packed, sizes):
    flat = packed.reshape(packed.shape[0], -1)
    out, at = [], 0
    for size in sizes:
        out.append(flat[:, at : at + size])
        at += size
    return out


def tiles_of(shard, experts):
    return -(-shard // 8), -(-experts // LANES) * LANES


def small_slab(router, short, width):
    lead, shard, experts = router.shape
    tall, lanes = tiles_of(shard, experts)
    router = jnp.pad(router, ((0, 0), (0, 8 * tall - shard), (0, lanes - experts)))
    parts = [router[:, 8 * at : 8 * at + 8] for at in range(tall)]
    parts.append(pack_rows(short, 8 * LANES).reshape(lead, 8, LANES))
    slab = jnp.concatenate(parts, axis=2)
    return jnp.pad(slab, ((0, 0), (0, 0), (0, width - slab.shape[2])))


def slab_parts(slab, shard, experts, sizes):
    tall, lanes = tiles_of(shard, experts)
    parts = [slab[:, :, lanes * at : lanes * at + experts] for at in range(tall)]
    short = slab[:, :, lanes * tall : lanes * tall + LANES]
    return jnp.concatenate(parts, axis=1)[:, :shard], unpack_rows(short, sizes)


def body(
    tokens,
    w_query,
    w_key,
    w_value,
    w_output,
    w_router,
    gain_attn,
    gain_ffn,
    rel_bias,
    router_bias,
    w_in,
    w_out,
    routes,
    fill_rank,
    bucket_map,
    upstream_grad,
):
    batches, length, width = tokens.shape
    devices = lax.axis_size(AXES)
    wide_bits = lax.axis_size("wide").bit_length() - 1
    bits = devices.bit_length() - 1
    local_experts = w_in.shape[0]
    experts = local_experts * devices
    capacity = max(2, 5 * length // (4 * experts))
    slots = experts * capacity
    span = 2 * length
    shard = w_query.shape[0]
    far = list(range(wide_bits, bits))
    near = list(range(1, wide_bits))
    turned = near[1:] + near[:1]

    expert_ids = jnp.arange(experts, dtype=jnp.int32)

    def plan(route, order):
        route_hot = (route[:, None] == expert_ids[None, :]).astype(f32)
        earlier = (order[None, :] < order[:, None]).astype(bf16)
        counts = jnp.dot(earlier, route_hot.astype(bf16), preferred_element_type=f32)
        slot = jnp.sum(counts * route_hot, axis=-1).astype(jnp.int32)
        first = jnp.where(slot < capacity, route * (2 * capacity) + slot, -1)
        second = jnp.where(first >= 0, first + capacity, -1)
        return jnp.stack([first, second], axis=0)

    short = [gain_attn, gain_ffn, rel_bias, router_bias]
    packed, short_router, *short = lax.optimization_barrier(
        (pack_call(w_query, w_key, w_value, w_output), w_router, *short)
    )
    sizes = [part.size for part in short]
    slab = small_slab(short_router[None], [part[None] for part in short], width)
    square, small = (packed, []), (slab[0], [])
    for bit in far[::-1]:
        square, small = gather_step(square, bit), gather_step(small, bit)
    spots = [plan(routes[at, :, 0], fill_rank[at]) for at in range(batches)]
    raw_spots = jnp.concatenate([spots[at][at] for at in range(batches)], axis=0)
    raw_ids = jnp.arange(2 * slots, dtype=jnp.int32)
    raw_sent = jnp.dot(
        (raw_ids[:, None] == raw_spots[None, :]).astype(bf16),
        upstream_grad.reshape(batches * length, width),
        preferred_element_type=f32,
    ).astype(bf16)
    value, small, raw_sent = lax.optimization_barrier((square[0], small[0], raw_sent))
    done = far[::-1]
    value = value.reshape((2,) * len(far) + (4, shard, width))
    value = [lax.index_in_dim(value, i, len(far), keepdims=False) for i in range(4)]
    low = (jnp.concatenate(value[:2] + [small], axis=-2), done)
    high = (jnp.concatenate(value[2:], axis=-2), done)
    for number, (one, two) in enumerate(zip(near[::-1], turned[::-1])):
        low, high = gather_step(low, one), gather_step(high, two)
        if number == 0:
            first, second, raw_sent = lax.optimization_barrier((low[0], high[0], raw_sent))
            low, high = (first, low[1]), (second, high[1])

    raw_arrived = exchange(raw_sent.reshape(devices, 2 * capacity, width))

    first, second = lax.optimization_barrier((low[0], high[0]))
    low, high = gather_step((first, low[1]), 0), gather_step((second, high[1]), 0)
    low, high = (part[0].reshape(devices, -1, width) for part in (low, high))
    wq, wk, wv, wo = (
        part[:, i * shard : (i + 1) * shard].reshape(width, width)
        for part in (low, high)
        for i in range(2)
    )
    wr_all, (gain_one, gain_two, rel_flat, bias_all) = slab_parts(
        low[:, 2 * shard :], shard, experts, sizes
    )
    wr_all = wr_all.reshape(width, experts)
    gain_one = gain_one.reshape(1, width).astype(f32)
    gain_two = gain_two.reshape(1, width).astype(f32)
    bias_all = bias_all.reshape(1, experts).astype(f32)
    table = rel_flat.reshape(BUCKETS, HEADS).T
    bucket_hot = (
        jnp.arange(BUCKETS, dtype=jnp.int32)[:, None]
        == jnp.pad(bucket_map, (0, 1), constant_values=-1)[None, :]
    ).astype(bf16)
    skewed = skew_call(jnp.dot(table, bucket_hot, preferred_element_type=f32), BLOCK)
    own = lax.axis_index(AXES).astype(jnp.int32).reshape(1)
    count = 8 if 8 * capacity % 16 == 0 else 16
    row = np.arange(count * capacity, dtype=np.int32)
    row = row + (row // capacity) * capacity
    place = jnp.asarray(np.stack([row, row + capacity], axis=1))
    fronts, arrived, returned = [], [], []
    acts = tokens
    for at in range(batches):
        if at == 1:
            acts, raw_arrived, targets = lax.optimization_barrier(
                (acts, raw_arrived, [(spots[i].T, routes[i]) for i in range(batches)])
            )
        front = front_call(
            at, acts, wq, wk, wv, wo, skewed, gain_one, gain_two, spots[at], slots
        )
        fronts.append(front)
        arrived.append(exchange(front[-1].reshape(devices, 2 * capacity, width // 2)))
    grad_in = grad_out = 0.0
    for at in range(batches):
        sent, rows, active, grad_inner, grad_result = expert_call(
            at,
            own,
            arrived[at].reshape(2 * slots, width // 2),
            raw_arrived.reshape(2 * slots, width),
            wr_all,
            bias_all,
            place,
            w_in[0],
            w_out[0],
        )
        if at == batches - 1:
            sent, grad_in, grad_out = lax.optimization_barrier((sent, grad_in, grad_out))
        grad_in += jnp.einsum("rd,rf->df", rows, grad_inner, preferred_element_type=f32)
        grad_out += jnp.einsum("rf,rd->fd", active, grad_result, preferred_element_type=f32)
        back = exchange(sent.reshape(devices, 2 * capacity, width))
        back, grad_in, grad_out = lax.optimization_barrier((back, grad_in, grad_out))
        returned.append(back)

    row_prior, head_prior, outputs, grads = [], [], [], []
    for at in range(batches):
        q, k, v, mixed, lse, sent = fronts[at]
        row_part = back_rows_call(
            at, batches, *targets[at], returned[at].reshape(2 * slots, width), upstream_grad,
            tokens, mixed, gain_two, wr_all, bias_all, wo, row_prior,
            outputs,
        )
        outputs = row_part[:1]
        row_prior = row_part[3:]
        head_part = back_heads_call(
            at, batches, tokens, gain_one, row_part[2], mixed, wq, wk, wv, q, k, v, skewed, lse,
            row_part[1], head_prior, grads,
        )
        grads = head_part[2:3]
        head_prior = [head_part[1], head_part[0], head_part[3]]

    g_output, g_router, g_gain_two, g_bias = row_prior
    g_heads, lines, g_gain_one = head_prior
    def halved(parts):
        value = jnp.concatenate([part.astype(bf16) for part in parts], axis=1)
        value = value.reshape((1,) + (2,) * bits + value.shape[1:])
        return scatter_step((value, list(range(bits))[::-1]), 0)

    outer = halved([g_output.reshape(devices, shard, width)])
    g_heads = g_heads.reshape(3, devices, shard, width)
    inner = halved(list(g_heads))
    cut = 2 * shard
    low = (inner[0][..., :cut, :], inner[1])
    high = (jnp.concatenate([inner[0][..., cut:, :], outer[0]], axis=-2), inner[1])
    for number, (one, two) in enumerate(zip(near, turned)):
        low, high = scatter_step(low, one), scatter_step(high, two)
        if number == 0:
            first, second, g_router, g_gain_two, g_bias, lines, g_gain_one = (
                lax.optimization_barrier(
                    (low[0], high[0], g_router, g_gain_two, g_bias, lines, g_gain_one)
                )
            )
            low, high = (first, low[1]), (second, high[1])
            g_rel = jnp.einsum(
                "hn,bn->bh",
                lines.reshape(HEADS, span),
                bucket_hot.astype(f32),
                precision=lax.Precision.HIGHEST,
            )
            short = [
                part.reshape(devices, -1) for part in (g_gain_one, g_gain_two, g_rel, g_bias)
            ]
            short_pack = pack_rows(short, 8 * LANES).reshape(devices, -1, LANES).astype(bf16)
            lanes = -(-experts // LANES) * LANES
            router_pack = jnp.pad(g_router.astype(bf16), ((0, 0), (0, lanes - experts)))
            router_pack = router_pack.reshape(devices, -1, LANES)
            small = jnp.concatenate([router_pack, short_pack], axis=1)
            small = (small.reshape((1,) + (2,) * bits + small.shape[1:]), list(range(bits))[::-1])
            for bit in [0] + near:
                small = scatter_step(small, bit)
    held = (jnp.concatenate([low[0], high[0]], axis=-2), low[1])
    for bit in far:
        value, ahead = lax.optimization_barrier((held[0], small[0]))
        held = scatter_step((value, held[1]), bit)
        small = scatter_step((ahead, small[1]), bit)
    r_query, r_key, r_value, r_output = jnp.split(
        held[0][0], [shard, 2 * shard, 3 * shard], axis=0
    )
    cut = router_pack.shape[1]
    r_router = small[0][0, :cut].reshape(shard, lanes)[:, :experts]
    tail = unpack_rows(small[0][:, cut:], [part.shape[1] for part in short])
    r_gain_one, r_gain_two, r_rel, r_bias = (
        part.reshape(shape)
        for part, shape in zip(
            tail, (gain_attn.shape, gain_ffn.shape, rel_bias.shape, router_bias.shape)
        )
    )
    return (
        outputs[0],
        grads[0],
        r_query,
        r_key,
        r_value,
        r_output,
        r_router,
        r_gain_one,
        r_gain_two,
        r_rel,
        r_bias,
        grad_in[None],
        grad_out[None],
    )


def solution(mesh):
    both = P(AXES)
    in_specs = (both,) * 14 + (P(), both)
    out_specs = (both,) * 13
    return jax.shard_map(body, mesh=mesh, in_specs=in_specs, out_specs=out_specs, check_vma=False)
```

```python
import functools
import jax
import jax.numpy as jnp
import numpy as np
from jax import lax
from jax.experimental import pallas as pl
from jax.experimental.pallas import tpu as pltpu
from jax.sharding import PartitionSpec as P

HEADS = 12
HEAD = 64
BUCKETS = 32
PAIR = 2 * HEAD
GROUP = 4
BLOCK = 128
LANES = 128
AXES = ("narrow", "wide")
MIB = 1024 * 1024

epsilon = 1e-06
f32 = jnp.float32
bf16 = jnp.bfloat16


def mm(a, b):
    return lax.dot_general(a, b, (((1,), (0,)), ((), ())), preferred_element_type=f32)


def mm_nt(a, b):
    return lax.dot_general(a, b, (((1,), (1,)), ((), ())), preferred_element_type=f32)


def mm_tn(a, b):
    return lax.dot_general(a, b, (((0,), (0,)), ((), ())), preferred_element_type=f32)


def norm_scale(values):
    return lax.rsqrt(jnp.mean(values * values, axis=-1, keepdims=True) + epsilon)


def softmax_rows(logits):
    shifted = jnp.exp(logits - jnp.max(logits, axis=-1, keepdims=True))
    return shifted / jnp.sum(shifted, axis=-1, keepdims=True)


def pair_mask(shape, half):
    lane = lax.broadcasted_iota(jnp.int32, shape, 1)
    return (lane < HEAD) if half == 0 else (lane >= HEAD)


def params(size):
    return pltpu.CompilerParams(vmem_limit_bytes=size * MIB)


def front_kernel(
    tokens_ref, wq_ref, wk_ref, wv_ref, wo_ref, skew_ref, gain_one_ref, gain_two_ref, spots_ref,
    q_ref, k_ref, v_ref, mixed_ref, lse_ref, sent_ref, normed_ref, resid_ref,
):
    step = pl.program_id(0)
    length, width = tokens_ref.shape

    @pl.when(step == 0)
    def start():
        acts = tokens_ref[...].astype(f32)
        normed_ref[...] = (acts * norm_scale(acts) * gain_one_ref[...]).astype(bf16)
        resid_ref[...] = acts

    normed = normed_ref[...]
    q_ref[...] = mm(normed, wq_ref[...]).astype(bf16)
    k_ref[...] = mm(normed, wk_ref[...]).astype(bf16)
    v_ref[...] = mm(normed, wv_ref[...]).astype(bf16)
    for pair in range(GROUP // 2):
        cols = slice(PAIR * pair, PAIR * (pair + 1))
        query, key, value = q_ref[:, cols], k_ref[:, cols], v_ref[:, cols]
        out = None
        for half in range(2):
            head = 2 * pair + half
            mask = pair_mask(query.shape, half)
            scores = mm_nt(jnp.where(mask, query, jnp.zeros_like(query)), key)
            parts = []
            for at in range(length // BLOCK):
                rows = slice(BLOCK * at, BLOCK * (at + 1))
                low = length - BLOCK * (at + 1)
                part = scores[rows, :] + skew_ref[head, :, low : low + length].astype(f32)
                peak = jnp.max(part, axis=-1, keepdims=True)
                part = jnp.exp(part - peak)
                total = jnp.sum(part, axis=-1, keepdims=True)
                lse_ref[0, rows, head : head + 1] = peak + jnp.log(total)
                parts.append((part * (1.0 / total)).astype(bf16))
            probs = jnp.concatenate(parts, axis=0)
            term = mm(probs, jnp.where(mask, value, jnp.zeros_like(value)))
            out = term if out is None else out + term
        mixed_ref[:, cols] = out.astype(bf16)
    resid_ref[...] += mm(mixed_ref[...], wo_ref[...])

    @pl.when(step == pl.num_programs(0) - 1)
    def finish():
        resid = resid_ref[...]
        normed_two = (resid * norm_scale(resid) * gain_two_ref[...]).astype(bf16)
        rows = lax.broadcasted_iota(jnp.int32, (sent_ref.shape[0], length), 0)
        left = mm((rows == spots_ref[0:1, :]).astype(bf16), normed_two[:, : width // 2])
        right = mm((rows == spots_ref[1:2, :]).astype(bf16), normed_two[:, width // 2 :])
        sent_ref[...] = (left + right).astype(bf16)


def one_in(at, length, width):
    return pl.BlockSpec((None, length, width), lambda *g: (at, 0, 0))


def front_call(at, tokens, wq, wk, wv, wo, skewed, gain_one, gain_two, spots, slots):
    length, width = tokens.shape[1:]
    part = GROUP * HEAD
    groups = HEADS // GROUP
    whole = lambda *shape: pl.BlockSpec(shape, lambda g: (0,) * len(shape))
    columns = lambda rows: pl.BlockSpec((rows, part), lambda g: (0, g))
    shape = jax.ShapeDtypeStruct
    return pl.pallas_call(
        front_kernel,
        grid=(groups,),
        in_specs=[
            one_in(at, length, width), columns(width), columns(width), columns(width),
            pl.BlockSpec((part, width), lambda g: (g, 0)),
            pl.BlockSpec((GROUP, BLOCK, skewed.shape[2]), lambda g: (g, 0, 0)),
            whole(1, width), whole(1, width), whole(2, length),
        ],
        out_specs=[
            columns(length), columns(length), columns(length), columns(length),
            pl.BlockSpec((1, length, GROUP), lambda g: (g, 0, 0)),
            whole(2 * slots, width // 2),
        ],
        out_shape=[
            *(4 * [shape((length, width), bf16)]), shape((groups, length, GROUP), f32),
            shape((2 * slots, width // 2), bf16),
        ],
        scratch_shapes=[pltpu.VMEM((length, width), bf16), pltpu.VMEM((length, width), f32)],
        compiler_params=params(60),
        cost_estimate=pl.CostEstimate(flops=1000000, bytes_accessed=MIB // 4, transcendentals=0),
        name="front",
    )(tokens, wq, wk, wv, wo, skewed, gain_one, gain_two, spots)


def bell(values):
    size = jnp.abs(values)
    t = 1.0 / (1.0 + (0.3275911 * 0.7071067811865476) * size)
    falling = jnp.exp(-0.5 * values * values)
    poly = t * (
        0.127414796
        + t * (-0.142248368 + t * (0.7107068705 + t * (-0.7265760135 + t * 0.5307027145)))
    )
    tail = poly * falling
    return jnp.where(values < 0, tail, 1.0 - tail), falling * 0.3989422804014327


def expert_kernel(
    mine_at, own_ref, arrived_ref, raw_ref, wr_ref, rbias_ref, place_ref, placed_ref, win_ref, wout_ref,
    sent_ref, rows_ref, active_ref, gradinner_ref, gradresult_ref, result_acc, rows_acc,
):
    step = pl.program_id(0)
    last = pl.num_programs(0) - 1
    count = rows_ref.shape[0]
    unit = place_ref.shape[0]

    @pl.when(step == 0)
    def start():
        half = arrived_ref.shape[1]
        ids = lax.broadcasted_iota(jnp.int32, (unit, 2 * unit), 1)
        for side in range(2):
            pick = (ids == place_ref[:, side : side + 1]).astype(bf16)
            for at in range(0, count, unit):
                rows_ref[at : at + unit, half * side : half * (side + 1)] = mm(
                    pick, arrived_ref[2 * at : 2 * (at + unit), :]
                ).astype(bf16)
        probs = softmax_rows(mm(rows_ref[...], wr_ref[...]) + rbias_ref[...])
        mine = lax.broadcasted_iota(jnp.int32, probs.shape, 1) == own_ref[0]
        gate = jnp.sum(jnp.where(mine, probs, 0.0), axis=-1, keepdims=True)
        pick = (ids == place_ref[:, mine_at : mine_at + 1]).astype(bf16)
        for at in range(0, count, unit):
            raw = mm(pick, raw_ref[2 * at : 2 * (at + unit), :])
            gradresult_ref[at : at + unit, :] = (gate[at : at + unit] * raw).astype(bf16)

    inner = mm(rows_ref[...], win_ref[...])
    grad_active = mm_nt(gradresult_ref[...], wout_ref[...])
    share, density = bell(inner)
    active = (inner * share).astype(bf16)
    grad_inner = (grad_active * (share + inner * density)).astype(bf16)
    active_ref[...] = active
    gradinner_ref[...] = grad_inner
    result = mm(active, wout_ref[...])
    grad_rows = mm_nt(grad_inner, win_ref[...])

    @pl.when(step == 0)
    def first():
        result_acc[...] = result
        rows_acc[...] = grad_rows

    @pl.when(step > 0)
    def more():
        result_acc[...] += result
        rows_acc[...] += grad_rows

    @pl.when(step == last)
    def finish():
        ids = lax.broadcasted_iota(jnp.int32, (2 * unit, unit), 0)
        picks = [(ids == placed_ref[side : side + 1, :]).astype(bf16) for side in range(2)]
        for at in range(0, count, unit):
            sent_ref[2 * at : 2 * (at + unit), :] = (
                mm(picks[0], result_acc[at : at + unit, :].astype(bf16))
                + mm(picks[1], rows_acc[at : at + unit, :].astype(bf16))
            ).astype(bf16)


def expert_call(mine_at, own, arrived, raw, wr, rbias, place, w_in, w_out, part=1024):
    count, width = raw.shape[0] // 2, raw.shape[1]
    hidden = w_in.shape[1]
    experts = wr.shape[1]
    whole = lambda *shape: pl.BlockSpec(shape, lambda g, own: (0,) * len(shape))
    columns = lambda n: pl.BlockSpec((n, part), lambda g, own: (0, g))
    return pl.pallas_call(
        functools.partial(expert_kernel, mine_at),
        grid_spec=pltpu.PrefetchScalarGridSpec(
            num_scalar_prefetch=1,
            grid=(hidden // part,),
            in_specs=[
                whole(2 * count, width // 2), whole(2 * count, width), whole(width, experts),
                whole(1, experts), whole(*place.shape), whole(*place.shape[::-1]),
                columns(width), pl.BlockSpec((part, width), lambda g, own: (g, 0)),
            ],
            out_specs=[
                whole(2 * count, width), whole(count, width), columns(count), columns(count),
                whole(count, width),
            ],
            scratch_shapes=[pltpu.VMEM((count, width), f32), pltpu.VMEM((count, width), f32)],
        ),
        out_shape=[
            jax.ShapeDtypeStruct((2 * count, width), bf16),
            jax.ShapeDtypeStruct((count, width), bf16),
            jax.ShapeDtypeStruct((count, hidden), bf16),
            jax.ShapeDtypeStruct((count, hidden), bf16),
            jax.ShapeDtypeStruct((count, width), bf16),
        ],
        compiler_params=params(60),
        cost_estimate=pl.CostEstimate(
            flops=8 * count * width * hidden, bytes_accessed=20 * MIB,
            transcendentals=count * hidden,
        ),
        name="expert",
    )(own, arrived, raw, wr, rbias, place, place.T, w_in, w_out)


def back_rows_kernel(
    target_ref, route_ref, returned_ref, up_ref, tokens_ref, mixed_ref, gain_ref, wr_ref,
    rbias_ref, wo_ref, *refs,
):
    output_ref, gradresid_ref, gradmixed_ref, go_ref, grw_ref, ggain_ref, gbias_ref = refs[-7:]
    length = up_ref.shape[0]
    experts = wr_ref.shape[1]
    mixed = mixed_ref[...]
    resid = tokens_ref[...].astype(f32) + mm(mixed, wo_ref[...])
    scale = norm_scale(resid)
    normed_two = (resid * scale * gain_ref[...]).astype(bf16)
    router = softmax_rows(mm(normed_two, wr_ref[...]) + rbias_ref[...])
    returned = returned_ref[...]
    ids = lax.broadcasted_iota(jnp.int32, (length, returned.shape[0]), 1)
    expert_rows = mm((ids == target_ref[:, 0:1]).astype(bf16), returned)
    grad_back = mm((ids == target_ref[:, 1:2]).astype(bf16), returned)
    up = up_ref[...].astype(f32)
    hot = lax.broadcasted_iota(jnp.int32, (length, experts), 1) == route_ref[...]
    gate = jnp.sum(jnp.where(hot, router, 0.0), axis=-1, keepdims=True)
    output_ref[0] = (resid + gate * expert_rows).astype(bf16)
    grad_gate = jnp.sum(up * expert_rows, axis=-1, keepdims=True)
    grad_logits = (router * (jnp.where(hot, grad_gate, 0.0) - gate * grad_gate)).astype(bf16)
    grad_normed = mm_nt(grad_logits, wr_ref[...]) + grad_back
    gbias = jnp.sum(grad_logits.astype(f32), axis=0, keepdims=True)
    grw = mm_tn(normed_two, grad_logits)
    ggain = jnp.sum(grad_normed * resid * scale, axis=0, keepdims=True)
    weighted = grad_normed * gain_ref[...]
    slope = scale * scale * scale * jnp.mean(weighted * resid, axis=-1, keepdims=True)
    grad_resid = up + (scale * weighted - resid * slope)
    gradresid_ref[...] = grad_resid
    grad_branch = grad_resid.astype(bf16)
    go = mm_tn(mixed, grad_branch)
    sums = [go, grw, ggain, gbias]
    if len(refs) > 7:
        sums = [one + prior[...].astype(f32) for one, prior in zip(sums, refs)]
    for ref, one in zip((go_ref, grw_ref, ggain_ref, gbias_ref), sums):
        ref[...] = one.astype(ref.dtype)
    gradmixed_ref[...] = mm_nt(grad_branch, wo_ref[...]).astype(bf16)


def one_of(count, at, length, width):
    spec = pl.BlockSpec((1, length, width), lambda *g: (at, 0, 0))
    return spec, jax.ShapeDtypeStruct((count, length, width), bf16)


def back_rows_call(
    at, count, target, route, returned, up, tokens, mixed, gain, wr, rbias, wo, prior, output
):
    length, width = up.shape[1:]
    experts = wr.shape[1]
    shape = jax.ShapeDtypeStruct
    spec, full = one_of(count, at, length, width)
    vmem = pl.BlockSpec(memory_space=pltpu.VMEM)
    inputs = 10 + len(prior)
    return pl.pallas_call(
        back_rows_kernel,
        grid=(1,),
        in_specs=[vmem] * 3
        + [one_in(at, length, width)] * 2
        + [vmem] * (inputs - 5)
        + [pl.BlockSpec(memory_space=pl.ANY)] * len(output),
        out_specs=[spec] + [vmem] * 6,
        input_output_aliases={inputs: 0} if output else {},
        out_shape=[
            full, shape((length, width), f32),
            shape((length, width), bf16), shape((width, width), bf16),
            shape((width, experts), f32), shape((1, width), f32), shape((1, experts), f32),
        ],
        compiler_params=params(60),
        cost_estimate=pl.CostEstimate(
            flops=2 * length * width * (3 * width + 2 * returned.shape[0]),
            bytes_accessed=12 * MIB, transcendentals=0,
        ),
        name="back_rows",
    )(
        target, route, returned, up, tokens, mixed, gain, wr, rbias, wo, *prior, *output
    )


def back_heads_kernel(
    tokens_ref, gain_ref, gradmixed_ref, mixed_ref, wq_ref, wk_ref, wv_ref, q_ref, k_ref, v_ref,
    skew_ref, lse_ref, gradresid_ref, *refs,
):
    prior_refs = refs[: (len(refs) - 7) // 3 * 3]
    line_ref, gw_ref, gradacts_ref, ggain_ref, normedt_ref, acc_ref, fold_ref = refs[-7:]
    step = pl.program_id(0)
    last = pl.num_programs(0) - 1
    length, width = tokens_ref.shape
    span = 2 * length

    @pl.when(step == 0)
    def start():
        acts = tokens_ref[...].astype(f32)
        normed = (acts * norm_scale(acts) * gain_ref[...]).astype(bf16)
        normedt_ref[...] = normed.T
        acc_ref[...] = jnp.zeros_like(acc_ref)

    dq, dk, dv = [], [], []
    for pair in range(GROUP // 2):
        cols = slice(PAIR * pair, PAIR * (pair + 1))
        query, key, value = q_ref[:, cols], k_ref[:, cols], v_ref[:, cols]
        grad = gradmixed_ref[:, cols]
        product = grad.astype(f32) * mixed_ref[:, cols].astype(f32)
        gq = gk = gv = None
        for half in range(2):
            head = 2 * pair + half
            mask = pair_mask(query.shape, half)
            clear = lambda a: jnp.where(mask, a, jnp.zeros_like(a))
            own, asked = clear(grad), clear(query)
            center = jnp.sum(clear(product), axis=-1, keepdims=True)
            scores = mm_nt(asked, key)
            grad_probs = mm_nt(own, value)
            all_probs, all_grads = [], []
            for at in range(length // BLOCK):
                rows = slice(BLOCK * at, BLOCK * (at + 1))
                low = length - BLOCK * (at + 1)
                part = scores[rows, :] + skew_ref[head, :, low : low + length].astype(f32)
                probs = jnp.exp(part - lse_ref[0, rows, head : head + 1])
                piece = probs * (grad_probs[rows, :] - center[rows, :])
                if at == 0:
                    fold_ref[:, :low] = jnp.zeros((BLOCK, low), f32)
                    fold_ref[:, low : low + length] = piece
                    fold_ref[:, low + length :] = jnp.zeros((BLOCK, length - low), f32)
                else:
                    fold_ref[:, low : low + length] += piece
                all_probs.append(probs.astype(bf16))
                all_grads.append(piece.astype(bf16))
            rows = fold_ref[...]
            size = BLOCK
            while size > 1:
                size //= 2
                rows = rows[:size] + pltpu.roll(rows[size:], span - size, 1)
            line = pltpu.roll(rows, BLOCK - 1, 1)
            if prior_refs:
                line = line + prior_refs[1][0, head : head + 1, :]
            line_ref[0, head : head + 1, :] = line
            probs = jnp.concatenate(all_probs, axis=0)
            grad_scores = jnp.concatenate(all_grads, axis=0)
            a = mm(grad_scores, clear(key))
            b = mm(asked.T, grad_scores)
            c = mm(own.T, probs)
            gq = a if gq is None else gq + a
            gk = b if gk is None else gk + b
            gv = c if gv is None else gv + c
        dq.append(gq.astype(bf16))
        dk.append(gk.T.astype(bf16))
        dv.append(gv.T.astype(bf16))
    dq, dk, dv = (jnp.concatenate(x, axis=1) for x in (dq, dk, dv))
    normedt = normedt_ref[...]
    for i, grad in enumerate((dq, dk, dv)):
        total = mm(normedt, grad)
        if prior_refs:
            total = total + prior_refs[0][i].astype(f32)
        gw_ref[i] = total.astype(bf16)
    acc_ref[...] += mm_nt(dq, wq_ref[...]) + mm_nt(dk, wk_ref[...]) + mm_nt(dv, wv_ref[...])

    @pl.when(step == last)
    def finish():
        grad_normed = acc_ref[...]
        acts = tokens_ref[...].astype(f32)
        scale = norm_scale(acts)
        ggain = jnp.sum(grad_normed * acts * scale, axis=0, keepdims=True)
        if prior_refs:
            ggain = ggain + prior_refs[2][...]
        ggain_ref[...] = ggain
        weighted = grad_normed * gain_ref[...]
        slope = scale * scale * scale * jnp.mean(weighted * acts, axis=-1, keepdims=True)
        grad_acts = gradresid_ref[...] + (scale * weighted - acts * slope)
        gradacts_ref[0] = grad_acts.astype(bf16)


def back_heads_call(
    at, count, tokens, gain, grad_mixed, mixed, wq, wk, wv, q, k, v, skewed, lse, grad_resid,
    prior, grads,
):
    length, width = tokens.shape[1:]
    part = GROUP * HEAD
    groups = HEADS // GROUP
    whole = lambda *shape: pl.BlockSpec(shape, lambda g: (0,) * len(shape))
    columns = lambda size: pl.BlockSpec((size, part), lambda g: (0, g))
    shape = jax.ShapeDtypeStruct
    spec, full = one_of(count, at, length, width)
    weights = pl.BlockSpec((3, width, part), lambda g: (0, 0, g))
    lines = pl.BlockSpec((1, GROUP, 2 * length), lambda g: (g, 0, 0))
    return pl.pallas_call(
        back_heads_kernel,
        grid=(groups,),
        in_specs=[
            one_in(at, length, width), whole(1, width), columns(length), columns(length),
            columns(width), columns(width), columns(width),
            columns(length), columns(length), columns(length),
            pl.BlockSpec((GROUP, BLOCK, skewed.shape[2]), lambda g: (g, 0, 0)),
            pl.BlockSpec((1, length, GROUP), lambda g: (g, 0, 0)), whole(length, width),
            *([weights, lines, whole(1, width)] if prior else []),
            *([pl.BlockSpec(memory_space=pl.ANY)] * len(grads)),
        ],
        out_specs=[
            lines, weights,
            spec, whole(1, width),
        ],
        input_output_aliases={13 + len(prior): 2} if grads else {},
        out_shape=[
            shape((groups, GROUP, 2 * length), f32), shape((3, width, width), bf16),
            full, shape((1, width), f32),
        ],
        scratch_shapes=[
            pltpu.VMEM((width, length), bf16), pltpu.VMEM((length, width), f32),
            pltpu.VMEM((BLOCK, 2 * length), f32),
        ],
        compiler_params=params(60),
        cost_estimate=pl.CostEstimate(
            flops=groups * (2 * length * width * part * 6 + 8 * length * length * part * 4),
            bytes_accessed=21 * MIB, transcendentals=HEADS * length * length,
        ),
        name="back_heads",
    )(
        tokens, gain, grad_mixed, mixed, wq, wk, wv, q, k, v, skewed, lse, grad_resid,
        *prior, *grads,
    )


def pack_kernel(*refs):
    for at, ref in enumerate(refs[:-1]):
        refs[-1][at] = ref[...]


def pack_call(*parts):
    return pl.pallas_call(
        pack_kernel,
        out_shape=jax.ShapeDtypeStruct((len(parts), *parts[0].shape), parts[0].dtype),
        compiler_params=params(60),
        name="pack",
    )(*parts)


def skew_kernel(lines_ref, out_ref):
    heads, block, span = out_ref.shape
    full = lines_ref.shape[1]
    for head in range(heads):
        row = jnp.broadcast_to(lines_ref[head : head + 1, :], (16, full))
        base = pltpu.roll(row, full - (block - 1), 1, stride=1, stride_axis=0)
        for at in range(0, block, 16):
            turned = base if at == 0 else pltpu.roll(base, at, 1)
            out_ref[head, at : at + 16, :] = turned[:, :span].astype(bf16)


def skew_call(lines, block):
    heads, span = lines.shape
    return pl.pallas_call(
        skew_kernel,
        out_shape=jax.ShapeDtypeStruct((heads, block, span - block), bf16),
        compiler_params=params(16),
        name="skew",
    )(lines)


def exchange(buffer):
    return lax.all_to_all(buffer, AXES, split_axis=0, concat_axis=0, tiled=True)


def swap(value, bit):
    devices = lax.axis_size(AXES)
    return lax.ppermute(value, AXES, [(at, at ^ (1 << bit)) for at in range(devices)])


def own_bit(bit):
    return ((lax.axis_index(AXES) >> bit) & 1) == 1


def gather_step(held, bit):
    value, done = held
    theirs = swap(value, bit)
    upper = own_bit(bit)
    place = sum(1 for other in done if other > bit)
    value = jnp.stack(
        [jnp.where(upper, theirs, value), jnp.where(upper, value, theirs)], axis=place
    )
    return value, done + [bit]


def gather_all(value, order):
    held = (value, [])
    for bit in order:
        held = gather_step(held, bit)
    return held[0].reshape((-1,) + value.shape)


def scatter_step(held, bit):
    value, left = held
    place = 1 + left.index(bit)
    low = lax.index_in_dim(value, 0, place, keepdims=False)
    high = lax.index_in_dim(value, 1, place, keepdims=False)
    upper = own_bit(bit)
    sent = jnp.where(upper, low, high).astype(bf16)
    value = jnp.where(upper, high, low).astype(f32) + swap(sent, bit).astype(f32)
    return value, [other for other in left if other != bit]


def pack_rows(parts, width):
    lead = parts[0].shape[0]
    flat = jnp.concatenate([part.reshape(lead, -1) for part in parts], axis=1)
    short = -flat.shape[1] % width
    return jnp.pad(flat, ((0, 0), (0, short))).reshape(lead, -1, width)


def unpack_rows(packed, sizes):
    flat = packed.reshape(packed.shape[0], -1)
    out, at = [], 0
    for size in sizes:
        out.append(flat[:, at : at + size])
        at += size
    return out


def tiles_of(shard, experts):
    return -(-shard // 8), -(-experts // LANES) * LANES


def small_slab(router, short, width):
    lead, shard, experts = router.shape
    tall, lanes = tiles_of(shard, experts)
    router = jnp.pad(router, ((0, 0), (0, 8 * tall - shard), (0, lanes - experts)))
    parts = [router[:, 8 * at : 8 * at + 8] for at in range(tall)]
    parts.append(pack_rows(short, 8 * LANES).reshape(lead, 8, LANES))
    slab = jnp.concatenate(parts, axis=2)
    return jnp.pad(slab, ((0, 0), (0, 0), (0, width - slab.shape[2])))


def slab_parts(slab, shard, experts, sizes):
    tall, lanes = tiles_of(shard, experts)
    parts = [slab[:, :, lanes * at : lanes * at + experts] for at in range(tall)]
    short = slab[:, :, lanes * tall : lanes * tall + LANES]
    return jnp.concatenate(parts, axis=1)[:, :shard], unpack_rows(short, sizes)


def body(
    tokens,
    w_query,
    w_key,
    w_value,
    w_output,
    w_router,
    gain_attn,
    gain_ffn,
    rel_bias,
    router_bias,
    w_in,
    w_out,
    routes,
    fill_rank,
    bucket_map,
    upstream_grad,
):
    batches, length, width = tokens.shape
    devices = lax.axis_size(AXES)
    wide_bits = lax.axis_size("wide").bit_length() - 1
    bits = devices.bit_length() - 1
    local_experts = w_in.shape[0]
    experts = local_experts * devices
    capacity = max(2, 5 * length // (4 * experts))
    slots = experts * capacity
    span = 2 * length
    shard = w_query.shape[0]
    far = list(range(wide_bits, bits))
    near = list(range(1, wide_bits))
    turned = near[1:] + near[:1]

    expert_ids = jnp.arange(experts, dtype=jnp.int32)

    def plan(route, order):
        route_hot = (route[:, None] == expert_ids[None, :]).astype(f32)
        earlier = (order[None, :] < order[:, None]).astype(bf16)
        counts = jnp.dot(earlier, route_hot.astype(bf16), preferred_element_type=f32)
        slot = jnp.sum(counts * route_hot, axis=-1).astype(jnp.int32)
        first = jnp.where(slot < capacity, route * (2 * capacity) + slot, -1)
        second = jnp.where(first >= 0, first + capacity, -1)
        return jnp.stack([first, second], axis=0)

    short = [gain_attn, gain_ffn, rel_bias, router_bias]
    packed, short_router, *short = lax.optimization_barrier(
        (pack_call(w_query, w_key, w_value, w_output), w_router, *short)
    )
    sizes = [part.size for part in short]
    slab = small_slab(short_router[None], [part[None] for part in short], width)
    square, small = (packed, []), (slab[0], [])
    for bit in far[::-1]:
        square, small = gather_step(square, bit), gather_step(small, bit)
    spots = [plan(routes[at, :, 0], fill_rank[at]) for at in range(batches)]
    raw_spots = jnp.concatenate([spots[at][at] for at in range(batches)], axis=0)
    raw_ids = jnp.arange(2 * slots, dtype=jnp.int32)
    raw_sent = jnp.dot(
        (raw_ids[:, None] == raw_spots[None, :]).astype(bf16),
        upstream_grad.reshape(batches * length, width),
        preferred_element_type=f32,
    ).astype(bf16)
    value, small, raw_sent = lax.optimization_barrier((square[0], small[0], raw_sent))
    done = far[::-1]
    value = value.reshape((2,) * len(far) + (4, shard, width))
    value = [lax.index_in_dim(value, i, len(far), keepdims=False) for i in range(4)]
    low = (jnp.concatenate(value[:2] + [small], axis=-2), done)
    high = (jnp.concatenate(value[2:], axis=-2), done)
    for number, (one, two) in enumerate(zip(near[::-1], turned[::-1])):
        low, high = gather_step(low, one), gather_step(high, two)
        if number == 0:
            first, second, raw_sent = lax.optimization_barrier((low[0], high[0], raw_sent))
            low, high = (first, low[1]), (second, high[1])

    raw_arrived = exchange(raw_sent.reshape(devices, 2 * capacity, width))

    first, second = lax.optimization_barrier((low[0], high[0]))
    low, high = gather_step((first, low[1]), 0), gather_step((second, high[1]), 0)
    low, high = (part[0].reshape(devices, -1, width) for part in (low, high))
    wq, wk, wv, wo = (
        part[:, i * shard : (i + 1) * shard].reshape(width, width)
        for part in (low, high)
        for i in range(2)
    )
    wr_all, (gain_one, gain_two, rel_flat, bias_all) = slab_parts(
        low[:, 2 * shard :], shard, experts, sizes
    )
    wr_all = wr_all.reshape(width, experts)
    gain_one = gain_one.reshape(1, width).astype(f32)
    gain_two = gain_two.reshape(1, width).astype(f32)
    bias_all = bias_all.reshape(1, experts).astype(f32)
    table = rel_flat.reshape(BUCKETS, HEADS).T
    bucket_hot = (
        jnp.arange(BUCKETS, dtype=jnp.int32)[:, None]
        == jnp.pad(bucket_map, (0, 1), constant_values=-1)[None, :]
    ).astype(bf16)
    skewed = skew_call(jnp.dot(table, bucket_hot, preferred_element_type=f32), BLOCK)
    own = lax.axis_index(AXES).astype(jnp.int32).reshape(1)
    count = 8 if 8 * capacity % 16 == 0 else 16
    row = np.arange(count * capacity, dtype=np.int32)
    row = row + (row // capacity) * capacity
    place = jnp.asarray(np.stack([row, row + capacity], axis=1))
    fronts, arrived, returned = [], [], []
    acts = tokens
    for at in range(batches):
        if at == 1:
            targets = [(spots[i].T, routes[i]) for i in range(batches)]
            acts, raw_arrived, targets, place, wr_all, bias_all = lax.optimization_barrier(
                (acts, raw_arrived, targets, place, wr_all, bias_all)
            )
        front = front_call(
            at, acts, wq, wk, wv, wo, skewed, gain_one, gain_two, spots[at], slots
        )
        fronts.append(front)
        arrived.append(exchange(front[-1].reshape(devices, 2 * capacity, width // 2)))
    grad_in = grad_out = 0.0
    for at in range(batches):
        sent, rows, active, grad_inner, grad_result = expert_call(
            at,
            own,
            arrived[at].reshape(2 * slots, width // 2),
            raw_arrived.reshape(2 * slots, width),
            wr_all,
            bias_all,
            place,
            w_in[0],
            w_out[0],
        )
        if at == batches - 1:
            sent, grad_in, grad_out = lax.optimization_barrier((sent, grad_in, grad_out))
        grad_in += jnp.einsum("rd,rf->df", rows, grad_inner, preferred_element_type=f32)
        grad_out += jnp.einsum("rf,rd->fd", active, grad_result, preferred_element_type=f32)
        back = exchange(sent.reshape(devices, 2 * capacity, width))
        back, grad_in, grad_out = lax.optimization_barrier((back, grad_in, grad_out))
        returned.append(back)

    row_prior, head_prior, outputs, grads = [], [], [], []
    for at in range(batches):
        q, k, v, mixed, lse, sent = fronts[at]
        row_part = back_rows_call(
            at, batches, *targets[at], returned[at].reshape(2 * slots, width), upstream_grad,
            tokens, mixed, gain_two, wr_all, bias_all, wo, row_prior,
            outputs,
        )
        outputs = row_part[:1]
        row_prior = row_part[3:]
        head_part = back_heads_call(
            at, batches, tokens, gain_one, row_part[2], mixed, wq, wk, wv, q, k, v, skewed, lse,
            row_part[1], head_prior, grads,
        )
        grads = head_part[2:3]
        head_prior = [head_part[1], head_part[0], head_part[3]]

    g_output, g_router, g_gain_two, g_bias = row_prior
    g_heads, lines, g_gain_one = head_prior
    def halved(parts):
        value = jnp.concatenate([part.astype(bf16) for part in parts], axis=1)
        value = value.reshape((1,) + (2,) * bits + value.shape[1:])
        return scatter_step((value, list(range(bits))[::-1]), 0)

    outer = halved([g_output.reshape(devices, shard, width)])
    g_heads = g_heads.reshape(3, devices, shard, width)
    inner = halved(list(g_heads))
    cut = 2 * shard
    low = (inner[0][..., :cut, :], inner[1])
    high = (jnp.concatenate([inner[0][..., cut:, :], outer[0]], axis=-2), inner[1])
    for number, (one, two) in enumerate(zip(near, turned)):
        low, high = scatter_step(low, one), scatter_step(high, two)
        if number == 0:
            first, second, g_router, g_gain_two, g_bias, lines, g_gain_one = (
                lax.optimization_barrier(
                    (low[0], high[0], g_router, g_gain_two, g_bias, lines, g_gain_one)
                )
            )
            low, high = (first, low[1]), (second, high[1])
            g_rel = jnp.einsum(
                "hn,bn->bh",
                lines.reshape(HEADS, span),
                bucket_hot.astype(f32),
                precision=lax.Precision.HIGHEST,
            )
            short = [
                part.reshape(devices, -1) for part in (g_gain_one, g_gain_two, g_rel, g_bias)
            ]
            short_pack = pack_rows(short, 8 * LANES).reshape(devices, -1, LANES).astype(bf16)
            lanes = -(-experts // LANES) * LANES
            router_pack = jnp.pad(g_router.astype(bf16), ((0, 0), (0, lanes - experts)))
            router_pack = router_pack.reshape(devices, -1, LANES)
            small = jnp.concatenate([router_pack, short_pack], axis=1)
            small = jnp.sum(exchange(small).astype(f32), axis=0)
    held = (jnp.concatenate([low[0], high[0]], axis=-2), low[1])
    for bit in far:
        held = scatter_step(held, bit)
    r_query, r_key, r_value, r_output = jnp.split(
        held[0][0], [shard, 2 * shard, 3 * shard], axis=0
    )
    cut = router_pack.shape[1]
    r_router = small[:cut].reshape(shard, lanes)[:, :experts]
    tail = unpack_rows(small[None, cut:], [part.shape[1] for part in short])
    r_gain_one, r_gain_two, r_rel, r_bias = (
        part.reshape(shape)
        for part, shape in zip(
            tail, (gain_attn.shape, gain_ffn.shape, rel_bias.shape, router_bias.shape)
        )
    )
    return (
        outputs[0],
        grads[0],
        r_query,
        r_key,
        r_value,
        r_output,
        r_router,
        r_gain_one,
        r_gain_two,
        r_rel,
        r_bias,
        grad_in[None],
        grad_out[None],
    )


def solution(mesh):
    both = P(AXES)
    in_specs = (both,) * 14 + (P(), both)
    out_specs = (both,) * 13
    return jax.shard_map(body, mesh=mesh, in_specs=in_specs, out_specs=out_specs, check_vma=False)
```

```python
import functools
import jax
import jax.numpy as jnp
import numpy as np
from jax import lax
from jax.experimental import pallas as pl
from jax.experimental.pallas import tpu as pltpu
from jax.sharding import PartitionSpec as P

HEADS = 12
HEAD = 64
BUCKETS = 32
PAIR = 2 * HEAD
GROUP = 4
BLOCK = 128
LANES = 128
AXES = ("narrow", "wide")
MIB = 1024 * 1024

epsilon = 1e-06
f32 = jnp.float32
bf16 = jnp.bfloat16


def mm(a, b):
    return lax.dot_general(a, b, (((1,), (0,)), ((), ())), preferred_element_type=f32)


def mm_nt(a, b):
    return lax.dot_general(a, b, (((1,), (1,)), ((), ())), preferred_element_type=f32)


def mm_tn(a, b):
    return lax.dot_general(a, b, (((0,), (0,)), ((), ())), preferred_element_type=f32)


def norm_scale(values):
    return lax.rsqrt(jnp.mean(values * values, axis=-1, keepdims=True) + epsilon)


def softmax_rows(logits):
    shifted = jnp.exp(logits - jnp.max(logits, axis=-1, keepdims=True))
    return shifted / jnp.sum(shifted, axis=-1, keepdims=True)


def pair_mask(shape, half):
    lane = lax.broadcasted_iota(jnp.int32, shape, 1)
    return (lane < HEAD) if half == 0 else (lane >= HEAD)


def params(size):
    return pltpu.CompilerParams(vmem_limit_bytes=size * MIB)


def front_kernel(
    tokens_ref, wq_ref, wk_ref, wv_ref, wo_ref, skew_ref, gain_one_ref, gain_two_ref, spots_ref,
    q_ref, k_ref, v_ref, mixed_ref, lse_ref, sent_ref, normed_ref, resid_ref,
):
    step = pl.program_id(0)
    length, width = tokens_ref.shape

    @pl.when(step == 0)
    def start():
        acts = tokens_ref[...].astype(f32)
        normed_ref[...] = (acts * norm_scale(acts) * gain_one_ref[...]).astype(bf16)
        resid_ref[...] = acts

    normed = normed_ref[...]
    q_ref[...] = mm(normed, wq_ref[...]).astype(bf16)
    k_ref[...] = mm(normed, wk_ref[...]).astype(bf16)
    v_ref[...] = mm(normed, wv_ref[...]).astype(bf16)
    for pair in range(GROUP // 2):
        cols = slice(PAIR * pair, PAIR * (pair + 1))
        query, key, value = q_ref[:, cols], k_ref[:, cols], v_ref[:, cols]
        out = None
        for half in range(2):
            head = 2 * pair + half
            mask = pair_mask(query.shape, half)
            scores = mm_nt(jnp.where(mask, query, jnp.zeros_like(query)), key)
            parts = []
            for at in range(length // BLOCK):
                rows = slice(BLOCK * at, BLOCK * (at + 1))
                low = length - BLOCK * (at + 1)
                part = scores[rows, :] + skew_ref[head, :, low : low + length].astype(f32)
                peak = jnp.max(part, axis=-1, keepdims=True)
                part = jnp.exp(part - peak)
                total = jnp.sum(part, axis=-1, keepdims=True)
                lse_ref[0, rows, head : head + 1] = peak + jnp.log(total)
                parts.append((part * (1.0 / total)).astype(bf16))
            probs = jnp.concatenate(parts, axis=0)
            term = mm(probs, jnp.where(mask, value, jnp.zeros_like(value)))
            out = term if out is None else out + term
        mixed_ref[:, cols] = out.astype(bf16)
    resid_ref[...] += mm(mixed_ref[...], wo_ref[...])

    @pl.when(step == pl.num_programs(0) - 1)
    def finish():
        resid = resid_ref[...]
        normed_two = (resid * norm_scale(resid) * gain_two_ref[...]).astype(bf16)
        rows = lax.broadcasted_iota(jnp.int32, (sent_ref.shape[0], length), 0)
        left = mm((rows == spots_ref[0:1, :]).astype(bf16), normed_two[:, : width // 2])
        right = mm((rows == spots_ref[1:2, :]).astype(bf16), normed_two[:, width // 2 :])
        sent_ref[...] = (left + right).astype(bf16)


def one_in(at, length, width):
    return pl.BlockSpec((None, length, width), lambda *g: (at, 0, 0))


def front_call(at, tokens, wq, wk, wv, wo, skewed, gain_one, gain_two, spots, slots):
    length, width = tokens.shape[1:]
    part = GROUP * HEAD
    groups = HEADS // GROUP
    whole = lambda *shape: pl.BlockSpec(shape, lambda g: (0,) * len(shape))
    columns = lambda rows: pl.BlockSpec((rows, part), lambda g: (0, g))
    shape = jax.ShapeDtypeStruct
    return pl.pallas_call(
        front_kernel,
        grid=(groups,),
        in_specs=[
            one_in(at, length, width), columns(width), columns(width), columns(width),
            pl.BlockSpec((part, width), lambda g: (g, 0)),
            pl.BlockSpec((GROUP, BLOCK, skewed.shape[2]), lambda g: (g, 0, 0)),
            whole(1, width), whole(1, width), whole(2, length),
        ],
        out_specs=[
            columns(length), columns(length), columns(length), columns(length),
            pl.BlockSpec((1, length, GROUP), lambda g: (g, 0, 0)),
            whole(2 * slots, width // 2),
        ],
        out_shape=[
            *(4 * [shape((length, width), bf16)]), shape((groups, length, GROUP), f32),
            shape((2 * slots, width // 2), bf16),
        ],
        scratch_shapes=[pltpu.VMEM((length, width), bf16), pltpu.VMEM((length, width), f32)],
        compiler_params=params(60),
        cost_estimate=pl.CostEstimate(flops=1000000, bytes_accessed=MIB // 4, transcendentals=0),
        name="front",
    )(tokens, wq, wk, wv, wo, skewed, gain_one, gain_two, spots)


def bell(values):
    size = jnp.abs(values)
    t = 1.0 / (1.0 + (0.3275911 * 0.7071067811865476) * size)
    falling = jnp.exp(-0.5 * values * values)
    poly = t * (
        0.127414796
        + t * (-0.142248368 + t * (0.7107068705 + t * (-0.7265760135 + t * 0.5307027145)))
    )
    tail = poly * falling
    return jnp.where(values < 0, tail, 1.0 - tail), falling * 0.3989422804014327


def expert_kernel(
    mine_at, own_ref, arrived_ref, raw_ref, wr_ref, rbias_ref, place_ref, placed_ref, win_ref, wout_ref,
    sent_ref, rows_ref, active_ref, gradinner_ref, gradresult_ref, result_acc, rows_acc,
):
    step = pl.program_id(0)
    last = pl.num_programs(0) - 1
    count = rows_ref.shape[0]
    unit = place_ref.shape[0]

    @pl.when(step == 0)
    def start():
        half = arrived_ref.shape[1]
        ids = lax.broadcasted_iota(jnp.int32, (unit, 2 * unit), 1)
        for side in range(2):
            pick = (ids == place_ref[:, side : side + 1]).astype(bf16)
            for at in range(0, count, unit):
                rows_ref[at : at + unit, half * side : half * (side + 1)] = mm(
                    pick, arrived_ref[2 * at : 2 * (at + unit), :]
                ).astype(bf16)
        probs = softmax_rows(mm(rows_ref[...], wr_ref[...]) + rbias_ref[...])
        mine = lax.broadcasted_iota(jnp.int32, probs.shape, 1) == own_ref[0]
        gate = jnp.sum(jnp.where(mine, probs, 0.0), axis=-1, keepdims=True)
        pick = (ids == place_ref[:, mine_at : mine_at + 1]).astype(bf16)
        for at in range(0, count, unit):
            raw = mm(pick, raw_ref[2 * at : 2 * (at + unit), :])
            gradresult_ref[at : at + unit, :] = (gate[at : at + unit] * raw).astype(bf16)

    inner = mm(rows_ref[...], win_ref[...])
    grad_active = mm_nt(gradresult_ref[...], wout_ref[...])
    share, density = bell(inner)
    active = (inner * share).astype(bf16)
    grad_inner = (grad_active * (share + inner * density)).astype(bf16)
    active_ref[...] = active
    gradinner_ref[...] = grad_inner
    result = mm(active, wout_ref[...])
    grad_rows = mm_nt(grad_inner, win_ref[...])

    @pl.when(step == 0)
    def first():
        result_acc[...] = result
        rows_acc[...] = grad_rows

    @pl.when(step > 0)
    def more():
        result_acc[...] += result
        rows_acc[...] += grad_rows

    @pl.when(step == last)
    def finish():
        ids = lax.broadcasted_iota(jnp.int32, (2 * unit, unit), 0)
        picks = [(ids == placed_ref[side : side + 1, :]).astype(bf16) for side in range(2)]
        for at in range(0, count, unit):
            sent_ref[2 * at : 2 * (at + unit), :] = (
                mm(picks[0], result_acc[at : at + unit, :].astype(bf16))
                + mm(picks[1], rows_acc[at : at + unit, :].astype(bf16))
            ).astype(bf16)


def expert_call(mine_at, own, arrived, raw, wr, rbias, place, w_in, w_out, part=1024):
    count, width = raw.shape[0] // 2, raw.shape[1]
    hidden = w_in.shape[1]
    experts = wr.shape[1]
    whole = lambda *shape: pl.BlockSpec(shape, lambda g, own: (0,) * len(shape))
    columns = lambda n: pl.BlockSpec((n, part), lambda g, own: (0, g))
    return pl.pallas_call(
        functools.partial(expert_kernel, mine_at),
        grid_spec=pltpu.PrefetchScalarGridSpec(
            num_scalar_prefetch=1,
            grid=(hidden // part,),
            in_specs=[
                whole(2 * count, width // 2), whole(2 * count, width), whole(width, experts),
                whole(1, experts), whole(*place.shape), whole(*place.shape[::-1]),
                columns(width), pl.BlockSpec((part, width), lambda g, own: (g, 0)),
            ],
            out_specs=[
                whole(2 * count, width), whole(count, width), columns(count), columns(count),
                whole(count, width),
            ],
            scratch_shapes=[pltpu.VMEM((count, width), f32), pltpu.VMEM((count, width), f32)],
        ),
        out_shape=[
            jax.ShapeDtypeStruct((2 * count, width), bf16),
            jax.ShapeDtypeStruct((count, width), bf16),
            jax.ShapeDtypeStruct((count, hidden), bf16),
            jax.ShapeDtypeStruct((count, hidden), bf16),
            jax.ShapeDtypeStruct((count, width), bf16),
        ],
        compiler_params=params(60),
        cost_estimate=pl.CostEstimate(
            flops=8 * count * width * hidden, bytes_accessed=20 * MIB,
            transcendentals=count * hidden,
        ),
        name="expert",
    )(own, arrived, raw, wr, rbias, place, place.T, w_in, w_out)


def back_rows_kernel(
    target_ref, route_ref, returned_ref, up_ref, tokens_ref, mixed_ref, gain_ref, wr_ref,
    rbias_ref, wo_ref, *refs,
):
    output_ref, gradresid_ref, gradmixed_ref, go_ref, grw_ref, ggain_ref, gbias_ref = refs[-7:]
    length = up_ref.shape[0]
    experts = wr_ref.shape[1]
    mixed = mixed_ref[...]
    resid = tokens_ref[...].astype(f32) + mm(mixed, wo_ref[...])
    scale = norm_scale(resid)
    normed_two = (resid * scale * gain_ref[...]).astype(bf16)
    router = softmax_rows(mm(normed_two, wr_ref[...]) + rbias_ref[...])
    returned = returned_ref[...]
    ids = lax.broadcasted_iota(jnp.int32, (length, returned.shape[0]), 1)
    expert_rows = mm((ids == target_ref[:, 0:1]).astype(bf16), returned)
    grad_back = mm((ids == target_ref[:, 1:2]).astype(bf16), returned)
    up = up_ref[...].astype(f32)
    hot = lax.broadcasted_iota(jnp.int32, (length, experts), 1) == route_ref[...]
    gate = jnp.sum(jnp.where(hot, router, 0.0), axis=-1, keepdims=True)
    output_ref[0] = (resid + gate * expert_rows).astype(bf16)
    grad_gate = jnp.sum(up * expert_rows, axis=-1, keepdims=True)
    grad_logits = (router * (jnp.where(hot, grad_gate, 0.0) - gate * grad_gate)).astype(bf16)
    grad_normed = mm_nt(grad_logits, wr_ref[...]) + grad_back
    gbias = jnp.sum(grad_logits.astype(f32), axis=0, keepdims=True)
    grw = mm_tn(normed_two, grad_logits)
    ggain = jnp.sum(grad_normed * resid * scale, axis=0, keepdims=True)
    weighted = grad_normed * gain_ref[...]
    slope = scale * scale * scale * jnp.mean(weighted * resid, axis=-1, keepdims=True)
    grad_resid = up + (scale * weighted - resid * slope)
    gradresid_ref[...] = grad_resid
    grad_branch = grad_resid.astype(bf16)
    go = mm_tn(mixed, grad_branch)
    sums = [go, grw, ggain, gbias]
    if len(refs) > 7:
        sums = [one + prior[...].astype(f32) for one, prior in zip(sums, refs)]
    for ref, one in zip((go_ref, grw_ref, ggain_ref, gbias_ref), sums):
        ref[...] = one.astype(ref.dtype)
    gradmixed_ref[...] = mm_nt(grad_branch, wo_ref[...]).astype(bf16)


def one_of(count, at, length, width):
    spec = pl.BlockSpec((1, length, width), lambda *g: (at, 0, 0))
    return spec, jax.ShapeDtypeStruct((count, length, width), bf16)


def back_rows_call(
    at, count, target, route, returned, up, tokens, mixed, gain, wr, rbias, wo, prior, output
):
    length, width = up.shape[1:]
    experts = wr.shape[1]
    shape = jax.ShapeDtypeStruct
    spec, full = one_of(count, at, length, width)
    vmem = pl.BlockSpec(memory_space=pltpu.VMEM)
    inputs = 10 + len(prior)
    return pl.pallas_call(
        back_rows_kernel,
        grid=(1,),
        in_specs=[vmem] * 3
        + [one_in(at, length, width)] * 2
        + [vmem] * (inputs - 5)
        + [pl.BlockSpec(memory_space=pl.ANY)] * len(output),
        out_specs=[spec] + [vmem] * 6,
        input_output_aliases={inputs: 0} if output else {},
        out_shape=[
            full, shape((length, width), f32),
            shape((length, width), bf16), shape((width, width), bf16),
            shape((width, experts), f32), shape((1, width), f32), shape((1, experts), f32),
        ],
        compiler_params=params(60),
        cost_estimate=pl.CostEstimate(
            flops=2 * length * width * (3 * width + 2 * returned.shape[0]),
            bytes_accessed=12 * MIB, transcendentals=0,
        ),
        name="back_rows",
    )(
        target, route, returned, up, tokens, mixed, gain, wr, rbias, wo, *prior, *output
    )


def back_heads_kernel(
    tokens_ref, gain_ref, gradmixed_ref, mixed_ref, wq_ref, wk_ref, wv_ref, q_ref, k_ref, v_ref,
    skew_ref, lse_ref, gradresid_ref, *refs,
):
    prior_refs = refs[: (len(refs) - 7) // 3 * 3]
    line_ref, gw_ref, gradacts_ref, ggain_ref, normedt_ref, acc_ref, fold_ref = refs[-7:]
    step = pl.program_id(0)
    last = pl.num_programs(0) - 1
    length, width = tokens_ref.shape
    span = 2 * length

    @pl.when(step == 0)
    def start():
        acts = tokens_ref[...].astype(f32)
        normed = (acts * norm_scale(acts) * gain_ref[...]).astype(bf16)
        normedt_ref[...] = normed.T
        acc_ref[...] = jnp.zeros_like(acc_ref)

    dq, dk, dv = [], [], []
    for pair in range(GROUP // 2):
        cols = slice(PAIR * pair, PAIR * (pair + 1))
        query, key, value = q_ref[:, cols], k_ref[:, cols], v_ref[:, cols]
        grad = gradmixed_ref[:, cols]
        product = grad.astype(f32) * mixed_ref[:, cols].astype(f32)
        gq = gk = gv = None
        for half in range(2):
            head = 2 * pair + half
            mask = pair_mask(query.shape, half)
            clear = lambda a: jnp.where(mask, a, jnp.zeros_like(a))
            own, asked = clear(grad), clear(query)
            center = jnp.sum(clear(product), axis=-1, keepdims=True)
            scores = mm_nt(asked, key)
            grad_probs = mm_nt(own, value)
            all_probs, all_grads = [], []
            for at in range(length // BLOCK):
                rows = slice(BLOCK * at, BLOCK * (at + 1))
                low = length - BLOCK * (at + 1)
                part = scores[rows, :] + skew_ref[head, :, low : low + length].astype(f32)
                probs = jnp.exp(part - lse_ref[0, rows, head : head + 1])
                piece = probs * (grad_probs[rows, :] - center[rows, :])
                if at == 0:
                    fold_ref[:, :low] = jnp.zeros((BLOCK, low), f32)
                    fold_ref[:, low : low + length] = piece
                    fold_ref[:, low + length :] = jnp.zeros((BLOCK, length - low), f32)
                else:
                    fold_ref[:, low : low + length] += piece
                all_probs.append(probs.astype(bf16))
                all_grads.append(piece.astype(bf16))
            rows = fold_ref[...]
            size = BLOCK
            while size > 1:
                size //= 2
                rows = rows[:size] + pltpu.roll(rows[size:], span - size, 1)
            line = pltpu.roll(rows, BLOCK - 1, 1)
            if prior_refs:
                line = line + prior_refs[1][0, head : head + 1, :]
            line_ref[0, head : head + 1, :] = line
            probs = jnp.concatenate(all_probs, axis=0)
            grad_scores = jnp.concatenate(all_grads, axis=0)
            a = mm(grad_scores, clear(key))
            b = mm(asked.T, grad_scores)
            c = mm(own.T, probs)
            gq = a if gq is None else gq + a
            gk = b if gk is None else gk + b
            gv = c if gv is None else gv + c
        dq.append(gq.astype(bf16))
        dk.append(gk.T.astype(bf16))
        dv.append(gv.T.astype(bf16))
    dq, dk, dv = (jnp.concatenate(x, axis=1) for x in (dq, dk, dv))
    normedt = normedt_ref[...]
    for i, grad in enumerate((dq, dk, dv)):
        total = mm(normedt, grad)
        if prior_refs:
            total = total + prior_refs[0][i].astype(f32)
        gw_ref[i] = total.astype(bf16)
    acc_ref[...] += mm_nt(dq, wq_ref[...]) + mm_nt(dk, wk_ref[...]) + mm_nt(dv, wv_ref[...])

    @pl.when(step == last)
    def finish():
        grad_normed = acc_ref[...]
        acts = tokens_ref[...].astype(f32)
        scale = norm_scale(acts)
        ggain = jnp.sum(grad_normed * acts * scale, axis=0, keepdims=True)
        if prior_refs:
            ggain = ggain + prior_refs[2][...]
        ggain_ref[...] = ggain
        weighted = grad_normed * gain_ref[...]
        slope = scale * scale * scale * jnp.mean(weighted * acts, axis=-1, keepdims=True)
        grad_acts = gradresid_ref[...] + (scale * weighted - acts * slope)
        gradacts_ref[0] = grad_acts.astype(bf16)


def back_heads_call(
    at, count, tokens, gain, grad_mixed, mixed, wq, wk, wv, q, k, v, skewed, lse, grad_resid,
    prior, grads,
):
    length, width = tokens.shape[1:]
    part = GROUP * HEAD
    groups = HEADS // GROUP
    whole = lambda *shape: pl.BlockSpec(shape, lambda g: (0,) * len(shape))
    columns = lambda size: pl.BlockSpec((size, part), lambda g: (0, g))
    shape = jax.ShapeDtypeStruct
    spec, full = one_of(count, at, length, width)
    weights = pl.BlockSpec((3, width, part), lambda g: (0, 0, g))
    lines = pl.BlockSpec((1, GROUP, 2 * length), lambda g: (g, 0, 0))
    return pl.pallas_call(
        back_heads_kernel,
        grid=(groups,),
        in_specs=[
            one_in(at, length, width), whole(1, width), columns(length), columns(length),
            columns(width), columns(width), columns(width),
            columns(length), columns(length), columns(length),
            pl.BlockSpec((GROUP, BLOCK, skewed.shape[2]), lambda g: (g, 0, 0)),
            pl.BlockSpec((1, length, GROUP), lambda g: (g, 0, 0)), whole(length, width),
            *([weights, lines, whole(1, width)] if prior else []),
            *([pl.BlockSpec(memory_space=pl.ANY)] * len(grads)),
        ],
        out_specs=[
            lines, weights,
            spec, whole(1, width),
        ],
        input_output_aliases={13 + len(prior): 2} if grads else {},
        out_shape=[
            shape((groups, GROUP, 2 * length), f32), shape((3, width, width), bf16),
            full, shape((1, width), f32),
        ],
        scratch_shapes=[
            pltpu.VMEM((width, length), bf16), pltpu.VMEM((length, width), f32),
            pltpu.VMEM((BLOCK, 2 * length), f32),
        ],
        compiler_params=params(60),
        cost_estimate=pl.CostEstimate(
            flops=groups * (2 * length * width * part * 6 + 8 * length * length * part * 4),
            bytes_accessed=21 * MIB, transcendentals=HEADS * length * length,
        ),
        name="back_heads",
    )(
        tokens, gain, grad_mixed, mixed, wq, wk, wv, q, k, v, skewed, lse, grad_resid,
        *prior, *grads,
    )


def pack_kernel(*refs):
    for at, ref in enumerate(refs[:-1]):
        refs[-1][at] = ref[...]


def pack_call(*parts):
    return pl.pallas_call(
        pack_kernel,
        out_shape=jax.ShapeDtypeStruct((len(parts), *parts[0].shape), parts[0].dtype),
        compiler_params=params(60),
        name="pack",
    )(*parts)


def skew_kernel(lines_ref, out_ref):
    heads, block, span = out_ref.shape
    full = lines_ref.shape[1]
    for head in range(heads):
        row = jnp.broadcast_to(lines_ref[head : head + 1, :], (16, full))
        base = pltpu.roll(row, full - (block - 1), 1, stride=1, stride_axis=0)
        for at in range(0, block, 16):
            turned = base if at == 0 else pltpu.roll(base, at, 1)
            out_ref[head, at : at + 16, :] = turned[:, :span].astype(bf16)


def skew_call(lines, block):
    heads, span = lines.shape
    return pl.pallas_call(
        skew_kernel,
        out_shape=jax.ShapeDtypeStruct((heads, block, span - block), bf16),
        compiler_params=params(16),
        name="skew",
    )(lines)


def exchange(buffer):
    return lax.all_to_all(buffer, AXES, split_axis=0, concat_axis=0, tiled=True)


def swap(value, bit):
    devices = lax.axis_size(AXES)
    return lax.ppermute(value, AXES, [(at, at ^ (1 << bit)) for at in range(devices)])


def own_bit(bit):
    return ((lax.axis_index(AXES) >> bit) & 1) == 1


def gather_step(held, bit):
    value, done = held
    theirs = swap(value, bit)
    upper = own_bit(bit)
    place = sum(1 for other in done if other > bit)
    value = jnp.stack(
        [jnp.where(upper, theirs, value), jnp.where(upper, value, theirs)], axis=place
    )
    return value, done + [bit]


def gather_all(value, order):
    held = (value, [])
    for bit in order:
        held = gather_step(held, bit)
    return held[0].reshape((-1,) + value.shape)


def halves(value, left, bit):
    place = 1 + left.index(bit)
    low = lax.index_in_dim(value, 0, place, keepdims=False)
    high = lax.index_in_dim(value, 1, place, keepdims=False)
    upper = own_bit(bit)
    return jnp.where(upper, low, high).astype(bf16), jnp.where(upper, high, low).astype(f32)


def scatter_step(held, bit):
    value, left = held
    sent, kept = halves(value, left, bit)
    value = kept + swap(sent, bit).astype(f32)
    return value, [other for other in left if other != bit]


def pack_rows(parts, width):
    lead = parts[0].shape[0]
    flat = jnp.concatenate([part.reshape(lead, -1) for part in parts], axis=1)
    short = -flat.shape[1] % width
    return jnp.pad(flat, ((0, 0), (0, short))).reshape(lead, -1, width)


def unpack_rows(packed, sizes):
    flat = packed.reshape(packed.shape[0], -1)
    out, at = [], 0
    for size in sizes:
        out.append(flat[:, at : at + size])
        at += size
    return out


def tiles_of(shard, experts):
    return -(-shard // 8), -(-experts // LANES) * LANES


def small_slab(router, short, width):
    lead, shard, experts = router.shape
    tall, lanes = tiles_of(shard, experts)
    router = jnp.pad(router, ((0, 0), (0, 8 * tall - shard), (0, lanes - experts)))
    parts = [router[:, 8 * at : 8 * at + 8] for at in range(tall)]
    parts.append(pack_rows(short, 8 * LANES).reshape(lead, 8, LANES))
    slab = jnp.concatenate(parts, axis=2)
    return jnp.pad(slab, ((0, 0), (0, 0), (0, width - slab.shape[2])))


def slab_parts(slab, shard, experts, sizes):
    tall, lanes = tiles_of(shard, experts)
    parts = [slab[:, :, lanes * at : lanes * at + experts] for at in range(tall)]
    short = slab[:, :, lanes * tall : lanes * tall + LANES]
    return jnp.concatenate(parts, axis=1)[:, :shard], unpack_rows(short, sizes)


def body(
    tokens,
    w_query,
    w_key,
    w_value,
    w_output,
    w_router,
    gain_attn,
    gain_ffn,
    rel_bias,
    router_bias,
    w_in,
    w_out,
    routes,
    fill_rank,
    bucket_map,
    upstream_grad,
):
    batches, length, width = tokens.shape
    devices = lax.axis_size(AXES)
    wide_bits = lax.axis_size("wide").bit_length() - 1
    bits = devices.bit_length() - 1
    local_experts = w_in.shape[0]
    experts = local_experts * devices
    capacity = max(2, 5 * length // (4 * experts))
    slots = experts * capacity
    span = 2 * length
    shard = w_query.shape[0]
    far = list(range(wide_bits, bits))
    near = list(range(1, wide_bits))
    turned = near[1:] + near[:1]

    expert_ids = jnp.arange(experts, dtype=jnp.int32)

    def plan(route, order):
        route_hot = (route[:, None] == expert_ids[None, :]).astype(f32)
        earlier = (order[None, :] < order[:, None]).astype(bf16)
        counts = jnp.dot(earlier, route_hot.astype(bf16), preferred_element_type=f32)
        slot = jnp.sum(counts * route_hot, axis=-1).astype(jnp.int32)
        first = jnp.where(slot < capacity, route * (2 * capacity) + slot, -1)
        second = jnp.where(first >= 0, first + capacity, -1)
        return jnp.stack([first, second], axis=0)

    short = [gain_attn, gain_ffn, rel_bias, router_bias]
    packed, short_router, *short = lax.optimization_barrier(
        (pack_call(w_query, w_key, w_value, w_output), w_router, *short)
    )
    sizes = [part.size for part in short]
    slab = small_slab(short_router[None], [part[None] for part in short], width)
    square, small = (packed, []), (slab[0], [])
    for bit in far[::-1]:
        square, small = gather_step(square, bit), gather_step(small, bit)
    spots = [plan(routes[at, :, 0], fill_rank[at]) for at in range(batches)]
    raw_spots = jnp.concatenate([spots[at][at] for at in range(batches)], axis=0)
    raw_ids = jnp.arange(2 * slots, dtype=jnp.int32)
    raw_sent = jnp.dot(
        (raw_ids[:, None] == raw_spots[None, :]).astype(bf16),
        upstream_grad.reshape(batches * length, width),
        preferred_element_type=f32,
    ).astype(bf16)
    value, small, raw_sent = lax.optimization_barrier((square[0], small[0], raw_sent))
    done = far[::-1]
    value = value.reshape((2,) * len(far) + (4, shard, width))
    value = [lax.index_in_dim(value, i, len(far), keepdims=False) for i in range(4)]
    low = (jnp.concatenate(value[:2] + [small], axis=-2), done)
    high = (jnp.concatenate(value[2:], axis=-2), done)
    for number, (one, two) in enumerate(zip(near[::-1], turned[::-1])):
        low, high = gather_step(low, one), gather_step(high, two)
        if number == 0:
            first, second, raw_sent = lax.optimization_barrier((low[0], high[0], raw_sent))
            low, high = (first, low[1]), (second, high[1])

    raw_arrived = exchange(raw_sent.reshape(devices, 2 * capacity, width))

    first, second = lax.optimization_barrier((low[0], high[0]))
    low, high = gather_step((first, low[1]), 0), gather_step((second, high[1]), 0)
    low, high = (part[0].reshape(devices, -1, width) for part in (low, high))
    wq, wk, wv, wo = (
        part[:, i * shard : (i + 1) * shard].reshape(width, width)
        for part in (low, high)
        for i in range(2)
    )
    wr_all, (gain_one, gain_two, rel_flat, bias_all) = slab_parts(
        low[:, 2 * shard :], shard, experts, sizes
    )
    wr_all = wr_all.reshape(width, experts)
    gain_one = gain_one.reshape(1, width).astype(f32)
    gain_two = gain_two.reshape(1, width).astype(f32)
    bias_all = bias_all.reshape(1, experts).astype(f32)
    table = rel_flat.reshape(BUCKETS, HEADS).T
    bucket_hot = (
        jnp.arange(BUCKETS, dtype=jnp.int32)[:, None]
        == jnp.pad(bucket_map, (0, 1), constant_values=-1)[None, :]
    ).astype(bf16)
    skewed = skew_call(jnp.dot(table, bucket_hot, preferred_element_type=f32), BLOCK)
    own = lax.axis_index(AXES).astype(jnp.int32).reshape(1)
    count = 8 if 8 * capacity % 16 == 0 else 16
    row = np.arange(count * capacity, dtype=np.int32)
    row = row + (row // capacity) * capacity
    place = jnp.asarray(np.stack([row, row + capacity], axis=1))
    fronts, arrived, returned = [], [], []
    acts = tokens
    for at in range(batches):
        if at == 1:
            targets = [(spots[i].T, routes[i]) for i in range(batches)]
            acts, raw_arrived, targets, place, wr_all, bias_all = lax.optimization_barrier(
                (acts, raw_arrived, targets, place, wr_all, bias_all)
            )
        front = front_call(
            at, acts, wq, wk, wv, wo, skewed, gain_one, gain_two, spots[at], slots
        )
        fronts.append(front)
        arrived.append(exchange(front[-1].reshape(devices, 2 * capacity, width // 2)))
    grad_in = grad_out = 0.0
    for at in range(batches):
        sent, rows, active, grad_inner, grad_result = expert_call(
            at,
            own,
            arrived[at].reshape(2 * slots, width // 2),
            raw_arrived.reshape(2 * slots, width),
            wr_all,
            bias_all,
            place,
            w_in[0],
            w_out[0],
        )
        if at == batches - 1:
            sent, grad_in, grad_out = lax.optimization_barrier((sent, grad_in, grad_out))
        grad_in += jnp.einsum("rd,rf->df", rows, grad_inner, preferred_element_type=f32)
        grad_out += jnp.einsum("rf,rd->fd", active, grad_result, preferred_element_type=f32)
        back = exchange(sent.reshape(devices, 2 * capacity, width))
        back, grad_in, grad_out = lax.optimization_barrier((back, grad_in, grad_out))
        returned.append(back)

    row_prior, head_prior, outputs, grads = [], [], [], []
    for at in range(batches):
        q, k, v, mixed, lse, sent = fronts[at]
        row_part = back_rows_call(
            at, batches, *targets[at], returned[at].reshape(2 * slots, width), upstream_grad,
            tokens, mixed, gain_two, wr_all, bias_all, wo, row_prior,
            outputs,
        )
        outputs = row_part[:1]
        row_prior = row_part[3:]
        head_part = back_heads_call(
            at, batches, tokens, gain_one, row_part[2], mixed, wq, wk, wv, q, k, v, skewed, lse,
            row_part[1], head_prior, grads,
        )
        grads = head_part[2:3]
        head_prior = [head_part[1], head_part[0], head_part[3]]

    g_output, g_router, g_gain_two, g_bias = row_prior
    g_heads, lines, g_gain_one = head_prior
    def halved(parts):
        value = jnp.concatenate([part.astype(bf16) for part in parts], axis=1)
        value = value.reshape((1,) + (2,) * bits + value.shape[1:])
        return scatter_step((value, list(range(bits))[::-1]), 0)

    outer = halved([g_output.reshape(devices, shard, width)])
    g_heads = g_heads.reshape(3, devices, shard, width)
    inner = halved(list(g_heads))
    cut = 2 * shard
    low = (inner[0][..., :cut, :], inner[1])
    high = (jnp.concatenate([inner[0][..., cut:, :], outer[0]], axis=-2), inner[1])
    for number, (one, two) in enumerate(zip(near, turned)):
        low, high = scatter_step(low, one), scatter_step(high, two)
        if number == 0:
            first, second, g_router, g_gain_two, g_bias, lines, g_gain_one = (
                lax.optimization_barrier(
                    (low[0], high[0], g_router, g_gain_two, g_bias, lines, g_gain_one)
                )
            )
            low, high = (first, low[1]), (second, high[1])
            g_rel = jnp.einsum(
                "hn,bn->bh",
                lines.reshape(HEADS, span),
                bucket_hot.astype(f32),
                precision=lax.Precision.HIGHEST,
            )
            short = [
                part.reshape(devices, -1) for part in (g_gain_one, g_gain_two, g_rel, g_bias)
            ]
            short_pack = pack_rows(short, 8 * LANES).reshape(devices, -1, LANES).astype(bf16)
            lanes = -(-experts // LANES) * LANES
            router_pack = jnp.pad(g_router.astype(bf16), ((0, 0), (0, lanes - experts)))
            router_pack = router_pack.reshape(devices, -1, LANES)
            small = jnp.concatenate([router_pack, short_pack], axis=1)
            small = exchange(small)
    held = (jnp.concatenate([low[0], high[0]], axis=-2), low[1])
    for bit in far[:-1]:
        held = scatter_step(held, bit)
    value, left = held
    sent, value = halves(value, left, far[-1])
    theirs = swap(sent, far[-1])
    theirs, small = lax.optimization_barrier((theirs, small))
    total = (value + theirs.astype(f32))[0]
    small = jnp.sum(small.astype(f32), axis=0)
    r_query, r_key, r_value, r_output = jnp.split(
        total, [shard, 2 * shard, 3 * shard], axis=0
    )
    cut = router_pack.shape[1]
    r_router = small[:cut].reshape(shard, lanes)[:, :experts]
    tail = unpack_rows(small[None, cut:], [part.shape[1] for part in short])
    r_gain_one, r_gain_two, r_rel, r_bias = (
        part.reshape(shape)
        for part, shape in zip(
            tail, (gain_attn.shape, gain_ffn.shape, rel_bias.shape, router_bias.shape)
        )
    )
    return (
        outputs[0],
        grads[0],
        r_query,
        r_key,
        r_value,
        r_output,
        r_router,
        r_gain_one,
        r_gain_two,
        r_rel,
        r_bias,
        grad_in[None],
        grad_out[None],
    )


def solution(mesh):
    both = P(AXES)
    in_specs = (both,) * 14 + (P(), both)
    out_specs = (both,) * 13
    return jax.shard_map(body, mesh=mesh, in_specs=in_specs, out_specs=out_specs, check_vma=False)
```

```python
import functools
import jax
import jax.numpy as jnp
import numpy as np
from jax import lax
from jax.experimental import pallas as pl
from jax.experimental.pallas import tpu as pltpu
from jax.sharding import PartitionSpec as P

HEADS = 12
HEAD = 64
BUCKETS = 32
PAIR = 2 * HEAD
GROUP = 4
BLOCK = 128
LANES = 128
AXES = ("narrow", "wide")
MIB = 1024 * 1024

epsilon = 1e-06
f32 = jnp.float32
bf16 = jnp.bfloat16


def mm(a, b):
    return lax.dot_general(a, b, (((1,), (0,)), ((), ())), preferred_element_type=f32)


def mm_nt(a, b):
    return lax.dot_general(a, b, (((1,), (1,)), ((), ())), preferred_element_type=f32)


def mm_tn(a, b):
    return lax.dot_general(a, b, (((0,), (0,)), ((), ())), preferred_element_type=f32)


def norm_scale(values):
    return lax.rsqrt(jnp.mean(values * values, axis=-1, keepdims=True) + epsilon)


def softmax_rows(logits):
    shifted = jnp.exp(logits - jnp.max(logits, axis=-1, keepdims=True))
    return shifted / jnp.sum(shifted, axis=-1, keepdims=True)


def pair_mask(shape, half):
    lane = lax.broadcasted_iota(jnp.int32, shape, 1)
    return (lane < HEAD) if half == 0 else (lane >= HEAD)


def params(size):
    return pltpu.CompilerParams(vmem_limit_bytes=size * MIB)


def front_kernel(
    tokens_ref, wq_ref, wk_ref, wv_ref, wo_ref, skew_ref, gain_one_ref, gain_two_ref, spots_ref,
    q_ref, k_ref, v_ref, mixed_ref, lse_ref, sent_ref, normed_ref, resid_ref,
):
    step = pl.program_id(0)
    length, width = tokens_ref.shape

    @pl.when(step == 0)
    def start():
        acts = tokens_ref[...].astype(f32)
        normed_ref[...] = (acts * norm_scale(acts) * gain_one_ref[...]).astype(bf16)
        resid_ref[...] = acts

    normed = normed_ref[...]
    q_ref[...] = mm(normed, wq_ref[...]).astype(bf16)
    k_ref[...] = mm(normed, wk_ref[...]).astype(bf16)
    v_ref[...] = mm(normed, wv_ref[...]).astype(bf16)
    for pair in range(GROUP // 2):
        cols = slice(PAIR * pair, PAIR * (pair + 1))
        query, key, value = q_ref[:, cols], k_ref[:, cols], v_ref[:, cols]
        out = None
        for half in range(2):
            head = 2 * pair + half
            mask = pair_mask(query.shape, half)
            scores = mm_nt(jnp.where(mask, query, jnp.zeros_like(query)), key)
            parts = []
            for at in range(length // BLOCK):
                rows = slice(BLOCK * at, BLOCK * (at + 1))
                low = length - BLOCK * (at + 1)
                part = scores[rows, :] + skew_ref[head, :, low : low + length].astype(f32)
                peak = jnp.max(part, axis=-1, keepdims=True)
                part = jnp.exp(part - peak)
                total = jnp.sum(part, axis=-1, keepdims=True)
                lse_ref[0, rows, head : head + 1] = peak + jnp.log(total)
                parts.append((part * (1.0 / total)).astype(bf16))
            probs = jnp.concatenate(parts, axis=0)
            term = mm(probs, jnp.where(mask, value, jnp.zeros_like(value)))
            out = term if out is None else out + term
        mixed_ref[:, cols] = out.astype(bf16)
    resid_ref[...] += mm(mixed_ref[...], wo_ref[...])

    @pl.when(step == pl.num_programs(0) - 1)
    def finish():
        resid = resid_ref[...]
        normed_two = (resid * norm_scale(resid) * gain_two_ref[...]).astype(bf16)
        rows = lax.broadcasted_iota(jnp.int32, (sent_ref.shape[0], length), 0)
        left = mm((rows == spots_ref[0:1, :]).astype(bf16), normed_two[:, : width // 2])
        right = mm((rows == spots_ref[1:2, :]).astype(bf16), normed_two[:, width // 2 :])
        sent_ref[...] = (left + right).astype(bf16)


def one_in(at, length, width):
    return pl.BlockSpec((None, length, width), lambda *g: (at, 0, 0))


def front_call(at, tokens, wq, wk, wv, wo, skewed, gain_one, gain_two, spots, slots):
    length, width = tokens.shape[1:]
    part = GROUP * HEAD
    groups = HEADS // GROUP
    whole = lambda *shape: pl.BlockSpec(shape, lambda g: (0,) * len(shape))
    columns = lambda rows: pl.BlockSpec((rows, part), lambda g: (0, g))
    shape = jax.ShapeDtypeStruct
    return pl.pallas_call(
        front_kernel,
        grid=(groups,),
        in_specs=[
            one_in(at, length, width), columns(width), columns(width), columns(width),
            pl.BlockSpec((part, width), lambda g: (g, 0)),
            pl.BlockSpec((GROUP, BLOCK, skewed.shape[2]), lambda g: (g, 0, 0)),
            whole(1, width), whole(1, width), whole(2, length),
        ],
        out_specs=[
            columns(length), columns(length), columns(length), columns(length),
            pl.BlockSpec((1, length, GROUP), lambda g: (g, 0, 0)),
            whole(2 * slots, width // 2),
        ],
        out_shape=[
            *(4 * [shape((length, width), bf16)]), shape((groups, length, GROUP), f32),
            shape((2 * slots, width // 2), bf16),
        ],
        scratch_shapes=[pltpu.VMEM((length, width), bf16), pltpu.VMEM((length, width), f32)],
        compiler_params=params(60),
        cost_estimate=pl.CostEstimate(flops=1000000, bytes_accessed=MIB // 4, transcendentals=0),
        name="front",
    )(tokens, wq, wk, wv, wo, skewed, gain_one, gain_two, spots)


def bell(values):
    size = jnp.abs(values)
    t = 1.0 / (1.0 + (0.3275911 * 0.7071067811865476) * size)
    falling = jnp.exp(-0.5 * values * values)
    poly = t * (
        0.127414796
        + t * (-0.142248368 + t * (0.7107068705 + t * (-0.7265760135 + t * 0.5307027145)))
    )
    tail = poly * falling
    return jnp.where(values < 0, tail, 1.0 - tail), falling * 0.3989422804014327


def expert_kernel(
    mine_at, own_ref, arrived_ref, raw_ref, wr_ref, rbias_ref, place_ref, placed_ref, win_ref, wout_ref,
    sent_ref, rows_ref, active_ref, gradinner_ref, gradresult_ref, result_acc, rows_acc,
):
    step = pl.program_id(0)
    last = pl.num_programs(0) - 1
    count = rows_ref.shape[0]
    unit = place_ref.shape[0]

    @pl.when(step == 0)
    def start():
        half = arrived_ref.shape[1]
        ids = lax.broadcasted_iota(jnp.int32, (unit, 2 * unit), 1)
        for side in range(2):
            pick = (ids == place_ref[:, side : side + 1]).astype(bf16)
            for at in range(0, count, unit):
                rows_ref[at : at + unit, half * side : half * (side + 1)] = mm(
                    pick, arrived_ref[2 * at : 2 * (at + unit), :]
                ).astype(bf16)
        probs = softmax_rows(mm(rows_ref[...], wr_ref[...]) + rbias_ref[...])
        mine = lax.broadcasted_iota(jnp.int32, probs.shape, 1) == own_ref[0]
        gate = jnp.sum(jnp.where(mine, probs, 0.0), axis=-1, keepdims=True)
        pick = (ids == place_ref[:, mine_at : mine_at + 1]).astype(bf16)
        for at in range(0, count, unit):
            raw = mm(pick, raw_ref[2 * at : 2 * (at + unit), :])
            gradresult_ref[at : at + unit, :] = (gate[at : at + unit] * raw).astype(bf16)

    inner = mm(rows_ref[...], win_ref[...])
    grad_active = mm_nt(gradresult_ref[...], wout_ref[...])
    share, density = bell(inner)
    active = (inner * share).astype(bf16)
    grad_inner = (grad_active * (share + inner * density)).astype(bf16)
    active_ref[...] = active
    gradinner_ref[...] = grad_inner
    result = mm(active, wout_ref[...])
    grad_rows = mm_nt(grad_inner, win_ref[...])

    @pl.when(step == 0)
    def first():
        result_acc[...] = result
        rows_acc[...] = grad_rows

    @pl.when(step > 0)
    def more():
        result_acc[...] += result
        rows_acc[...] += grad_rows

    @pl.when(step == last)
    def finish():
        ids = lax.broadcasted_iota(jnp.int32, (2 * unit, unit), 0)
        picks = [(ids == placed_ref[side : side + 1, :]).astype(bf16) for side in range(2)]
        for at in range(0, count, unit):
            sent_ref[2 * at : 2 * (at + unit), :] = (
                mm(picks[0], result_acc[at : at + unit, :].astype(bf16))
                + mm(picks[1], rows_acc[at : at + unit, :].astype(bf16))
            ).astype(bf16)


def expert_call(mine_at, own, arrived, raw, wr, rbias, place, w_in, w_out, part=1024):
    count, width = raw.shape[0] // 2, raw.shape[1]
    hidden = w_in.shape[1]
    experts = wr.shape[1]
    whole = lambda *shape: pl.BlockSpec(shape, lambda g, own: (0,) * len(shape))
    columns = lambda n: pl.BlockSpec((n, part), lambda g, own: (0, g))
    return pl.pallas_call(
        functools.partial(expert_kernel, mine_at),
        grid_spec=pltpu.PrefetchScalarGridSpec(
            num_scalar_prefetch=1,
            grid=(hidden // part,),
            in_specs=[
                whole(2 * count, width // 2), whole(2 * count, width), whole(width, experts),
                whole(1, experts), whole(*place.shape), whole(*place.shape[::-1]),
                columns(width), pl.BlockSpec((part, width), lambda g, own: (g, 0)),
            ],
            out_specs=[
                whole(2 * count, width), whole(count, width), columns(count), columns(count),
                whole(count, width),
            ],
            scratch_shapes=[pltpu.VMEM((count, width), f32), pltpu.VMEM((count, width), f32)],
        ),
        out_shape=[
            jax.ShapeDtypeStruct((2 * count, width), bf16),
            jax.ShapeDtypeStruct((count, width), bf16),
            jax.ShapeDtypeStruct((count, hidden), bf16),
            jax.ShapeDtypeStruct((count, hidden), bf16),
            jax.ShapeDtypeStruct((count, width), bf16),
        ],
        compiler_params=params(60),
        cost_estimate=pl.CostEstimate(
            flops=8 * count * width * hidden, bytes_accessed=20 * MIB,
            transcendentals=count * hidden,
        ),
        name="expert",
    )(own, arrived, raw, wr, rbias, place, place.T, w_in, w_out)


def back_rows_kernel(
    target_ref, route_ref, returned_ref, up_ref, tokens_ref, mixed_ref, gain_ref, wr_ref,
    rbias_ref, wo_ref, *refs,
):
    output_ref, gradresid_ref, gradmixed_ref, go_ref, grw_ref, ggain_ref, gbias_ref = refs[-7:]
    length = up_ref.shape[0]
    experts = wr_ref.shape[1]
    mixed = mixed_ref[...]
    resid = tokens_ref[...].astype(f32) + mm(mixed, wo_ref[...])
    scale = norm_scale(resid)
    normed_two = (resid * scale * gain_ref[...]).astype(bf16)
    router = softmax_rows(mm(normed_two, wr_ref[...]) + rbias_ref[...])
    returned = returned_ref[...]
    ids = lax.broadcasted_iota(jnp.int32, (length, returned.shape[0]), 1)
    expert_rows = mm((ids == target_ref[:, 0:1]).astype(bf16), returned)
    grad_back = mm((ids == target_ref[:, 1:2]).astype(bf16), returned)
    up = up_ref[...].astype(f32)
    hot = lax.broadcasted_iota(jnp.int32, (length, experts), 1) == route_ref[...]
    gate = jnp.sum(jnp.where(hot, router, 0.0), axis=-1, keepdims=True)
    output_ref[0] = (resid + gate * expert_rows).astype(bf16)
    grad_gate = jnp.sum(up * expert_rows, axis=-1, keepdims=True)
    grad_logits = (router * (jnp.where(hot, grad_gate, 0.0) - gate * grad_gate)).astype(bf16)
    grad_normed = mm_nt(grad_logits, wr_ref[...]) + grad_back
    gbias = jnp.sum(grad_logits.astype(f32), axis=0, keepdims=True)
    grw = mm_tn(normed_two, grad_logits)
    ggain = jnp.sum(grad_normed * resid * scale, axis=0, keepdims=True)
    weighted = grad_normed * gain_ref[...]
    slope = scale * scale * scale * jnp.mean(weighted * resid, axis=-1, keepdims=True)
    grad_resid = up + (scale * weighted - resid * slope)
    gradresid_ref[...] = grad_resid
    grad_branch = grad_resid.astype(bf16)
    go = mm_tn(mixed, grad_branch)
    sums = [go, grw, ggain, gbias]
    if len(refs) > 7:
        sums = [one + prior[...].astype(f32) for one, prior in zip(sums, refs)]
    for ref, one in zip((go_ref, grw_ref, ggain_ref, gbias_ref), sums):
        ref[...] = one.astype(ref.dtype)
    gradmixed_ref[...] = mm_nt(grad_branch, wo_ref[...]).astype(bf16)


def one_of(count, at, length, width):
    spec = pl.BlockSpec((1, length, width), lambda *g: (at, 0, 0))
    return spec, jax.ShapeDtypeStruct((count, length, width), bf16)


def back_rows_call(
    at, count, target, route, returned, up, tokens, mixed, gain, wr, rbias, wo, prior, output
):
    length, width = up.shape[1:]
    experts = wr.shape[1]
    shape = jax.ShapeDtypeStruct
    spec, full = one_of(count, at, length, width)
    vmem = pl.BlockSpec(memory_space=pltpu.VMEM)
    inputs = 10 + len(prior)
    return pl.pallas_call(
        back_rows_kernel,
        grid=(1,),
        in_specs=[vmem] * 3
        + [one_in(at, length, width)] * 2
        + [vmem] * (inputs - 5)
        + [pl.BlockSpec(memory_space=pl.ANY)] * len(output),
        out_specs=[spec] + [vmem] * 6,
        input_output_aliases={inputs: 0} if output else {},
        out_shape=[
            full, shape((length, width), f32),
            shape((length, width), bf16), shape((width, width), bf16),
            shape((width, experts), f32), shape((1, width), f32), shape((1, experts), f32),
        ],
        compiler_params=params(44),
        cost_estimate=pl.CostEstimate(
            flops=2 * length * width * (3 * width + 2 * returned.shape[0]),
            bytes_accessed=12 * MIB, transcendentals=0,
        ),
        name="back_rows",
    )(
        target, route, returned, up, tokens, mixed, gain, wr, rbias, wo, *prior, *output
    )


def back_heads_kernel(
    tokens_ref, gain_ref, gradmixed_ref, mixed_ref, wq_ref, wk_ref, wv_ref, q_ref, k_ref, v_ref,
    skew_ref, lse_ref, gradresid_ref, *refs,
):
    prior_refs = refs[: (len(refs) - 7) // 3 * 3]
    line_ref, gw_ref, gradacts_ref, ggain_ref, normedt_ref, acc_ref, fold_ref = refs[-7:]
    step = pl.program_id(0)
    last = pl.num_programs(0) - 1
    length, width = tokens_ref.shape
    span = 2 * length

    @pl.when(step == 0)
    def start():
        acts = tokens_ref[...].astype(f32)
        normed = (acts * norm_scale(acts) * gain_ref[...]).astype(bf16)
        normedt_ref[...] = normed.T
        acc_ref[...] = jnp.zeros_like(acc_ref)

    dq, dk, dv = [], [], []
    for pair in range(GROUP // 2):
        cols = slice(PAIR * pair, PAIR * (pair + 1))
        query, key, value = q_ref[:, cols], k_ref[:, cols], v_ref[:, cols]
        grad = gradmixed_ref[:, cols]
        product = grad.astype(f32) * mixed_ref[:, cols].astype(f32)
        gq = gk = gv = None
        for half in range(2):
            head = 2 * pair + half
            mask = pair_mask(query.shape, half)
            clear = lambda a: jnp.where(mask, a, jnp.zeros_like(a))
            own, asked = clear(grad), clear(query)
            center = jnp.sum(clear(product), axis=-1, keepdims=True)
            scores = mm_nt(asked, key)
            grad_probs = mm_nt(own, value)
            all_probs, all_grads = [], []
            for at in range(length // BLOCK):
                rows = slice(BLOCK * at, BLOCK * (at + 1))
                low = length - BLOCK * (at + 1)
                part = scores[rows, :] + skew_ref[head, :, low : low + length].astype(f32)
                probs = jnp.exp(part - lse_ref[0, rows, head : head + 1])
                piece = probs * (grad_probs[rows, :] - center[rows, :])
                if at == 0:
                    fold_ref[:, :low] = jnp.zeros((BLOCK, low), f32)
                    fold_ref[:, low : low + length] = piece
                    fold_ref[:, low + length :] = jnp.zeros((BLOCK, length - low), f32)
                else:
                    fold_ref[:, low : low + length] += piece
                all_probs.append(probs.astype(bf16))
                all_grads.append(piece.astype(bf16))
            rows = fold_ref[...]
            size = BLOCK
            while size > 1:
                size //= 2
                rows = rows[:size] + pltpu.roll(rows[size:], span - size, 1)
            line = pltpu.roll(rows, BLOCK - 1, 1)
            if prior_refs:
                line = line + prior_refs[1][0, head : head + 1, :]
            line_ref[0, head : head + 1, :] = line
            probs = jnp.concatenate(all_probs, axis=0)
            grad_scores = jnp.concatenate(all_grads, axis=0)
            a = mm(grad_scores, clear(key))
            b = mm(asked.T, grad_scores)
            c = mm(own.T, probs)
            gq = a if gq is None else gq + a
            gk = b if gk is None else gk + b
            gv = c if gv is None else gv + c
        dq.append(gq.astype(bf16))
        dk.append(gk.T.astype(bf16))
        dv.append(gv.T.astype(bf16))
    dq, dk, dv = (jnp.concatenate(x, axis=1) for x in (dq, dk, dv))
    normedt = normedt_ref[...]
    for i, grad in enumerate((dq, dk, dv)):
        total = mm(normedt, grad)
        if prior_refs:
            total = total + prior_refs[0][i].astype(f32)
        gw_ref[i] = total.astype(bf16)
    acc_ref[...] += mm_nt(dq, wq_ref[...]) + mm_nt(dk, wk_ref[...]) + mm_nt(dv, wv_ref[...])

    @pl.when(step == last)
    def finish():
        grad_normed = acc_ref[...]
        acts = tokens_ref[...].astype(f32)
        scale = norm_scale(acts)
        ggain = jnp.sum(grad_normed * acts * scale, axis=0, keepdims=True)
        if prior_refs:
            ggain = ggain + prior_refs[2][...]
        ggain_ref[...] = ggain
        weighted = grad_normed * gain_ref[...]
        slope = scale * scale * scale * jnp.mean(weighted * acts, axis=-1, keepdims=True)
        grad_acts = gradresid_ref[...] + (scale * weighted - acts * slope)
        gradacts_ref[0] = grad_acts.astype(bf16)


def back_heads_call(
    at, count, tokens, gain, grad_mixed, mixed, wq, wk, wv, q, k, v, skewed, lse, grad_resid,
    prior, grads,
):
    length, width = tokens.shape[1:]
    part = GROUP * HEAD
    groups = HEADS // GROUP
    whole = lambda *shape: pl.BlockSpec(shape, lambda g: (0,) * len(shape))
    columns = lambda size: pl.BlockSpec((size, part), lambda g: (0, g))
    shape = jax.ShapeDtypeStruct
    spec, full = one_of(count, at, length, width)
    weights = pl.BlockSpec((3, width, part), lambda g: (0, 0, g))
    lines = pl.BlockSpec((1, GROUP, 2 * length), lambda g: (g, 0, 0))
    return pl.pallas_call(
        back_heads_kernel,
        grid=(groups,),
        in_specs=[
            one_in(at, length, width), whole(1, width), columns(length), columns(length),
            columns(width), columns(width), columns(width),
            columns(length), columns(length), columns(length),
            pl.BlockSpec((GROUP, BLOCK, skewed.shape[2]), lambda g: (g, 0, 0)),
            pl.BlockSpec((1, length, GROUP), lambda g: (g, 0, 0)), whole(length, width),
            *([weights, lines, whole(1, width)] if prior else []),
            *([pl.BlockSpec(memory_space=pl.ANY)] * len(grads)),
        ],
        out_specs=[
            lines, weights,
            spec, whole(1, width),
        ],
        input_output_aliases={13 + len(prior): 2} if grads else {},
        out_shape=[
            shape((groups, GROUP, 2 * length), f32), shape((3, width, width), bf16),
            full, shape((1, width), f32),
        ],
        scratch_shapes=[
            pltpu.VMEM((width, length), bf16), pltpu.VMEM((length, width), f32),
            pltpu.VMEM((BLOCK, 2 * length), f32),
        ],
        compiler_params=params(60),
        cost_estimate=pl.CostEstimate(
            flops=groups * (2 * length * width * part * 6 + 8 * length * length * part * 4),
            bytes_accessed=21 * MIB, transcendentals=HEADS * length * length,
        ),
        name="back_heads",
    )(
        tokens, gain, grad_mixed, mixed, wq, wk, wv, q, k, v, skewed, lse, grad_resid,
        *prior, *grads,
    )


def pack_kernel(*refs):
    for at, ref in enumerate(refs[:-1]):
        refs[-1][at] = ref[...]


def pack_call(*parts):
    return pl.pallas_call(
        pack_kernel,
        out_shape=jax.ShapeDtypeStruct((len(parts), *parts[0].shape), parts[0].dtype),
        compiler_params=params(60),
        name="pack",
    )(*parts)


def skew_kernel(lines_ref, out_ref):
    heads, block, span = out_ref.shape
    full = lines_ref.shape[1]
    for head in range(heads):
        row = jnp.broadcast_to(lines_ref[head : head + 1, :], (16, full))
        base = pltpu.roll(row, full - (block - 1), 1, stride=1, stride_axis=0)
        for at in range(0, block, 16):
            turned = base if at == 0 else pltpu.roll(base, at, 1)
            out_ref[head, at : at + 16, :] = turned[:, :span].astype(bf16)


def skew_call(lines, block):
    heads, span = lines.shape
    return pl.pallas_call(
        skew_kernel,
        out_shape=jax.ShapeDtypeStruct((heads, block, span - block), bf16),
        compiler_params=params(16),
        name="skew",
    )(lines)


def exchange(buffer):
    return lax.all_to_all(buffer, AXES, split_axis=0, concat_axis=0, tiled=True)


def swap(value, bit):
    devices = lax.axis_size(AXES)
    return lax.ppermute(value, AXES, [(at, at ^ (1 << bit)) for at in range(devices)])


def own_bit(bit):
    return ((lax.axis_index(AXES) >> bit) & 1) == 1


def gather_step(held, bit):
    value, done = held
    theirs = swap(value, bit)
    upper = own_bit(bit)
    place = sum(1 for other in done if other > bit)
    value = jnp.stack(
        [jnp.where(upper, theirs, value), jnp.where(upper, value, theirs)], axis=place
    )
    return value, done + [bit]


def gather_all(value, order):
    held = (value, [])
    for bit in order:
        held = gather_step(held, bit)
    return held[0].reshape((-1,) + value.shape)


def scatter_step(held, bit):
    value, left = held
    place = 1 + left.index(bit)
    low = lax.index_in_dim(value, 0, place, keepdims=False)
    high = lax.index_in_dim(value, 1, place, keepdims=False)
    upper = own_bit(bit)
    sent = jnp.where(upper, low, high).astype(bf16)
    value = jnp.where(upper, high, low).astype(f32) + swap(sent, bit).astype(f32)
    return value, [other for other in left if other != bit]


def pack_rows(parts, width):
    lead = parts[0].shape[0]
    flat = jnp.concatenate([part.reshape(lead, -1) for part in parts], axis=1)
    short = -flat.shape[1] % width
    return jnp.pad(flat, ((0, 0), (0, short))).reshape(lead, -1, width)


def unpack_rows(packed, sizes):
    flat = packed.reshape(packed.shape[0], -1)
    out, at = [], 0
    for size in sizes:
        out.append(flat[:, at : at + size])
        at += size
    return out


def tiles_of(shard, experts):
    return -(-shard // 8), -(-experts // LANES) * LANES


def small_slab(router, short, width):
    lead, shard, experts = router.shape
    tall, lanes = tiles_of(shard, experts)
    router = jnp.pad(router, ((0, 0), (0, 8 * tall - shard), (0, lanes - experts)))
    parts = [router[:, 8 * at : 8 * at + 8] for at in range(tall)]
    parts.append(pack_rows(short, 8 * LANES).reshape(lead, 8, LANES))
    slab = jnp.concatenate(parts, axis=2)
    return jnp.pad(slab, ((0, 0), (0, 0), (0, width - slab.shape[2])))


def slab_parts(slab, shard, experts, sizes):
    tall, lanes = tiles_of(shard, experts)
    parts = [slab[:, :, lanes * at : lanes * at + experts] for at in range(tall)]
    short = slab[:, :, lanes * tall : lanes * tall + LANES]
    return jnp.concatenate(parts, axis=1)[:, :shard], unpack_rows(short, sizes)


def body(
    tokens,
    w_query,
    w_key,
    w_value,
    w_output,
    w_router,
    gain_attn,
    gain_ffn,
    rel_bias,
    router_bias,
    w_in,
    w_out,
    routes,
    fill_rank,
    bucket_map,
    upstream_grad,
):
    batches, length, width = tokens.shape
    devices = lax.axis_size(AXES)
    wide_bits = lax.axis_size("wide").bit_length() - 1
    bits = devices.bit_length() - 1
    local_experts = w_in.shape[0]
    experts = local_experts * devices
    capacity = max(2, 5 * length // (4 * experts))
    slots = experts * capacity
    span = 2 * length
    shard = w_query.shape[0]
    far = list(range(wide_bits, bits))
    near = list(range(1, wide_bits))
    turned = near[1:] + near[:1]

    expert_ids = jnp.arange(experts, dtype=jnp.int32)

    def plan(route, order):
        route_hot = (route[:, None] == expert_ids[None, :]).astype(f32)
        earlier = (order[None, :] < order[:, None]).astype(bf16)
        counts = jnp.dot(earlier, route_hot.astype(bf16), preferred_element_type=f32)
        slot = jnp.sum(counts * route_hot, axis=-1).astype(jnp.int32)
        first = jnp.where(slot < capacity, route * (2 * capacity) + slot, -1)
        second = jnp.where(first >= 0, first + capacity, -1)
        return jnp.stack([first, second], axis=0)

    short = [gain_attn, gain_ffn, rel_bias, router_bias]
    packed, short_router, *short = lax.optimization_barrier(
        (pack_call(w_query, w_key, w_value, w_output), w_router, *short)
    )
    sizes = [part.size for part in short]
    slab = small_slab(short_router[None], [part[None] for part in short], width)
    square, small = (packed, []), (slab[0], [])
    for bit in far[::-1]:
        square, small = gather_step(square, bit), gather_step(small, bit)
    spots = [plan(routes[at, :, 0], fill_rank[at]) for at in range(batches)]
    raw_spots = jnp.concatenate([spots[at][at] for at in range(batches)], axis=0)
    raw_ids = jnp.arange(2 * slots, dtype=jnp.int32)
    raw_sent = jnp.dot(
        (raw_ids[:, None] == raw_spots[None, :]).astype(bf16),
        upstream_grad.reshape(batches * length, width),
        preferred_element_type=f32,
    ).astype(bf16)
    value, small, raw_sent = lax.optimization_barrier((square[0], small[0], raw_sent))
    done = far[::-1]
    value = value.reshape((2,) * len(far) + (4, shard, width))
    value = [lax.index_in_dim(value, i, len(far), keepdims=False) for i in range(4)]
    low = (jnp.concatenate(value[:2] + [small], axis=-2), done)
    high = (jnp.concatenate(value[2:], axis=-2), done)
    for number, (one, two) in enumerate(zip(near[::-1], turned[::-1])):
        low, high = gather_step(low, one), gather_step(high, two)
        if number == 0:
            first, second, raw_sent = lax.optimization_barrier((low[0], high[0], raw_sent))
            low, high = (first, low[1]), (second, high[1])

    raw_arrived = exchange(raw_sent.reshape(devices, 2 * capacity, width))

    first, second = lax.optimization_barrier((low[0], high[0]))
    low, high = gather_step((first, low[1]), 0), gather_step((second, high[1]), 0)
    low, high = (part[0].reshape(devices, -1, width) for part in (low, high))
    wq, wk, wv, wo = (
        part[:, i * shard : (i + 1) * shard].reshape(width, width)
        for part in (low, high)
        for i in range(2)
    )
    wr_all, (gain_one, gain_two, rel_flat, bias_all) = slab_parts(
        low[:, 2 * shard :], shard, experts, sizes
    )
    wr_all = wr_all.reshape(width, experts)
    gain_one = gain_one.reshape(1, width).astype(f32)
    gain_two = gain_two.reshape(1, width).astype(f32)
    bias_all = bias_all.reshape(1, experts).astype(f32)
    table = rel_flat.reshape(BUCKETS, HEADS).T
    bucket_hot = (
        jnp.arange(BUCKETS, dtype=jnp.int32)[:, None]
        == jnp.pad(bucket_map, (0, 1), constant_values=-1)[None, :]
    ).astype(bf16)
    skewed = skew_call(jnp.dot(table, bucket_hot, preferred_element_type=f32), BLOCK)
    own = lax.axis_index(AXES).astype(jnp.int32).reshape(1)
    count = 8 if 8 * capacity % 16 == 0 else 16
    row = np.arange(count * capacity, dtype=np.int32)
    row = row + (row // capacity) * capacity
    place = jnp.asarray(np.stack([row, row + capacity], axis=1))
    fronts, arrived, returned = [], [], []
    acts = tokens
    for at in range(batches):
        if at == 1:
            targets = [(spots[i].T, routes[i]) for i in range(batches)]
            acts, raw_arrived, targets, place, wr_all, bias_all = lax.optimization_barrier(
                (acts, raw_arrived, targets, place, wr_all, bias_all)
            )
        front = front_call(
            at, acts, wq, wk, wv, wo, skewed, gain_one, gain_two, spots[at], slots
        )
        fronts.append(front)
        arrived.append(exchange(front[-1].reshape(devices, 2 * capacity, width // 2)))
    grad_in = grad_out = 0.0
    for at in range(batches):
        sent, rows, active, grad_inner, grad_result = expert_call(
            at,
            own,
            arrived[at].reshape(2 * slots, width // 2),
            raw_arrived.reshape(2 * slots, width),
            wr_all,
            bias_all,
            place,
            w_in[0],
            w_out[0],
        )
        if at == batches - 1:
            sent, grad_in, grad_out = lax.optimization_barrier((sent, grad_in, grad_out))
        grad_in += jnp.einsum("rd,rf->df", rows, grad_inner, preferred_element_type=f32)
        grad_out += jnp.einsum("rf,rd->fd", active, grad_result, preferred_element_type=f32)
        back = exchange(sent.reshape(devices, 2 * capacity, width))
        back, grad_in, grad_out = lax.optimization_barrier((back, grad_in, grad_out))
        returned.append(back)

    row_prior, head_prior, outputs, grads = [], [], [], []
    for at in range(batches):
        q, k, v, mixed, lse, sent = fronts[at]
        row_part = back_rows_call(
            at, batches, *targets[at], returned[at].reshape(2 * slots, width), upstream_grad,
            tokens, mixed, gain_two, wr_all, bias_all, wo, row_prior,
            outputs,
        )
        outputs = row_part[:1]
        row_prior = row_part[3:]
        head_part = back_heads_call(
            at, batches, tokens, gain_one, row_part[2], mixed, wq, wk, wv, q, k, v, skewed, lse,
            row_part[1], head_prior, grads,
        )
        grads = head_part[2:3]
        head_prior = [head_part[1], head_part[0], head_part[3]]

    g_output, g_router, g_gain_two, g_bias = row_prior
    g_heads, lines, g_gain_one = head_prior
    def halved(parts):
        value = jnp.concatenate([part.astype(bf16) for part in parts], axis=1)
        value = value.reshape((1,) + (2,) * bits + value.shape[1:])
        return scatter_step((value, list(range(bits))[::-1]), 0)

    outer = halved([g_output.reshape(devices, shard, width)])
    g_heads = g_heads.reshape(3, devices, shard, width)
    inner = halved(list(g_heads))
    cut = 2 * shard
    low = (inner[0][..., :cut, :], inner[1])
    high = (jnp.concatenate([inner[0][..., cut:, :], outer[0]], axis=-2), inner[1])
    for number, (one, two) in enumerate(zip(near, turned)):
        low, high = scatter_step(low, one), scatter_step(high, two)
        if number == 0:
            first, second, g_router, g_gain_two, g_bias, lines, g_gain_one = (
                lax.optimization_barrier(
                    (low[0], high[0], g_router, g_gain_two, g_bias, lines, g_gain_one)
                )
            )
            low, high = (first, low[1]), (second, high[1])
            g_rel = jnp.einsum(
                "hn,bn->bh",
                lines.reshape(HEADS, span),
                bucket_hot.astype(f32),
                precision=lax.Precision.HIGHEST,
            )
            short = [
                part.reshape(devices, -1) for part in (g_gain_one, g_gain_two, g_rel, g_bias)
            ]
            short_pack = pack_rows(short, 8 * LANES).reshape(devices, -1, LANES).astype(bf16)
            lanes = -(-experts // LANES) * LANES
            router_pack = jnp.pad(g_router.astype(bf16), ((0, 0), (0, lanes - experts)))
            router_pack = router_pack.reshape(devices, -1, LANES)
            small = jnp.concatenate([router_pack, short_pack], axis=1)
            small = jnp.sum(exchange(small).astype(f32), axis=0)
    held = (jnp.concatenate([low[0], high[0]], axis=-2), low[1])
    for bit in far:
        held = scatter_step(held, bit)
    r_query, r_key, r_value, r_output = jnp.split(
        held[0][0], [shard, 2 * shard, 3 * shard], axis=0
    )
    cut = router_pack.shape[1]
    r_router = small[:cut].reshape(shard, lanes)[:, :experts]
    tail = unpack_rows(small[None, cut:], [part.shape[1] for part in short])
    r_gain_one, r_gain_two, r_rel, r_bias = (
        part.reshape(shape)
        for part, shape in zip(
            tail, (gain_attn.shape, gain_ffn.shape, rel_bias.shape, router_bias.shape)
        )
    )
    return (
        outputs[0],
        grads[0],
        r_query,
        r_key,
        r_value,
        r_output,
        r_router,
        r_gain_one,
        r_gain_two,
        r_rel,
        r_bias,
        grad_in[None],
        grad_out[None],
    )


def solution(mesh):
    both = P(AXES)
    in_specs = (both,) * 14 + (P(), both)
    out_specs = (both,) * 13
    return jax.shard_map(body, mesh=mesh, in_specs=in_specs, out_specs=out_specs, check_vma=False)
```
